32 devices in a mesh: section: 2 (over core), dp: 4 (over y, x), seq: 4 (over z).
Axes of the slice: x: 2, y: 2, z: 4, core: 2. Of those that a mesh axis runs over, the one named last changes fastest.
Arguments:
- inputs: bfloat16 [2, 16, 1024, 512], P('section', 'dp', 'seq'), may hold values from -6 to 6
- cotangent: bfloat16 [16, 1024, 512], P('dp', 'seq'), may hold values from -6 to 6
- qkv_weight: bfloat16 [2, 512, 1536], P('section'), may hold values from -0.25 to 0.25
- out_weight: bfloat16 [2, 512, 512], P('section'), may hold values from -3 to 3
- up_weight: bfloat16 [2, 512, 2048], P('section'), may hold values from -0.25 to 0.25
- down_weight: bfloat16 [2, 2048, 512], P('section'), may hold values from -0.125 to 0.125
- norm_gain: float32 [2, 2, 512], P('section'), may hold values from 0.5 to 1.5
- norm_bias: float32 [2, 2, 512], P('section'), may hold values from -1.2 to 1.2
- cross_q_weight: bfloat16 [512, 512], replicated, may hold values from -0.25 to 0.25
- cross_kv_weight: bfloat16 [512, 1024], replicated, may hold values from -0.25 to 0.25
- cross_out_weight: bfloat16 [512, 512], replicated, may hold values from -3 to 3
- cross_gain: float32 [512], replicated, may hold values from 0.5 to 1.5
- cross_bias: float32 [512], replicated, may hold values from -1.2 to 1.2
- source_segments: int32 [16, 1024], P('dp'), may hold values from 0 to 3, as said below
- target_segments: int32 [16, 1024], P('dp'), may hold values from 0 to 3, as said below
Outputs:
- layer_outputs: bfloat16 [2, 16, 1024, 512], P('section', 'dp', 'seq')
- input_grads: float32 [2, 16, 1024, 512], P('section', 'dp', 'seq')
- qkv_grad: float32 [2, 512, 1536], P('section')
- out_grad: float32 [2, 512, 512], P('section')
- up_grad: float32 [2, 512, 2048], P('section')
- down_grad: float32 [2, 2048, 512], P('section')
- gain_grad: float32 [2, 2, 512], P('section')
- bias_grad: float32 [2, 2, 512], P('section')
- cross_q_grad: float32 [512, 512], replicated
- cross_kv_grad: float32 [512, 1024], replicated
- cross_out_grad: float32 [512, 512], replicated
- cross_gain_grad: float32 [512], replicated
- cross_bias_grad: float32 [512], replicated
The draws below stay inside these ranges and needn't reach their ends.
Inputs may be any that keep to these rules, and one draw needn't show every extreme that they name: `source_segments`: each row numbers its documents 0 to 3 in order, never falling, each document one token or more; target document j of a row is attended against source document j of the same row. `target_segments`: as for source_segments.
All inputs are finite; a program needn't handle non-finite values.
Results may differ from the reference program's by a relative error of at most 0.02.
Values may be sent and summed in bfloat16 or wider, within the bound.
A program may use at most 320 MiB of HBM per device.

```python
import jax
import jax.numpy as jnp
from jax import lax

D = 512
FF = 2048
H = 8
DH = 64
SEQ_LEN = 1024
DOCS = 4
SHARD = 256
ROWS = 16


def long_choice(key):
    return jax.random.randint(key, (ROWS,), 0, DOCS)


def document_ids(key, long_doc):
    short_most = (SHARD - 1) // (DOCS - 1)
    short_len = jax.random.randint(key, (ROWS, DOCS), 1, short_most + 1)
    marked = jnp.arange(DOCS)[None, :] == long_doc[:, None]
    short_len = jnp.where(marked, 0, short_len)
    long_len = SEQ_LEN - jnp.sum(short_len, axis=1, keepdims=True)
    lengths = jnp.where(marked, long_len, short_len)
    doc_ends = jnp.cumsum(lengths, axis=1)
    places = jnp.arange(SEQ_LEN)
    counted = (places[None, :, None] >= doc_ends[:, None, :]).astype(jnp.int32)
    return jnp.sum(counted, axis=2).astype(jnp.int32)


def draw_source_segments(key, part):
    long_doc = long_choice(key)
    key = jax.random.fold_in(key, 11)
    return document_ids(key, long_doc)


def draw_target_segments(key, part):
    long_doc = long_choice(key)
    key = jax.random.fold_in(key, 12)
    return document_ids(key, long_doc)


def shard_levels(stream_key, extent, pieces, low, largest):
    loudness, own = 1.0, jax.random.fold_in(stream_key, 6)
    for axis_at, parts in pieces:
        draws = jnp.exp(jax.random.uniform(jax.random.fold_in(own, axis_at), (parts,), jnp.float32, low / len(pieces), largest / len(pieces)))
        loudness = loudness * jnp.repeat(draws, extent[axis_at] // parts).reshape([-1 if axis == axis_at else 1 for axis in range(len(extent))])
    return loudness


def noise(own_key, dims, width, limit, pieces=(), held_as=jnp.bfloat16):
    array = jax.random.normal(own_key, dims, jnp.float32) * width
    if len(pieces) > 0:
        array = shard_levels(own_key, dims, pieces, -0.22, 0.18) * array
    return jnp.clip(array, min=-limit, max=limit).astype(held_as)


def setup_inputs(seed: int = 0) -> dict:
    seeds = jax.random.split(jax.random.key(seed), 16)
    return {
        "inputs": noise(seeds[0], (2, ROWS, SEQ_LEN, D), 1.0, 6.0, ((0, 2), (1, 4), (2, 4))),
        "cotangent": noise(seeds[1], (ROWS, SEQ_LEN, D), 1.0, 6.0, ((0, 4), (1, 4))),
        "qkv_weight": noise(seeds[2], (2, D, 3 * D), D ** -0.5, 0.25, ((0, 2),)),
        "out_weight": noise(seeds[3], (2, D, D), 4 ** -0.5, 3.0, ((0, 2),)),
        "up_weight": noise(seeds[4], (2, D, FF), D ** -0.5, 0.25, ((0, 2),)),
        "down_weight": noise(seeds[5], (2, FF, D), FF ** -0.5, 0.125, ((0, 2),)),
        "norm_gain": jnp.clip(1.0 + 0.1 * jax.random.normal(seeds[6], (2, 2, D), jnp.float32), 0.5, 1.5),
        "norm_bias": noise(seeds[7], (2, 2, D), 0.3, 1.2, ((0, 2),), jnp.float32),
        "cross_q_weight": noise(seeds[8], (D, D), D ** -0.5, 0.25),
        "cross_kv_weight": noise(seeds[9], (D, 2 * D), D ** -0.5, 0.25),
        "cross_out_weight": noise(seeds[10], (D, D), 4 ** -0.5, 3.0),
        "cross_gain": jnp.clip(1.0 + 0.1 * jax.random.normal(seeds[11], (D,), jnp.float32), 0.5, 1.5),
        "cross_bias": noise(seeds[12], (D,), 0.3, 1.2, (), jnp.float32),
        "source_segments": draw_source_segments(jax.random.fold_in(seeds[15], 71), 0),
        "target_segments": draw_target_segments(jax.random.fold_in(seeds[15], 71), 0),
    }


@jax.custom_vjp
def low(v):
    return lax.optimization_barrier(v.astype(jnp.bfloat16)).astype(jnp.float32)

@jax.custom_vjp
def low_back(v):
    return v

def low_keep(v):
    return (low(v), None)

def low_pass(kept, grad):
    return (grad,)

def back_keep(v):
    return (v, None)

def back_low(kept, grad):
    return (low(grad),)
low.defvjp(low_keep, low_pass)
low_back.defvjp(back_keep, back_low)
EPSILON = 1e-05
NEGATIVE = -1e+30
PRECISE = lax.Precision.HIGHEST

def matmul(left_side, right_side):
    return jnp.einsum('...d,de->...e', left_side, right_side, precision=PRECISE)

def layer_norm(vector, gain_row, bias_row):
    centre = vector - lax.optimization_barrier(jnp.mean(vector, axis=-1, keepdims=True))
    spread = lax.optimization_barrier(jnp.mean(centre * centre, axis=-1, keepdims=True))
    return centre * lax.rsqrt(spread + EPSILON) * gain_row + bias_row

def split_heads(vector):
    return vector.reshape(vector.shape[:-1] + (H, DH))

def attend(queries, key_rows, value_rows, allowed):
    scores = jnp.einsum('gqhd,gkhd->ghqk', split_heads(queries), split_heads(key_rows), precision=PRECISE) * DH ** (-0.5)
    scores = low_back(scores)
    scores = jnp.where(allowed[:, None], scores, NEGATIVE)
    weights = jax.nn.softmax(scores, axis=-1)
    mixed_out = jnp.einsum('ghqk,gkhd->gqhd', low(weights), split_heads(value_rows), precision=PRECISE)
    return mixed_out.reshape(queries.shape)

def self_block(tokens, qkv_matrix, out_matrix, allowed):
    packed = low_back(low(matmul(low(tokens), qkv_matrix)))
    queries, key_rows, value_rows = jnp.split(packed, 3, axis=-1)
    mixed_out = low_back(low(attend(queries, key_rows, value_rows, allowed)))
    return low_back(matmul(mixed_out, out_matrix))

def feed_forward(hidden, up_matrix, down_matrix):
    upward = low_back(matmul(low(hidden), up_matrix))
    return low_back(matmul(low(jax.nn.gelu(upward, approximate=True)), down_matrix))

def forward(embedded, weight_set, source_rows, target_rows):
    qkv_matrix, out_matrix, up_matrix, down_matrix, norm_gains, norm_biases, query_matrix, pair_matrix, cross_matrix, cross_gains, cross_shift = weight_set
    positions = jnp.arange(SEQ_LEN)
    causal = positions[None, :] <= positions[:, None]
    source_mask = source_rows[:, :, None] == source_rows[:, None, :]
    target_mask = (target_rows[:, :, None] == target_rows[:, None, :]) & causal[None]
    cross_mask = target_rows[:, :, None] == source_rows[:, None, :]
    source = embedded[0]
    first_norm = layer_norm(source + self_block(source, qkv_matrix[0], out_matrix[0], source_mask), norm_gains[0, 0], norm_biases[0, 0])
    memory = layer_norm(first_norm + feed_forward(first_norm, up_matrix[0], down_matrix[0]), norm_gains[0, 1], norm_biases[0, 1])
    target = embedded[1]
    second = layer_norm(target + self_block(target, qkv_matrix[1], out_matrix[1], target_mask), norm_gains[1, 0], norm_biases[1, 0])
    cross_query = low_back(low(matmul(low(second), query_matrix)))
    cross_pair = low_back(low(matmul(low_back(low(memory)), pair_matrix)))
    cross_keys, cross_values = jnp.split(cross_pair, 2, axis=-1)
    cross_mixed = low_back(low(attend(cross_query, cross_keys, cross_values, cross_mask)))
    third_norm = layer_norm(second + low_back(matmul(cross_mixed, cross_matrix)), cross_gains, cross_shift)
    decoded = layer_norm(third_norm + feed_forward(third_norm, up_matrix[1], down_matrix[1]), norm_gains[1, 1], norm_biases[1, 1])
    return (decoded, memory)

def reference(inputs, cotangent, qkv_weight, out_weight, up_weight, down_weight, norm_gain, norm_bias, cross_q_weight, cross_kv_weight, cross_out_weight, cross_gain, cross_bias, source_segments, target_segments):
    weight_set = tuple((arr_item.astype(jnp.float32) for arr_item in (qkv_weight, out_weight, up_weight, down_weight, norm_gain, norm_bias, cross_q_weight, cross_kv_weight, cross_out_weight, cross_gain, cross_bias)))
    embedded = jnp.moveaxis(inputs.astype(jnp.float32), 1, 0)[:, :, None]
    cotangents = cotangent.astype(jnp.float32)[:, None]
    source_rows = source_segments[:, None]
    target_rows = target_segments[:, None]

    def one_group(totals, group_items):
        embedded_in, cot_rows, source_ids, target_ids = group_items

        def run_group(embedded_part, weight_part):
            return forward(embedded_part, weight_part, source_ids, target_ids)
        (decoded, memory), pull = jax.vjp(run_group, embedded_in, weight_set)
        grad_in, grad_weights = pull((cot_rows, jnp.zeros_like(memory)))
        totals = jax.tree.map(lambda total_sum, new_term: total_sum + new_term, totals, grad_weights)
        return (totals, (decoded, memory, grad_in))
    zero_grads = tuple((jnp.zeros(arr_item.shape, jnp.float32) for arr_item in weight_set))
    totals, (decoded, memory, grad_in) = lax.scan(one_group, zero_grads, (embedded, cotangents, source_rows, target_rows))
    layer_outputs = jnp.stack([memory.reshape(ROWS, SEQ_LEN, D), decoded.reshape(ROWS, SEQ_LEN, D)]).astype(jnp.bfloat16)
    input_grads = jnp.moveaxis(grad_in, 1, 0).reshape(2, ROWS, SEQ_LEN, D)
    return (layer_outputs, input_grads, totals[0], totals[1], totals[2], totals[3], totals[4], totals[5], totals[6], totals[7], totals[8], totals[9], totals[10])
```

```python
import functools

import jax
import jax.numpy as jnp
from jax import lax
from jax.experimental import pallas as pl
from jax.experimental.pallas import tpu as pltpu
from jax.sharding import PartitionSpec as P

DH = 64
MICRO = 2
MB_ROWS = 2


EPSILON = 1e-05
NEGATIVE = -1e30


def from_behind(value, axis, steps):
    count = lax.axis_size(axis)
    leading, last = (max(0, -steps), min(count, count - steps))
    return lax.ppermute(value, axis, [(source, source + steps) for source in range(leading, last)])


def layer_norm(vector, gain_row, bias_row):
    centre = vector - jnp.mean(vector, axis=-1, keepdims=True)
    spread = jnp.mean(centre * centre, axis=-1, keepdims=True)
    return centre * lax.rsqrt(spread + EPSILON) * gain_row + bias_row


def gelu_tanh(vector):
    return jax.nn.gelu(vector, approximate=True)


def heads_view(vector):
    return vector.reshape(vector.shape[:-1] + (vector.shape[-1] // DH, DH))


def joined_view(vector):
    return vector.reshape(vector.shape[:-2] + (vector.shape[-2] * vector.shape[-1],))


def dense_rows(left_side, right_side):
    return jnp.einsum("rsd,de->rse", left_side, right_side, preferred_element_type=jnp.float32)


def dense_back(left_side, right_side):
    return jnp.einsum("rse,de->rsd", left_side, right_side, preferred_element_type=jnp.float32)


def outer_sum(left_side, right_side):
    return jnp.einsum("rsd,rse->de", left_side, right_side, preferred_element_type=jnp.float32)


def build_mask(query_ids, key_ids, query_places, key_places, causal):
    same_doc = query_ids[:, :, None] == key_ids[:, None, :]
    ordered = (key_places[None, :] <= query_places[:, None]) | jnp.logical_not(causal)
    return same_doc & ordered[None]


def soft_forward(queries, key_rows, value_rows, allowed):
    score_scale = DH ** (-0.5)
    scores = (
        jnp.einsum(
            "rqhe,rkhe->rhqk",
            heads_view(queries),
            heads_view(key_rows),
            preferred_element_type=jnp.float32,
        )
        * score_scale
    )
    scores = jnp.where(allowed[:, None], scores, NEGATIVE)
    highest = jnp.max(scores, axis=-1, keepdims=True)
    exp_terms = jnp.exp(scores - highest)
    totals = jnp.sum(exp_terms, axis=-1, keepdims=True)
    weights = exp_terms / totals
    log_total = (highest + jnp.log(totals))[..., 0]
    mixed_out = jnp.einsum(
        "rhqk,rkhe->rqhe",
        weights.astype(jnp.bfloat16),
        heads_view(value_rows),
        preferred_element_type=jnp.float32,
    )
    return (joined_view(mixed_out), weights, log_total)


def score_grads(grad_mixed, value_rows, weights):
    grad_weights = jnp.einsum(
        "rqhe,rkhe->rhqk",
        heads_view(grad_mixed),
        heads_view(value_rows),
        preferred_element_type=jnp.float32,
    )
    inner_sum = jnp.sum(grad_weights * weights, axis=-1, keepdims=True)
    grad_scores = (weights * (grad_weights - inner_sum)).astype(jnp.bfloat16)
    return (grad_scores, inner_sum[..., 0])


def attend_keys(queries, key_rows, value_rows, query_ids, key_ids, causal):
    span_len = key_rows.shape[1]
    offset = lax.axis_index("seq") * span_len
    whole_keys, whole_values = (
        lax.all_gather(key_rows, "seq", axis=1, tiled=True),
        lax.all_gather(value_rows, "seq", axis=1, tiled=True),
    )
    own_positions = offset + jnp.arange(span_len)
    all_positions = jnp.arange(whole_keys.shape[1])
    own_ids = lax.dynamic_slice_in_dim(query_ids, offset, span_len, 1)
    allowed = build_mask(own_ids, key_ids, own_positions, all_positions, causal)
    mixed_out, weights, log_total = soft_forward(queries, whole_keys, whole_values, allowed)
    kept_state = (
        queries,
        key_rows,
        value_rows,
        whole_keys,
        whole_values,
        weights,
        log_total,
        query_ids,
        key_ids,
        causal,
    )
    return (mixed_out, kept_state)


def attend_back(kept_state, grad_mixed):
    (
        queries,
        key_rows,
        value_rows,
        whole_keys,
        whole_values,
        weights,
        log_total,
        query_ids,
        key_ids,
        causal,
    ) = kept_state
    score_scale = DH ** (-0.5)
    grad_scores, inner_sum = score_grads(grad_mixed, whole_values, weights)
    grad_queries = (
        jnp.einsum(
            "rhqk,rkhe->rqhe",
            grad_scores,
            heads_view(whole_keys),
            preferred_element_type=jnp.float32,
        )
        * score_scale
    )
    part_keys = (
        jnp.einsum(
            "rhqk,rqhe->rkhe", grad_scores, heads_view(queries), preferred_element_type=jnp.float32
        )
        * score_scale
    )
    part_values = jnp.einsum(
        "rhqk,rqhe->rkhe",
        weights.astype(jnp.bfloat16),
        heads_view(grad_mixed),
        preferred_element_type=jnp.float32,
    )
    grad_keys, grad_values = (
        lax.psum_scatter(
            joined_view(part_keys).astype(jnp.bfloat16), "seq", scatter_dimension=1, tiled=True
        ).astype(jnp.float32),
        lax.psum_scatter(
            joined_view(part_values).astype(jnp.bfloat16), "seq", scatter_dimension=1, tiled=True
        ).astype(jnp.float32),
    )
    return (joined_view(grad_queries), grad_keys, grad_values)


def layer_forward(tokens, memory_in, own_ids, source_ids, target_ids, params, decoder):
    (
        qkv_matrix,
        out_matrix,
        up_matrix,
        down_matrix,
        norm_gains,
        norm_biases,
        query_matrix,
        pair_matrix,
        cross_matrix,
        cross_gains,
        cross_shift,
    ) = params
    residual = tokens.astype(jnp.float32)
    packed = dense_rows(tokens, qkv_matrix).astype(jnp.bfloat16)
    queries, key_rows, value_rows = jnp.split(packed, 3, axis=-1)
    mixed_out, self_state = attend_keys(queries, key_rows, value_rows, own_ids, own_ids, decoder)
    mixed_low = mixed_out.astype(jnp.bfloat16)
    first_sum = residual + dense_rows(mixed_low, out_matrix)
    first_norm = layer_norm(first_sum, norm_gains[0], norm_biases[0])
    first_low = first_norm.astype(jnp.bfloat16)
    cross_query = dense_rows(first_low, query_matrix).astype(jnp.bfloat16)
    cross_pair = dense_rows(memory_in, pair_matrix).astype(jnp.bfloat16)
    cross_keys, cross_values = jnp.split(cross_pair, 2, axis=-1)
    cross_mixed, cross_state = attend_keys(
        cross_query, cross_keys, cross_values, target_ids, source_ids, False
    )
    cross_low = cross_mixed.astype(jnp.bfloat16)
    cross_sum = first_norm + dense_rows(cross_low, cross_matrix)
    second = jnp.where(decoder, layer_norm(cross_sum, cross_gains, cross_shift), first_norm)
    second_low = second.astype(jnp.bfloat16)
    upward = dense_rows(second_low, up_matrix)
    gated_low = gelu_tanh(upward).astype(jnp.bfloat16)
    last_sum = second + dense_rows(gated_low, down_matrix)
    output = layer_norm(last_sum, norm_gains[1], norm_biases[1])
    kept_state = (
        tokens,
        self_state,
        mixed_low,
        first_sum,
        first_low,
        cross_state,
        cross_low,
        cross_sum,
        second_low,
        upward,
        gated_low,
        last_sum,
    )
    return (output, kept_state)


def layer_backward(kept_state, grad_out, params, decoder):
    (
        qkv_matrix,
        out_matrix,
        up_matrix,
        down_matrix,
        norm_gains,
        norm_biases,
        query_matrix,
        pair_matrix,
        cross_matrix,
        cross_gains,
        cross_shift,
    ) = params
    (
        tokens,
        self_state,
        mixed_low,
        first_sum,
        first_low,
        cross_state,
        cross_low,
        cross_sum,
        second_low,
        upward,
        gated_low,
        last_sum,
    ) = kept_state
    unused, pull_last = jax.vjp(layer_norm, last_sum, norm_gains[1], norm_biases[1])
    grad_last, grad_gain_last, grad_bias_last = pull_last(grad_out)
    down_in = grad_last.astype(jnp.bfloat16)
    grad_down = outer_sum(gated_low, down_in)
    grad_gated = dense_back(down_in, down_matrix)
    unused, pull_gelu = jax.vjp(gelu_tanh, upward)
    up_in = pull_gelu(grad_gated)[0].astype(jnp.bfloat16)
    grad_up = outer_sum(second_low, up_in)
    grad_second = grad_last + dense_back(up_in, up_matrix)
    unused, pull_cross = jax.vjp(layer_norm, cross_sum, cross_gains, cross_shift)
    grad_cross_sum, grad_cross_gain, grad_cross_bias = pull_cross(
        jnp.where(decoder, grad_second, 0.0)
    )
    grad_first = jnp.where(decoder, grad_cross_sum, grad_second)
    cross_in = grad_cross_sum.astype(jnp.bfloat16)
    grad_cross_out = outer_sum(cross_low, cross_in)
    grad_cross_mixed = dense_back(cross_in, cross_matrix).astype(jnp.bfloat16)
    grad_cross_query, grad_cross_keys, grad_cross_values = attend_back(
        cross_state, grad_cross_mixed
    )
    query_in = grad_cross_query.astype(jnp.bfloat16)
    grad_query_matrix = outer_sum(first_low, query_in)
    grad_first = grad_first + dense_back(query_in, query_matrix)
    pair_in = jnp.concatenate([grad_cross_keys, grad_cross_values], axis=-1).astype(jnp.bfloat16)
    unused, pull_first = jax.vjp(layer_norm, first_sum, norm_gains[0], norm_biases[0])
    grad_first_sum, grad_gain_first, grad_bias_first = pull_first(grad_first)
    out_in = grad_first_sum.astype(jnp.bfloat16)
    grad_out_matrix = outer_sum(mixed_low, out_in)
    grad_mixed = dense_back(out_in, out_matrix).astype(jnp.bfloat16)
    grad_queries, grad_keys, grad_values = attend_back(self_state, grad_mixed)
    qkv_in = jnp.concatenate([grad_queries, grad_keys, grad_values], axis=-1).astype(jnp.bfloat16)
    grad_qkv_matrix = outer_sum(tokens, qkv_in)
    grad_tokens = grad_first_sum + dense_back(qkv_in, qkv_matrix)
    grad_set = (
        grad_qkv_matrix,
        grad_out_matrix,
        grad_up,
        grad_down,
        jnp.stack([grad_gain_first, grad_gain_last]),
        jnp.stack([grad_bias_first, grad_bias_last]),
        grad_query_matrix,
        jnp.zeros(pair_matrix.shape, jnp.float32),
        grad_cross_out,
        grad_cross_gain,
        grad_cross_bias,
    )
    return (grad_tokens, pair_in, grad_set)


def shards(
    inputs,
    cotangent,
    qkv_weight,
    out_weight,
    up_weight,
    down_weight,
    norm_gain,
    norm_bias,
    cross_q_weight,
    cross_kv_weight,
    cross_out_weight,
    cross_gain,
    cross_bias,
    source_segments,
    target_segments,
):
    section_index = lax.axis_index("section")
    decoder = section_index == 1
    params = (
        qkv_weight[0],
        out_weight[0],
        up_weight[0],
        down_weight[0],
        norm_gain[0],
        norm_bias[0],
        cross_q_weight,
        cross_kv_weight,
        cross_out_weight,
        cross_gain,
        cross_bias,
    )
    tokens_all = inputs[0]
    own_all = jnp.where(decoder, target_segments, source_segments)
    span_len = tokens_all.shape[1]
    features = tokens_all.shape[2]
    memory_in = jnp.zeros((MB_ROWS, span_len, features), jnp.bfloat16)
    outputs_all = jnp.zeros(tokens_all.shape, jnp.bfloat16)
    caches = []
    sent_rows = []
    for forward_tick in range(MICRO + 1):
        micro_index = forward_tick - section_index
        active = (micro_index >= 0) & (micro_index < MICRO)
        first_row = jnp.clip(micro_index, 0, MICRO - 1) * MB_ROWS
        rows_now = lax.dynamic_slice_in_dim(tokens_all, first_row, MB_ROWS, 0)
        own_now = lax.dynamic_slice_in_dim(own_all, first_row, MB_ROWS, 0)
        source_now = lax.dynamic_slice_in_dim(source_segments, first_row, MB_ROWS, 0)
        target_now = lax.dynamic_slice_in_dim(target_segments, first_row, MB_ROWS, 0)
        output, kept_state = layer_forward(
            rows_now, memory_in, own_now, source_now, target_now, params, decoder
        )
        output_low = output.astype(jnp.bfloat16)
        current = lax.dynamic_slice_in_dim(outputs_all, first_row, MB_ROWS, 0)
        outputs_all = lax.dynamic_update_slice_in_dim(
            outputs_all, jnp.where(active, output_low, current), first_row, 0
        )
        caches.append(kept_state)
        sent_rows.append(output_low)
        if forward_tick < MICRO:
            memory_in = from_behind(output_low, "section", 1)
    grad_pair_in = jnp.zeros((MB_ROWS, span_len, 2 * features), jnp.bfloat16)
    totals = tuple((jnp.zeros(param_item.shape, jnp.float32) for param_item in params))
    input_all = jnp.zeros(tokens_all.shape, jnp.float32)
    for backward_tick in range(MICRO + 1):
        forward_tick = MICRO - backward_tick
        micro_index = forward_tick - section_index
        active = (micro_index >= 0) & (micro_index < MICRO)
        first_row = jnp.clip(micro_index, 0, MICRO - 1) * MB_ROWS
        cot_now = lax.dynamic_slice_in_dim(cotangent, first_row, MB_ROWS, 0).astype(jnp.float32)
        memory_grad = lax.optimization_barrier(
            dense_back(grad_pair_in, params[7]).astype(jnp.bfloat16)
        ).astype(jnp.float32)
        pair_term = outer_sum(sent_rows[forward_tick], grad_pair_in)
        grad_out = jnp.where(decoder, cot_now, memory_grad)
        grad_tokens, pair_in, grad_set = layer_backward(
            caches[forward_tick], grad_out, params, decoder
        )
        grad_set = grad_set[:7] + (jnp.where(decoder, 0.0, pair_term),) + grad_set[8:]
        totals = jax.tree.map(
            lambda total_sum, new_term: total_sum + jnp.where(active, new_term, 0.0),
            totals,
            grad_set,
        )
        current = lax.dynamic_slice_in_dim(input_all, first_row, MB_ROWS, 0)
        input_all = lax.dynamic_update_slice_in_dim(
            input_all, jnp.where(active, grad_tokens, current), first_row, 0
        )
        if backward_tick < MICRO:
            grad_pair_in = from_behind(pair_in, "section", -1)
    layer_part = lax.psum(
        (totals[0], totals[1], totals[2], totals[3], totals[4], totals[5]), ("dp", "seq")
    )
    cross_part = lax.psum(
        (totals[6], totals[7], totals[8], totals[9], totals[10]), ("section", "dp", "seq")
    )
    return (
        outputs_all[None],
        input_all[None],
        layer_part[0][None],
        layer_part[1][None],
        layer_part[2][None],
        layer_part[3][None],
        layer_part[4][None],
        layer_part[5][None],
        cross_part[0],
        cross_part[1],
        cross_part[2],
        cross_part[3],
        cross_part[4],
    )


BF = jnp.bfloat16
F32 = jnp.float32
AXES = ("section", "dp", "seq")
PAIR = 2 * DH
STAT = 8


def swap(value, move):
    pairs = []
    for core in range(2):
        for group in range(4):
            for depth in range(4):
                to = move(core, group, depth)
                if to is not None:
                    pairs.append(
                        ((core * 4 + group) * 4 + depth, (to[0] * 4 + to[1]) * 4 + to[2])
                    )
    return lax.ppermute(value, AXES, pairs)


def to_core(value):
    return swap(value, lambda core, group, depth: (1 - core, group, depth))


def side_of(depth):
    return (depth ^ (depth >> 1)) & 1


def block_of(core, at):
    return 2 * at + (core ^ at)


def pick(parts, order):
    odd = (order & 1) == 1
    high = (order & 2) == 2
    a = [jnp.where(odd, parts[j ^ 1], parts[j]) for j in range(4)]
    return [jnp.where(high, a[j ^ 2], a[j]) for j in range(4)]


def replace_block(whole, block, at, axis):
    size, count = block.shape[axis], whole.shape[axis]
    parts = [lax.slice_in_dim(whole, 0, at, axis=axis)] if at > 0 else []
    parts.append(block)
    if at + size < count:
        parts.append(lax.slice_in_dim(whole, at + size, count, axis=axis))
    return jnp.concatenate(parts, axis=axis)


def attend_kernel(causal, q_ref, k_ref, v_ref, ko_ref, vo_ref, qf_ref, kf_ref, kfo_ref, o_ref, lse_ref):
    size = q_ref.shape[0]
    half = size // 2
    lane = lax.broadcasted_iota(jnp.int32, (size, PAIR), 1)
    low_lanes = lane < DH
    q = q_ref[...] * jnp.array(DH ** (-0.5), BF)
    qf, kf, kfo = qf_ref[...], kf_ref[...], kfo_ref[...]
    k, v, ko, vo = k_ref[...], v_ref[...], ko_ref[...], vo_ref[...]
    one = jnp.ones_like(v)
    outs, stats = [], []
    for head in range(2):
        mine = low_lanes if head == 0 else jnp.logical_not(low_lanes)
        qa = jnp.where(mine, q, qf)
        ka = jnp.concatenate([jnp.where(mine, k, kf), jnp.where(mine, ko, kfo)], axis=0)
        va = jnp.concatenate([jnp.where(mine, v, one), jnp.where(mine, vo, one)], axis=0)
        if causal:
            pieces = [
                (0, half, [(0, half), (size, size + half)], 0),
                (half, size, [(0, 2 * size)], half),
            ]
        else:
            pieces = [(0, size, [(0, 2 * size)], None)]
        o_rows, s_rows = [], []
        for start, stop, spans, diagonal in pieces:
            kk = jnp.concatenate([ka[a:b] for a, b in spans], axis=0)
            vv = jnp.concatenate([va[a:b] for a, b in spans], axis=0)
            s = lax.dot_general(
                qa[start:stop], kk, (((1,), (1,)), ((), ())), preferred_element_type=F32
            )
            if diagonal is not None:
                row = lax.broadcasted_iota(jnp.int32, (half, half), 0)
                col = lax.broadcasted_iota(jnp.int32, (half, half), 1)
                cut = jnp.where(col <= row, s[:, diagonal : diagonal + half], NEGATIVE)
                s = replace_block(s, cut, diagonal, 1)
            top = jnp.max(s, axis=1, keepdims=True)
            p = jnp.exp(s - top).astype(BF)
            o = lax.dot_general(p, vv, (((1,), (0,)), ((), ())), preferred_element_type=F32)
            o_rows.append(o / pltpu.roll(o, DH, 1))
            s_rows.append(top + jnp.log(o))
        outs.append(jnp.concatenate(o_rows, axis=0))
        stats.append(jnp.concatenate(s_rows, axis=0))
    o_ref[...] = jnp.where(low_lanes, outs[0], outs[1]).astype(BF)
    lse_ref[...] = jnp.where(low_lanes, stats[1], stats[0])


def split3(value):
    a = value.astype(BF)
    rest = value - a.astype(F32)
    b = rest.astype(BF)
    c = (rest - b.astype(F32)).astype(BF)
    return a, b, c


def with_stat(base, value, lane):
    a, b, c = split3(-value)
    at = lane & (DH - 1)
    base = jnp.where(at == STAT, a, base)
    base = jnp.where(at == STAT + 1, b, base)
    return jnp.where(at == STAT + 2, c, base)


def attend_back_kernel(
    causal,
    q_ref, k_ref, v_ref, ko_ref, vo_ref, qf_ref, kf_ref, kfo_ref, o_ref, lse_ref, do_ref,
    dq_ref, dk_ref, dv_ref, dko_ref, dvo_ref,
):
    size = q_ref.shape[0]
    half = size // 2
    lane = lax.broadcasted_iota(jnp.int32, (size, PAIR), 1)
    low_lanes = lane < DH
    scale = DH ** (-0.5)
    q = q_ref[...] * jnp.array(scale, BF)
    qf, kf, kfo = qf_ref[...], kf_ref[...], kfo_ref[...]
    k, v, ko, vo = k_ref[...], v_ref[...], ko_ref[...], vo_ref[...]
    do = do_ref[...]
    product = do.astype(F32) * o_ref[...].astype(F32)
    qstat = with_stat(qf, lse_ref[...], lane)
    kall = jnp.concatenate([k, ko], axis=0)
    zero = jnp.zeros_like(do)
    dqs, dks, dvs = [], [], []
    for head in range(2):
        mine = low_lanes if head == 0 else jnp.logical_not(low_lanes)
        inner = jnp.sum(jnp.where(mine, product, 0.0), axis=1, keepdims=True)
        dstat = with_stat(zero, jnp.broadcast_to(inner, product.shape), lane)
        qa = jnp.where(mine, q, qstat)
        da = jnp.where(mine, do, dstat)
        ka = jnp.concatenate([jnp.where(mine, k, kf), jnp.where(mine, ko, kfo)], axis=0)
        va = jnp.concatenate([jnp.where(mine, v, kf), jnp.where(mine, vo, kfo)], axis=0)
        if causal:
            pieces = [
                (0, half, [(0, half), (size, size + half)], 0),
                (half, size, [(0, 2 * size)], half),
            ]
        else:
            pieces = [(0, size, [(0, 2 * size)], None)]
        dq_rows = []
        dk_parts = [None] * 4
        dv_parts = [None] * 4
        for start, stop, spans, diagonal in pieces:
            kk = jnp.concatenate([ka[a:b] for a, b in spans], axis=0)
            vv = jnp.concatenate([va[a:b] for a, b in spans], axis=0)
            kp = jnp.concatenate([kall[a:b] for a, b in spans], axis=0)
            s = lax.dot_general(
                kk, qa[start:stop], (((1,), (1,)), ((), ())), preferred_element_type=F32
            )
            if diagonal is not None:
                row = lax.broadcasted_iota(jnp.int32, (half, half), 0)
                col = lax.broadcasted_iota(jnp.int32, (half, half), 1)
                cut = jnp.where(row <= col, s[diagonal : diagonal + half], NEGATIVE)
                s = replace_block(s, cut, diagonal, 0)
            p = jnp.exp(s)
            dp = lax.dot_general(
                vv, da[start:stop], (((1,), (1,)), ((), ())), preferred_element_type=F32
            )
            ds = (p * dp).astype(BF)
            pb = p.astype(BF)
            dv = lax.dot_general(
                pb, do[start:stop], (((1,), (0,)), ((), ())), preferred_element_type=F32
            )
            dk = lax.dot_general(
                ds, q[start:stop], (((1,), (0,)), ((), ())), preferred_element_type=F32
            )
            dq = lax.dot_general(
                ds, kp, (((0,), (0,)), ((), ())), preferred_element_type=F32
            )
            dq_rows.append(dq * scale)
            at = 0
            for a, b in spans:
                for block in range(a // half, b // half):
                    rows = slice(at, at + half)
                    dk_parts[block] = (
                        dk[rows] if dk_parts[block] is None else dk_parts[block] + dk[rows]
                    )
                    dv_parts[block] = (
                        dv[rows] if dv_parts[block] is None else dv_parts[block] + dv[rows]
                    )
                    at += half
        dqs.append(jnp.concatenate(dq_rows, axis=0))
        dks.append(jnp.concatenate(dk_parts, axis=0))
        dvs.append(jnp.concatenate(dv_parts, axis=0))
    dq_ref[...] = jnp.where(low_lanes, dqs[0], dqs[1]).astype(BF)
    dk_ref[...] = jnp.where(low_lanes, dks[0][:size], dks[1][:size])
    dv_ref[...] = jnp.where(low_lanes, dvs[0][:size], dvs[1][:size])
    dko_ref[...] = jnp.where(low_lanes, dks[0][size:], dks[1][size:]).astype(BF)
    dvo_ref[...] = jnp.where(low_lanes, dvs[0][size:], dvs[1][size:]).astype(BF)


def column(size, at):
    return pl.BlockSpec((size, PAIR), lambda p: (0, at + p))


def shared(size):
    return pl.BlockSpec((size, PAIR), lambda p: (0, 0))


def attend_forward(q, k, v, ko, vo, qf, kf, kfo, causal):
    size = q[0].shape[0]
    steps = 8 // 2
    width = steps * PAIR
    return pl.pallas_call(
        functools.partial(attend_kernel, causal),
        grid=(steps,),
        in_specs=[column(size, x[1]) for x in (q, k, v, ko, vo)] + [shared(size)] * 3,
        out_specs=[column(size, 0)] * 2,
        out_shape=[
            jax.ShapeDtypeStruct((size, width), BF),
            jax.ShapeDtypeStruct((size, width), F32),
        ],
        compiler_params=pltpu.CompilerParams(vmem_limit_bytes=48 << 20),
        cost_estimate=pl.CostEstimate(
            flops=16 * size * size * width, bytes_accessed=16 * size * width, transcendentals=0
        ),
        name="attend_forward",
    )(q[0], k[0], v[0], ko[0], vo[0], qf, kf, kfo)


def attend_backward(q, k, v, ko, vo, qf, kf, kfo, o, lse, do, causal):
    size = q[0].shape[0]
    steps = 8 // 2
    width = steps * PAIR
    return pl.pallas_call(
        functools.partial(attend_back_kernel, causal),
        grid=(steps,),
        in_specs=[column(size, x[1]) for x in (q, k, v, ko, vo)]
        + [shared(size)] * 3
        + [column(size, 0)] * 3,
        out_specs=[column(size, 0)] * 5,
        out_shape=[
            jax.ShapeDtypeStruct((size, width), BF),
            jax.ShapeDtypeStruct((size, width), F32),
            jax.ShapeDtypeStruct((size, width), F32),
            jax.ShapeDtypeStruct((size, width), BF),
            jax.ShapeDtypeStruct((size, width), BF),
        ],
        compiler_params=pltpu.CompilerParams(vmem_limit_bytes=48 << 20),
        cost_estimate=pl.CostEstimate(
            flops=40 * size * size * width, bytes_accessed=30 * size * width, transcendentals=0
        ),
        name="attend_backward",
    )(q[0], k[0], v[0], ko[0], vo[0], qf, kf, kfo, o, lse, do)


def dot(a, b):
    return lax.dot_general(a, b, (((1,), (0,)), ((), ())), preferred_element_type=F32)


def dot_back(a, b):
    return lax.dot_general(a, b, (((1,), (1,)), ((), ())), preferred_element_type=F32)


def dot_outer(a, b):
    return lax.dot_general(a, b, (((0,), (0,)), ((), ())), preferred_element_type=F32)


def sum_over_all(part, core, group, depth, to_cores):
    rows = part.shape[0]
    half = rows // 2

    def take(value, at, count):
        return lax.dynamic_slice_in_dim(value, at * count, count, 0)

    def across(value, first):
        def move(c, g, z):
            return (c, g ^ (1 if (c == 0) == first else 2), z)

        return swap(value, move)

    along1 = functools.partial(swap, move=lambda c, g, z: (c, g, z ^ 1))
    along2 = functools.partial(swap, move=lambda c, g, z: (c, g, z ^ 2))
    bit_x, bit_y = group & 1, group >> 1
    bits = [
        core,
        jnp.where(core == 0, bit_x, bit_y),
        jnp.where(core == 0, bit_y, bit_x),
        depth & 1,
        depth >> 1,
    ]
    moves = [
        to_core,
        functools.partial(across, first=True),
        functools.partial(across, first=False),
        along1,
        along2,
    ]
    value = part
    count = rows
    for bit, move in zip(bits, moves):
        count //= 2
        arrived = move(take(value, 1 - bit, count))
        value = (take(value, bit, count).astype(F32) + arrived.astype(F32)).astype(BF)
    for bit, move in list(zip(bits, moves))[:0:-1]:
        arrived = move(value)
        value = jnp.where(
            bit == 0,
            jnp.concatenate([value, arrived], axis=0),
            jnp.concatenate([arrived, value], axis=0),
        )
    return value


def join_cores(value, core, from_core):
    if from_core is None:
        arrived = to_core(value)
    else:
        arrived = swap(value, lambda c, g, z: (1 - c, g, z) if c == from_core else None)
    return jnp.where(
        core == 0,
        jnp.concatenate([value, arrived], axis=0),
        jnp.concatenate([arrived, value], axis=0),
    )


def row_shards(
    inputs,
    cotangent,
    qkv_weight,
    out_weight,
    up_weight,
    down_weight,
    norm_gain,
    norm_bias,
    cross_q_weight,
    cross_kv_weight,
    cross_out_weight,
    cross_gain,
    cross_bias,
    source_segments,
    target_segments,
):
    core = lax.axis_index("section")
    group = lax.axis_index("dp")
    depth = lax.axis_index("seq")
    tokens = inputs[0]
    span = tokens.shape[1]
    width = tokens.shape[2]
    seat = 2 * core + (depth >> 1)

    arrived = []
    for k in range(4):
        block = lax.dynamic_index_in_dim(tokens, seat ^ k, 0, keepdims=False)
        arrived.append(
            swap(block, lambda c, g, z: (side_of(z), g, (2 * c + (z >> 1)) ^ k))
        )
    blocks = pick(arrived, depth)
    xs = jnp.concatenate(blocks[:2], axis=0)
    xt = jnp.concatenate(blocks[2:], axis=0)

    own = (qkv_weight[0], out_weight[0], up_weight[0], down_weight[0], norm_gain[0], norm_bias[0])
    other = tuple(to_core(w) for w in own)
    wqkv_e, wo_e, wu_e, wd_e, g_e, b_e = (jnp.where(core == 0, a, b) for a, b in zip(own, other))
    wqkv_d, wo_d, wu_d, wd_d, g_d, b_d = (jnp.where(core == 0, b, a) for a, b in zip(own, other))

    cots = []
    for k in range(2):
        block = lax.dynamic_index_in_dim(cotangent, seat ^ k, 0, keepdims=False)
        cots.append(swap(block, lambda c, g, z: (side_of(z), g, (2 * c + (z >> 1)) ^ k)))
    odd = (depth & 1) == 1
    cot = jnp.concatenate(
        [jnp.where(odd, cots[1], cots[0]), jnp.where(odd, cots[0], cots[1])], axis=0
    ).astype(F32)

    seg_s = lax.dynamic_index_in_dim(source_segments, depth, 0, keepdims=False).reshape(4, span)
    seg_t = lax.dynamic_index_in_dim(target_segments, depth, 0, keepdims=False).reshape(4, span)

    def in_order(seg):
        outer, inner = seg[jnp.array([0, 3])].reshape(-1), seg[jnp.array([1, 2])].reshape(-1)
        return jnp.where(core == 0, outer, inner), jnp.where(core == 0, inner, outer)

    lane = lax.broadcasted_iota(jnp.int32, (2 * span, PAIR), 1) & (DH - 1)
    late = lax.broadcasted_iota(jnp.int32, (2 * span, PAIR), 0) >= span

    def query_features(seg):
        hit = (seg[:, None] == lane) & (lane < 4)
        hit = hit | ((lane == 4) & ~late) | ((lane == 5) & late)
        return hit.astype(BF)

    def key_features(seg, barred):
        bad = ((seg[:, None] != lane) & (lane < 4)) | barred
        value = jnp.where(bad, NEGATIVE, 0.0)
        return jnp.where((lane >= STAT) & (lane < STAT + 3), 1.0, value).astype(BF)

    none = jnp.zeros(lane.shape, bool)
    seg_s0, seg_s1 = in_order(seg_s)
    seg_t0, seg_t1 = in_order(seg_t)
    qf_s, qf_t = query_features(seg_s0), query_features(seg_t0)
    kf_s0, kf_s1 = key_features(seg_s0, none), key_features(seg_s1, none)
    kf_t0 = key_features(seg_t0, (lane == 4) & late)
    kf_t1 = key_features(
        seg_t1, ((lane == 4) & (late | (core == 0))) | ((lane == 5) & late & (core == 1))
    )

    qkv_s = dot(xs, wqkv_e).astype(BF)
    kv_s1 = to_core(qkv_s[:, width:])
    qkv_t = dot(xt, wqkv_d).astype(BF)
    kv_t1 = to_core(qkv_t[:, width:])
    arg_s = ((qkv_s, 0), (qkv_s, 4), (qkv_s, 8), (kv_s1, 0), (kv_s1, 4), qf_s, kf_s0, kf_s1)
    o_s, lse_s = attend_forward(*arg_s, False)
    s1 = xs.astype(F32) + dot(o_s, wo_e)
    h_s = layer_norm(s1, g_e[0], b_e[0])
    h_s_low = h_s.astype(BF)
    u_s = dot(h_s_low, wu_e)
    gel_s = gelu_tanh(u_s).astype(BF)
    s2 = h_s + dot(gel_s, wd_e)
    memory = layer_norm(s2, g_e[1], b_e[1]).astype(BF)
    ckv = dot(memory, cross_kv_weight).astype(BF)
    ckv1 = to_core(ckv)

    arg_t = ((qkv_t, 0), (qkv_t, 4), (qkv_t, 8), (kv_t1, 0), (kv_t1, 4), qf_t, kf_t0, kf_t1)
    o_t, lse_t = attend_forward(*arg_t, True)
    t1 = xt.astype(F32) + dot(o_t, wo_d)
    h_t = layer_norm(t1, g_d[0], b_d[0])
    h_t_low = h_t.astype(BF)
    cq = dot(h_t_low, cross_q_weight).astype(BF)
    arg_c = ((cq, 0), (ckv, 0), (ckv, 4), (ckv1, 0), (ckv1, 4), qf_t, kf_s0, kf_s1)
    o_c, lse_c = attend_forward(*arg_c, False)
    t2 = h_t + dot(o_c, cross_out_weight)
    c_t = layer_norm(t2, cross_gain, cross_bias)
    c_t_low = c_t.astype(BF)
    u_t = dot(c_t_low, wu_d)
    gel_t = gelu_tanh(u_t).astype(BF)
    t3 = c_t + dot(gel_t, wd_d)
    decoded, pull_t3 = jax.vjp(layer_norm, t3, g_d[1], b_d[1])
    decoded = decoded.astype(BF)

    grad_t3, gg_d1, gb_d1 = pull_t3(cot)
    low_t3 = grad_t3.astype(BF)
    gw_down_d = dot_outer(gel_t, low_t3)
    grad_u_t = jax.vjp(gelu_tanh, u_t)[1](dot_back(low_t3, wd_d))[0].astype(BF)
    gw_up_d = dot_outer(c_t_low, grad_u_t)
    grad_c = grad_t3 + dot_back(grad_u_t, wu_d)
    grad_t2, gg_c, gb_c = jax.vjp(layer_norm, t2, cross_gain, cross_bias)[1](grad_c)
    low_t2 = grad_t2.astype(BF)
    gw_cross_out = dot_outer(o_c, low_t2)
    grad_o_c = dot_back(low_t2, cross_out_weight).astype(BF)
    grad_cq, gk, gv, gk1, gv1 = attend_backward(*arg_c, o_c, lse_c, grad_o_c, False)
    gkv1 = to_core(jnp.concatenate([gk1, gv1], axis=1))
    grad_ckv = (jnp.concatenate([gk, gv], axis=1) + gkv1.astype(F32)).astype(BF)
    gw_cross_q = dot_outer(h_t_low, grad_cq)
    grad_h = grad_t2 + dot_back(grad_cq, cross_q_weight)
    grad_t1, gg_d0, gb_d0 = jax.vjp(layer_norm, t1, g_d[0], b_d[0])[1](grad_h)
    low_t1 = grad_t1.astype(BF)
    gw_out_d = dot_outer(o_t, low_t1)
    grad_o_t = dot_back(low_t1, wo_d).astype(BF)
    gq, gk, gv, gk1, gv1 = attend_backward(*arg_t, o_t, lse_t, grad_o_t, True)
    gkv1 = to_core(jnp.concatenate([gk1, gv1], axis=1))
    grad_kv = (jnp.concatenate([gk, gv], axis=1) + gkv1.astype(F32)).astype(BF)
    grad_qkv_t = jnp.concatenate([gq, grad_kv], axis=1)
    gw_qkv_d = dot_outer(xt, grad_qkv_t)
    grad_xt = grad_t1 + dot_back(grad_qkv_t, wqkv_d)

    gw_cross_kv = dot_outer(memory, grad_ckv)
    grad_memory = dot_back(grad_ckv, cross_kv_weight).astype(BF).astype(F32)
    grad_s2, gg_e1, gb_e1 = jax.vjp(layer_norm, s2, g_e[1], b_e[1])[1](grad_memory)
    low_s2 = grad_s2.astype(BF)
    gw_down_e = dot_outer(gel_s, low_s2)
    grad_u_s = jax.vjp(gelu_tanh, u_s)[1](dot_back(low_s2, wd_e))[0].astype(BF)
    gw_up_e = dot_outer(h_s_low, grad_u_s)
    grad_h = grad_s2 + dot_back(grad_u_s, wu_e)
    grad_s1, gg_e0, gb_e0 = jax.vjp(layer_norm, s1, g_e[0], b_e[0])[1](grad_h)
    low_s1 = grad_s1.astype(BF)
    gw_out_e = dot_outer(o_s, low_s1)
    grad_o_s = dot_back(low_s1, wo_e).astype(BF)
    gq, gk, gv, gk1, gv1 = attend_backward(*arg_s, o_s, lse_s, grad_o_s, False)
    gkv1 = to_core(jnp.concatenate([gk1, gv1], axis=1))
    grad_kv = (jnp.concatenate([gk, gv], axis=1) + gkv1.astype(F32)).astype(BF)
    grad_qkv_s = jnp.concatenate([gq, grad_kv], axis=1)
    gw_qkv_e = dot_outer(xs, grad_qkv_s)
    grad_xs = grad_s1 + dot_back(grad_qkv_s, wqkv_e)

    def home(source, target):
        parts = [source[:span], source[span:], target[:span], target[span:]]
        sent = pick(parts, depth)
        back = [
            swap(
                sent[k],
                lambda c, g, z: ((z ^ k) >> 1, g, block_of(c, (z ^ k) & 1)),
            )
            for k in range(4)
        ]
        return jnp.stack(pick(back, seat))

    outputs = home(memory, decoded)
    grads = home(grad_xs.astype(BF), grad_xt.astype(BF)).astype(F32)

    def fold(value):
        return value.reshape(-1, width, value.shape[1])

    def pack(parts):
        return jnp.concatenate([p.astype(BF) for p in parts], axis=1)

    def down_columns(value):
        return [value[i * width : (i + 1) * width] for i in range(value.shape[0] // width)]

    ffn_d = pack([gw_up_d] + down_columns(gw_down_d))
    rest_d = pack([gw_cross_out, gw_cross_q, gw_out_d, gw_qkv_d])
    ffn_e = pack([gw_cross_kv, gw_up_e] + down_columns(gw_down_e))
    rest_e = pack([gw_out_e, gw_qkv_e])
    ffn_d, rest_d, ffn_e, rest_e = (
        sum_over_all(v, core, group, depth, None) for v in (ffn_d, rest_d, ffn_e, rest_e)
    )
    kv_at = cross_kv_weight.shape[1]
    shared_part = join_cores(
        jnp.concatenate([rest_d[:, : 2 * width], ffn_e[:, :kv_at]], axis=1), core, None
    )
    mine = jnp.where(
        core == 0,
        jnp.concatenate([ffn_e[:, kv_at:], rest_e], axis=1),
        jnp.concatenate([ffn_d, rest_d[:, 2 * width :]], axis=1),
    )
    theirs = jnp.where(
        core == 0,
        jnp.concatenate([ffn_d, rest_d[:, 2 * width :]], axis=1),
        jnp.concatenate([ffn_e[:, kv_at:], rest_e], axis=1),
    )
    lacking = to_core(theirs)
    whole = jnp.where(
        core == 0,
        jnp.concatenate([mine, lacking], axis=0),
        jnp.concatenate([lacking, mine], axis=0),
    ).astype(F32)
    shared_part = shared_part.astype(F32)
    ff = up_weight.shape[2]
    g_up = whole[:, :ff]
    g_down = jnp.concatenate(
        [whole[:, ff + i * width : ff + (i + 1) * width] for i in range(ff // width)], axis=0
    )
    g_out = whole[:, 2 * ff : 2 * ff + width]
    g_qkv = whole[:, 2 * ff + width :]
    g_cross_out = shared_part[:, :width]
    g_cross_q = shared_part[:, width : 2 * width]
    g_cross_kv = shared_part[:, 2 * width :]

    small = jnp.stack(
        [gg_e0, gg_e1, gb_e0, gb_e1, gg_d0, gg_d1, gb_d0, gb_d1, gg_c, gb_c]
        + [jnp.zeros_like(gg_c)] * 6
    )
    for move in (
        to_core,
        functools.partial(swap, move=lambda c, g, z: (c, g ^ 1, z)),
        functools.partial(swap, move=lambda c, g, z: (c, g ^ 2, z)),
        functools.partial(swap, move=lambda c, g, z: (c, g, z ^ 1)),
        functools.partial(swap, move=lambda c, g, z: (c, g, z ^ 2)),
    ):
        small = small + move(small)
    layer_small = jnp.where(core == 0, small[:4], small[4:8])
    return (
        outputs[None],
        grads[None],
        g_qkv[None],
        g_out[None],
        g_up[None],
        g_down[None],
        layer_small[None, :2],
        layer_small[None, 2:],
        g_cross_q,
        g_cross_kv,
        g_cross_out,
        small[8],
        small[9],
    )


def solution(mesh):
    in_specs = (
        P("section", "dp", "seq", None),
        P("dp", "seq", None),
        P("section", None, None),
        P("section", None, None),
        P("section", None, None),
        P("section", None, None),
        P("section", None, None),
        P("section", None, None),
        P(),
        P(),
        P(),
        P(),
        P(),
        P("dp", None),
        P("dp", None),
    )
    out_specs = (
        P("section", "dp", "seq", None),
        P("section", "dp", "seq", None),
        P("section", None, None),
        P("section", None, None),
        P("section", None, None),
        P("section", None, None),
        P("section", None, None),
        P("section", None, None),
        P(),
        P(),
        P(),
        P(),
        P(),
    )
    whole_rows = mesh.shape["section"] == 2 and mesh.shape["seq"] == 4 and mesh.shape["dp"] == 4
    body = row_shards if whole_rows else shards
    return jax.shard_map(body, mesh=mesh, in_specs=in_specs, out_specs=out_specs, check_vma=False)
```

```python
import functools

import jax
import jax.numpy as jnp
from jax import lax
from jax.experimental import pallas as pl
from jax.experimental.pallas import tpu as pltpu
from jax.sharding import PartitionSpec as P

DH = 64
MICRO = 2
MB_ROWS = 2


EPSILON = 1e-05
NEGATIVE = -1e30


def from_behind(value, axis, steps):
    count = lax.axis_size(axis)
    leading, last = (max(0, -steps), min(count, count - steps))
    return lax.ppermute(value, axis, [(source, source + steps) for source in range(leading, last)])


def layer_norm(vector, gain_row, bias_row):
    centre = vector - jnp.mean(vector, axis=-1, keepdims=True)
    spread = jnp.mean(centre * centre, axis=-1, keepdims=True)
    return centre * lax.rsqrt(spread + EPSILON) * gain_row + bias_row


def gelu_tanh(vector):
    return jax.nn.gelu(vector, approximate=True)


def heads_view(vector):
    return vector.reshape(vector.shape[:-1] + (vector.shape[-1] // DH, DH))


def joined_view(vector):
    return vector.reshape(vector.shape[:-2] + (vector.shape[-2] * vector.shape[-1],))


def dense_rows(left_side, right_side):
    return jnp.einsum("rsd,de->rse", left_side, right_side, preferred_element_type=jnp.float32)


def dense_back(left_side, right_side):
    return jnp.einsum("rse,de->rsd", left_side, right_side, preferred_element_type=jnp.float32)


def outer_sum(left_side, right_side):
    return jnp.einsum("rsd,rse->de", left_side, right_side, preferred_element_type=jnp.float32)


def build_mask(query_ids, key_ids, query_places, key_places, causal):
    same_doc = query_ids[:, :, None] == key_ids[:, None, :]
    ordered = (key_places[None, :] <= query_places[:, None]) | jnp.logical_not(causal)
    return same_doc & ordered[None]


def soft_forward(queries, key_rows, value_rows, allowed):
    score_scale = DH ** (-0.5)
    scores = (
        jnp.einsum(
            "rqhe,rkhe->rhqk",
            heads_view(queries),
            heads_view(key_rows),
            preferred_element_type=jnp.float32,
        )
        * score_scale
    )
    scores = jnp.where(allowed[:, None], scores, NEGATIVE)
    highest = jnp.max(scores, axis=-1, keepdims=True)
    exp_terms = jnp.exp(scores - highest)
    totals = jnp.sum(exp_terms, axis=-1, keepdims=True)
    weights = exp_terms / totals
    log_total = (highest + jnp.log(totals))[..., 0]
    mixed_out = jnp.einsum(
        "rhqk,rkhe->rqhe",
        weights.astype(jnp.bfloat16),
        heads_view(value_rows),
        preferred_element_type=jnp.float32,
    )
    return (joined_view(mixed_out), weights, log_total)


def score_grads(grad_mixed, value_rows, weights):
    grad_weights = jnp.einsum(
        "rqhe,rkhe->rhqk",
        heads_view(grad_mixed),
        heads_view(value_rows),
        preferred_element_type=jnp.float32,
    )
    inner_sum = jnp.sum(grad_weights * weights, axis=-1, keepdims=True)
    grad_scores = (weights * (grad_weights - inner_sum)).astype(jnp.bfloat16)
    return (grad_scores, inner_sum[..., 0])


def attend_keys(queries, key_rows, value_rows, query_ids, key_ids, causal):
    span_len = key_rows.shape[1]
    offset = lax.axis_index("seq") * span_len
    whole_keys, whole_values = (
        lax.all_gather(key_rows, "seq", axis=1, tiled=True),
        lax.all_gather(value_rows, "seq", axis=1, tiled=True),
    )
    own_positions = offset + jnp.arange(span_len)
    all_positions = jnp.arange(whole_keys.shape[1])
    own_ids = lax.dynamic_slice_in_dim(query_ids, offset, span_len, 1)
    allowed = build_mask(own_ids, key_ids, own_positions, all_positions, causal)
    mixed_out, weights, log_total = soft_forward(queries, whole_keys, whole_values, allowed)
    kept_state = (
        queries,
        key_rows,
        value_rows,
        whole_keys,
        whole_values,
        weights,
        log_total,
        query_ids,
        key_ids,
        causal,
    )
    return (mixed_out, kept_state)


def attend_back(kept_state, grad_mixed):
    (
        queries,
        key_rows,
        value_rows,
        whole_keys,
        whole_values,
        weights,
        log_total,
        query_ids,
        key_ids,
        causal,
    ) = kept_state
    score_scale = DH ** (-0.5)
    grad_scores, inner_sum = score_grads(grad_mixed, whole_values, weights)
    grad_queries = (
        jnp.einsum(
            "rhqk,rkhe->rqhe",
            grad_scores,
            heads_view(whole_keys),
            preferred_element_type=jnp.float32,
        )
        * score_scale
    )
    part_keys = (
        jnp.einsum(
            "rhqk,rqhe->rkhe", grad_scores, heads_view(queries), preferred_element_type=jnp.float32
        )
        * score_scale
    )
    part_values = jnp.einsum(
        "rhqk,rqhe->rkhe",
        weights.astype(jnp.bfloat16),
        heads_view(grad_mixed),
        preferred_element_type=jnp.float32,
    )
    grad_keys, grad_values = (
        lax.psum_scatter(
            joined_view(part_keys).astype(jnp.bfloat16), "seq", scatter_dimension=1, tiled=True
        ).astype(jnp.float32),
        lax.psum_scatter(
            joined_view(part_values).astype(jnp.bfloat16), "seq", scatter_dimension=1, tiled=True
        ).astype(jnp.float32),
    )
    return (joined_view(grad_queries), grad_keys, grad_values)


def layer_forward(tokens, memory_in, own_ids, source_ids, target_ids, params, decoder):
    (
        qkv_matrix,
        out_matrix,
        up_matrix,
        down_matrix,
        norm_gains,
        norm_biases,
        query_matrix,
        pair_matrix,
        cross_matrix,
        cross_gains,
        cross_shift,
    ) = params
    residual = tokens.astype(jnp.float32)
    packed = dense_rows(tokens, qkv_matrix).astype(jnp.bfloat16)
    queries, key_rows, value_rows = jnp.split(packed, 3, axis=-1)
    mixed_out, self_state = attend_keys(queries, key_rows, value_rows, own_ids, own_ids, decoder)
    mixed_low = mixed_out.astype(jnp.bfloat16)
    first_sum = residual + dense_rows(mixed_low, out_matrix)
    first_norm = layer_norm(first_sum, norm_gains[0], norm_biases[0])
    first_low = first_norm.astype(jnp.bfloat16)
    cross_query = dense_rows(first_low, query_matrix).astype(jnp.bfloat16)
    cross_pair = dense_rows(memory_in, pair_matrix).astype(jnp.bfloat16)
    cross_keys, cross_values = jnp.split(cross_pair, 2, axis=-1)
    cross_mixed, cross_state = attend_keys(
        cross_query, cross_keys, cross_values, target_ids, source_ids, False
    )
    cross_low = cross_mixed.astype(jnp.bfloat16)
    cross_sum = first_norm + dense_rows(cross_low, cross_matrix)
    second = jnp.where(decoder, layer_norm(cross_sum, cross_gains, cross_shift), first_norm)
    second_low = second.astype(jnp.bfloat16)
    upward = dense_rows(second_low, up_matrix)
    gated_low = gelu_tanh(upward).astype(jnp.bfloat16)
    last_sum = second + dense_rows(gated_low, down_matrix)
    output = layer_norm(last_sum, norm_gains[1], norm_biases[1])
    kept_state = (
        tokens,
        self_state,
        mixed_low,
        first_sum,
        first_low,
        cross_state,
        cross_low,
        cross_sum,
        second_low,
        upward,
        gated_low,
        last_sum,
    )
    return (output, kept_state)


def layer_backward(kept_state, grad_out, params, decoder):
    (
        qkv_matrix,
        out_matrix,
        up_matrix,
        down_matrix,
        norm_gains,
        norm_biases,
        query_matrix,
        pair_matrix,
        cross_matrix,
        cross_gains,
        cross_shift,
    ) = params
    (
        tokens,
        self_state,
        mixed_low,
        first_sum,
        first_low,
        cross_state,
        cross_low,
        cross_sum,
        second_low,
        upward,
        gated_low,
        last_sum,
    ) = kept_state
    unused, pull_last = jax.vjp(layer_norm, last_sum, norm_gains[1], norm_biases[1])
    grad_last, grad_gain_last, grad_bias_last = pull_last(grad_out)
    down_in = grad_last.astype(jnp.bfloat16)
    grad_down = outer_sum(gated_low, down_in)
    grad_gated = dense_back(down_in, down_matrix)
    unused, pull_gelu = jax.vjp(gelu_tanh, upward)
    up_in = pull_gelu(grad_gated)[0].astype(jnp.bfloat16)
    grad_up = outer_sum(second_low, up_in)
    grad_second = grad_last + dense_back(up_in, up_matrix)
    unused, pull_cross = jax.vjp(layer_norm, cross_sum, cross_gains, cross_shift)
    grad_cross_sum, grad_cross_gain, grad_cross_bias = pull_cross(
        jnp.where(decoder, grad_second, 0.0)
    )
    grad_first = jnp.where(decoder, grad_cross_sum, grad_second)
    cross_in = grad_cross_sum.astype(jnp.bfloat16)
    grad_cross_out = outer_sum(cross_low, cross_in)
    grad_cross_mixed = dense_back(cross_in, cross_matrix).astype(jnp.bfloat16)
    grad_cross_query, grad_cross_keys, grad_cross_values = attend_back(
        cross_state, grad_cross_mixed
    )
    query_in = grad_cross_query.astype(jnp.bfloat16)
    grad_query_matrix = outer_sum(first_low, query_in)
    grad_first = grad_first + dense_back(query_in, query_matrix)
    pair_in = jnp.concatenate([grad_cross_keys, grad_cross_values], axis=-1).astype(jnp.bfloat16)
    unused, pull_first = jax.vjp(layer_norm, first_sum, norm_gains[0], norm_biases[0])
    grad_first_sum, grad_gain_first, grad_bias_first = pull_first(grad_first)
    out_in = grad_first_sum.astype(jnp.bfloat16)
    grad_out_matrix = outer_sum(mixed_low, out_in)
    grad_mixed = dense_back(out_in, out_matrix).astype(jnp.bfloat16)
    grad_queries, grad_keys, grad_values = attend_back(self_state, grad_mixed)
    qkv_in = jnp.concatenate([grad_queries, grad_keys, grad_values], axis=-1).astype(jnp.bfloat16)
    grad_qkv_matrix = outer_sum(tokens, qkv_in)
    grad_tokens = grad_first_sum + dense_back(qkv_in, qkv_matrix)
    grad_set = (
        grad_qkv_matrix,
        grad_out_matrix,
        grad_up,
        grad_down,
        jnp.stack([grad_gain_first, grad_gain_last]),
        jnp.stack([grad_bias_first, grad_bias_last]),
        grad_query_matrix,
        jnp.zeros(pair_matrix.shape, jnp.float32),
        grad_cross_out,
        grad_cross_gain,
        grad_cross_bias,
    )
    return (grad_tokens, pair_in, grad_set)


def shards(
    inputs,
    cotangent,
    qkv_weight,
    out_weight,
    up_weight,
    down_weight,
    norm_gain,
    norm_bias,
    cross_q_weight,
    cross_kv_weight,
    cross_out_weight,
    cross_gain,
    cross_bias,
    source_segments,
    target_segments,
):
    section_index = lax.axis_index("section")
    decoder = section_index == 1
    params = (
        qkv_weight[0],
        out_weight[0],
        up_weight[0],
        down_weight[0],
        norm_gain[0],
        norm_bias[0],
        cross_q_weight,
        cross_kv_weight,
        cross_out_weight,
        cross_gain,
        cross_bias,
    )
    tokens_all = inputs[0]
    own_all = jnp.where(decoder, target_segments, source_segments)
    span_len = tokens_all.shape[1]
    features = tokens_all.shape[2]
    memory_in = jnp.zeros((MB_ROWS, span_len, features), jnp.bfloat16)
    outputs_all = jnp.zeros(tokens_all.shape, jnp.bfloat16)
    caches = []
    sent_rows = []
    for forward_tick in range(MICRO + 1):
        micro_index = forward_tick - section_index
        active = (micro_index >= 0) & (micro_index < MICRO)
        first_row = jnp.clip(micro_index, 0, MICRO - 1) * MB_ROWS
        rows_now = lax.dynamic_slice_in_dim(tokens_all, first_row, MB_ROWS, 0)
        own_now = lax.dynamic_slice_in_dim(own_all, first_row, MB_ROWS, 0)
        source_now = lax.dynamic_slice_in_dim(source_segments, first_row, MB_ROWS, 0)
        target_now = lax.dynamic_slice_in_dim(target_segments, first_row, MB_ROWS, 0)
        output, kept_state = layer_forward(
            rows_now, memory_in, own_now, source_now, target_now, params, decoder
        )
        output_low = output.astype(jnp.bfloat16)
        current = lax.dynamic_slice_in_dim(outputs_all, first_row, MB_ROWS, 0)
        outputs_all = lax.dynamic_update_slice_in_dim(
            outputs_all, jnp.where(active, output_low, current), first_row, 0
        )
        caches.append(kept_state)
        sent_rows.append(output_low)
        if forward_tick < MICRO:
            memory_in = from_behind(output_low, "section", 1)
    grad_pair_in = jnp.zeros((MB_ROWS, span_len, 2 * features), jnp.bfloat16)
    totals = tuple((jnp.zeros(param_item.shape, jnp.float32) for param_item in params))
    input_all = jnp.zeros(tokens_all.shape, jnp.float32)
    for backward_tick in range(MICRO + 1):
        forward_tick = MICRO - backward_tick
        micro_index = forward_tick - section_index
        active = (micro_index >= 0) & (micro_index < MICRO)
        first_row = jnp.clip(micro_index, 0, MICRO - 1) * MB_ROWS
        cot_now = lax.dynamic_slice_in_dim(cotangent, first_row, MB_ROWS, 0).astype(jnp.float32)
        memory_grad = lax.optimization_barrier(
            dense_back(grad_pair_in, params[7]).astype(jnp.bfloat16)
        ).astype(jnp.float32)
        pair_term = outer_sum(sent_rows[forward_tick], grad_pair_in)
        grad_out = jnp.where(decoder, cot_now, memory_grad)
        grad_tokens, pair_in, grad_set = layer_backward(
            caches[forward_tick], grad_out, params, decoder
        )
        grad_set = grad_set[:7] + (jnp.where(decoder, 0.0, pair_term),) + grad_set[8:]
        totals = jax.tree.map(
            lambda total_sum, new_term: total_sum + jnp.where(active, new_term, 0.0),
            totals,
            grad_set,
        )
        current = lax.dynamic_slice_in_dim(input_all, first_row, MB_ROWS, 0)
        input_all = lax.dynamic_update_slice_in_dim(
            input_all, jnp.where(active, grad_tokens, current), first_row, 0
        )
        if backward_tick < MICRO:
            grad_pair_in = from_behind(pair_in, "section", -1)
    layer_part = lax.psum(
        (totals[0], totals[1], totals[2], totals[3], totals[4], totals[5]), ("dp", "seq")
    )
    cross_part = lax.psum(
        (totals[6], totals[7], totals[8], totals[9], totals[10]), ("section", "dp", "seq")
    )
    return (
        outputs_all[None],
        input_all[None],
        layer_part[0][None],
        layer_part[1][None],
        layer_part[2][None],
        layer_part[3][None],
        layer_part[4][None],
        layer_part[5][None],
        cross_part[0],
        cross_part[1],
        cross_part[2],
        cross_part[3],
        cross_part[4],
    )


BF = jnp.bfloat16
F32 = jnp.float32
AXES = ("section", "dp", "seq")
PAIR = 2 * DH
STAT = 8


def swap(value, move):
    pairs = []
    for core in range(2):
        for group in range(4):
            for depth in range(4):
                to = move(core, group, depth)
                if to is not None:
                    pairs.append(
                        ((core * 4 + group) * 4 + depth, (to[0] * 4 + to[1]) * 4 + to[2])
                    )
    return lax.ppermute(value, AXES, pairs)


def to_core(value):
    return swap(value, lambda core, group, depth: (1 - core, group, depth))


def side_of(depth):
    return (depth ^ (depth >> 1)) & 1


def block_of(core, at):
    return 2 * at + (core ^ at)


def pick(parts, order):
    odd = (order & 1) == 1
    high = (order & 2) == 2
    a = [jnp.where(odd, parts[j ^ 1], parts[j]) for j in range(4)]
    return [jnp.where(high, a[j ^ 2], a[j]) for j in range(4)]


def replace_block(whole, block, at, axis):
    size, count = block.shape[axis], whole.shape[axis]
    parts = [lax.slice_in_dim(whole, 0, at, axis=axis)] if at > 0 else []
    parts.append(block)
    if at + size < count:
        parts.append(lax.slice_in_dim(whole, at + size, count, axis=axis))
    return jnp.concatenate(parts, axis=axis)


def attend_kernel(causal, q_ref, k_ref, v_ref, ko_ref, vo_ref, qf_ref, kf_ref, kfo_ref, o_ref, of_ref, lse_ref):
    size = q_ref.shape[0]
    half = size // 2
    lane = lax.broadcasted_iota(jnp.int32, (size, PAIR), 1)
    low_lanes = lane < DH
    q = q_ref[...] * jnp.array(DH ** (-0.5), BF)
    qf, kf, kfo = qf_ref[...], kf_ref[...], kfo_ref[...]
    k, v, ko, vo = k_ref[...], v_ref[...], ko_ref[...], vo_ref[...]
    one = jnp.ones_like(v)
    outs, stats = [], []
    for head in range(2):
        mine = low_lanes if head == 0 else jnp.logical_not(low_lanes)
        qa = jnp.where(mine, q, qf)
        ka = jnp.concatenate([jnp.where(mine, k, kf), jnp.where(mine, ko, kfo)], axis=0)
        va = jnp.concatenate([jnp.where(mine, v, one), jnp.where(mine, vo, one)], axis=0)
        if causal:
            pieces = [
                (0, half, [(0, half), (size, size + half)], 0),
                (half, size, [(0, 2 * size)], half),
            ]
        else:
            pieces = [(0, size, [(0, 2 * size)], None)]
        o_rows, s_rows = [], []
        for start, stop, spans, diagonal in pieces:
            kk = jnp.concatenate([ka[a:b] for a, b in spans], axis=0)
            vv = jnp.concatenate([va[a:b] for a, b in spans], axis=0)
            s = lax.dot_general(
                qa[start:stop], kk, (((1,), (1,)), ((), ())), preferred_element_type=F32
            )
            if diagonal is not None:
                row = lax.broadcasted_iota(jnp.int32, (half, half), 0)
                col = lax.broadcasted_iota(jnp.int32, (half, half), 1)
                cut = jnp.where(col <= row, s[:, diagonal : diagonal + half], NEGATIVE)
                s = replace_block(s, cut, diagonal, 1)
            top = jnp.max(s, axis=1, keepdims=True)
            p = jnp.exp(s - top).astype(BF)
            o = lax.dot_general(p, vv, (((1,), (0,)), ((), ())), preferred_element_type=F32)
            o_rows.append(o / pltpu.roll(o, DH, 1))
            s_rows.append(top + jnp.log(o))
        outs.append(jnp.concatenate(o_rows, axis=0))
        stats.append(jnp.concatenate(s_rows, axis=0))
    whole = jnp.where(low_lanes, outs[0], outs[1])
    o_ref[...] = whole.astype(BF)
    of_ref[...] = whole
    lse_ref[...] = jnp.where(low_lanes, stats[1], stats[0])


def split3(value):
    a = value.astype(BF)
    rest = value - a.astype(F32)
    b = rest.astype(BF)
    c = (rest - b.astype(F32)).astype(BF)
    return a, b, c


def with_stat(base, value, lane):
    a, b, c = split3(-value)
    at = lane & (DH - 1)
    base = jnp.where(at == STAT, a, base)
    base = jnp.where(at == STAT + 1, b, base)
    return jnp.where(at == STAT + 2, c, base)


def attend_back_kernel(
    causal,
    q_ref, k_ref, v_ref, ko_ref, vo_ref, qf_ref, kf_ref, kfo_ref, o_ref, lse_ref, do_ref,
    dq_ref, dk_ref, dv_ref, dko_ref, dvo_ref,
):
    size = q_ref.shape[0]
    half = size // 2
    lane = lax.broadcasted_iota(jnp.int32, (size, PAIR), 1)
    low_lanes = lane < DH
    scale = DH ** (-0.5)
    q = q_ref[...] * jnp.array(scale, BF)
    qf, kf, kfo = qf_ref[...], kf_ref[...], kfo_ref[...]
    k, v, ko, vo = k_ref[...], v_ref[...], ko_ref[...], vo_ref[...]
    do = do_ref[...]
    product = do.astype(F32) * o_ref[...]
    qstat = with_stat(qf, lse_ref[...], lane)
    kall = jnp.concatenate([k, ko], axis=0)
    zero = jnp.zeros_like(do)
    dqs, dks, dvs = [], [], []
    for head in range(2):
        mine = low_lanes if head == 0 else jnp.logical_not(low_lanes)
        inner = jnp.sum(jnp.where(mine, product, 0.0), axis=1, keepdims=True)
        dstat = with_stat(zero, jnp.broadcast_to(inner, product.shape), lane)
        qa = jnp.where(mine, q, qstat)
        da = jnp.where(mine, do, dstat)
        ka = jnp.concatenate([jnp.where(mine, k, kf), jnp.where(mine, ko, kfo)], axis=0)
        va = jnp.concatenate([jnp.where(mine, v, kf), jnp.where(mine, vo, kfo)], axis=0)
        if causal:
            pieces = [
                (0, half, [(0, half), (size, size + half)], 0),
                (half, size, [(0, 2 * size)], half),
            ]
        else:
            pieces = [(0, size, [(0, 2 * size)], None)]
        dq_rows = []
        dk_parts = [None] * 4
        dv_parts = [None] * 4
        for start, stop, spans, diagonal in pieces:
            kk = jnp.concatenate([ka[a:b] for a, b in spans], axis=0)
            vv = jnp.concatenate([va[a:b] for a, b in spans], axis=0)
            kp = jnp.concatenate([kall[a:b] for a, b in spans], axis=0)
            s = lax.dot_general(
                kk, qa[start:stop], (((1,), (1,)), ((), ())), preferred_element_type=F32
            )
            if diagonal is not None:
                row = lax.broadcasted_iota(jnp.int32, (half, half), 0)
                col = lax.broadcasted_iota(jnp.int32, (half, half), 1)
                cut = jnp.where(row <= col, s[diagonal : diagonal + half], NEGATIVE)
                s = replace_block(s, cut, diagonal, 0)
            p = jnp.exp(s)
            dp = lax.dot_general(
                vv, da[start:stop], (((1,), (1,)), ((), ())), preferred_element_type=F32
            )
            ds = (p * dp).astype(BF)
            pb = p.astype(BF)
            dv = lax.dot_general(
                pb, do[start:stop], (((1,), (0,)), ((), ())), preferred_element_type=F32
            )
            dk = lax.dot_general(
                ds, q[start:stop], (((1,), (0,)), ((), ())), preferred_element_type=F32
            )
            dq = lax.dot_general(
                ds, kp, (((0,), (0,)), ((), ())), preferred_element_type=F32
            )
            dq_rows.append(dq * scale)
            at = 0
            for a, b in spans:
                for block in range(a // half, b // half):
                    rows = slice(at, at + half)
                    dk_parts[block] = (
                        dk[rows] if dk_parts[block] is None else dk_parts[block] + dk[rows]
                    )
                    dv_parts[block] = (
                        dv[rows] if dv_parts[block] is None else dv_parts[block] + dv[rows]
                    )
                    at += half
        dqs.append(jnp.concatenate(dq_rows, axis=0))
        dks.append(jnp.concatenate(dk_parts, axis=0))
        dvs.append(jnp.concatenate(dv_parts, axis=0))
    dq_ref[...] = jnp.where(low_lanes, dqs[0], dqs[1]).astype(BF)
    dk_ref[...] = jnp.where(low_lanes, dks[0][:size], dks[1][:size])
    dv_ref[...] = jnp.where(low_lanes, dvs[0][:size], dvs[1][:size])
    dko_ref[...] = jnp.where(low_lanes, dks[0][size:], dks[1][size:]).astype(BF)
    dvo_ref[...] = jnp.where(low_lanes, dvs[0][size:], dvs[1][size:]).astype(BF)


def column(size, at):
    return pl.BlockSpec((size, PAIR), lambda p: (0, at + p))


def shared(size):
    return pl.BlockSpec((size, PAIR), lambda p: (0, 0))


def attend_forward(q, k, v, ko, vo, qf, kf, kfo, causal):
    size = q[0].shape[0]
    steps = 8 // 2
    width = steps * PAIR
    return pl.pallas_call(
        functools.partial(attend_kernel, causal),
        grid=(steps,),
        in_specs=[column(size, x[1]) for x in (q, k, v, ko, vo)] + [shared(size)] * 3,
        out_specs=[column(size, 0)] * 3,
        out_shape=[
            jax.ShapeDtypeStruct((size, width), BF),
            jax.ShapeDtypeStruct((size, width), F32),
            jax.ShapeDtypeStruct((size, width), F32),
        ],
        compiler_params=pltpu.CompilerParams(vmem_limit_bytes=48 << 20),
        cost_estimate=pl.CostEstimate(
            flops=16 * size * size * width, bytes_accessed=16 * size * width, transcendentals=0
        ),
        name="attend_forward",
    )(q[0], k[0], v[0], ko[0], vo[0], qf, kf, kfo)


def attend_backward(q, k, v, ko, vo, qf, kf, kfo, o, lse, do, causal):
    size = q[0].shape[0]
    steps = 8 // 2
    width = steps * PAIR
    return pl.pallas_call(
        functools.partial(attend_back_kernel, causal),
        grid=(steps,),
        in_specs=[column(size, x[1]) for x in (q, k, v, ko, vo)]
        + [shared(size)] * 3
        + [column(size, 0)] * 3,
        out_specs=[column(size, 0)] * 5,
        out_shape=[
            jax.ShapeDtypeStruct((size, width), BF),
            jax.ShapeDtypeStruct((size, width), F32),
            jax.ShapeDtypeStruct((size, width), F32),
            jax.ShapeDtypeStruct((size, width), BF),
            jax.ShapeDtypeStruct((size, width), BF),
        ],
        compiler_params=pltpu.CompilerParams(vmem_limit_bytes=48 << 20),
        cost_estimate=pl.CostEstimate(
            flops=40 * size * size * width, bytes_accessed=30 * size * width, transcendentals=0
        ),
        name="attend_backward",
    )(q[0], k[0], v[0], ko[0], vo[0], qf, kf, kfo, o, lse, do)


def dot(a, b):
    return lax.dot_general(a, b, (((1,), (0,)), ((), ())), preferred_element_type=F32)


def dot_back(a, b):
    return lax.dot_general(a, b, (((1,), (1,)), ((), ())), preferred_element_type=F32)


def dot_outer(a, b):
    return lax.dot_general(a, b, (((0,), (0,)), ((), ())), preferred_element_type=F32)


MESH = pl.DeviceIdType.MESH


def place():
    core = lax.axis_index("section")
    group = lax.axis_index("dp")
    depth = lax.axis_index("seq")
    return core, group, depth, ((depth + 1) // 2) % 2, depth // 2


def greet(others):
    barrier = pltpu.get_barrier_semaphore()
    for other in others:
        pl.semaphore_signal(barrier, inc=1, device_id=other, device_id_type=MESH)
    pl.semaphore_wait(barrier, len(others))


def row_mates(core, group, depth):
    mates = [(1 - core, group, depth)]
    for step in range(1, 4):
        there = (depth + step) % 4
        mates += [(core, group, there), (1 - core, group, there)]
    return mates


def remote(source, target, send, recv, device):
    return pltpu.make_async_remote_copy(
        src_ref=source,
        dst_ref=target,
        send_sem=send,
        recv_sem=recv,
        device_id=device,
        device_id_type=MESH,
    )


def spread_kernel(count, x_ref, *refs):
    weights, (x_out, *outs) = refs[:count], refs[count : 2 * count + 1]
    refs = refs[2 * count + 1 :]
    x_held, held = refs[0], refs[1 : count + 1]
    x_send, x_recv, x_own, w_send, w_recv, w_own, w_out = refs[count + 1 :]
    core, group, depth, side, at = place()
    span = x_ref.shape[1]
    loads = [pltpu.make_async_copy(weights[i], held[i], w_own.at[i]) for i in range(count)]
    for load in loads:
        load.start()
    x_load = pltpu.make_async_copy(x_ref.at[depth], x_held, x_own)
    x_load.start()
    greet(row_mates(core, group, depth))
    seat = 2 * core + at
    copies = []
    for step in (2, 1, 3, 0):
        row = (depth + step) % 4
        target = x_out.at[core, pl.ds(pl.multiple_of(at * span, span), span)]
        if step == 0:
            there = remote(
                x_held, target, x_send.at[step], x_recv.at[seat], (side, group, row)
            )
            here = pltpu.make_async_copy(x_held, target, x_recv.at[seat])
            x_load.wait()

            @pl.when(side == core)
            def _():
                here.start()

            @pl.when(side != core)
            def _():
                there.start()
        else:
            there = remote(
                x_ref.at[row], target, x_send.at[step], x_recv.at[seat], (side, group, row)
            )
            there.start()
        copies.append((step, there))
    moves = []
    for i in range(count):
        loads[i].wait()
        own = pltpu.make_async_copy(held[i], outs[i].at[core], w_out.at[i])
        gone = remote(
            held[i], outs[i].at[core], w_send.at[i], w_recv.at[i], (1 - core, group, depth)
        )
        gone.start()
        own.start()
        moves.append((own, gone))
    for own, gone in moves:
        own.wait()
        gone.wait()
    for step, there in copies:
        if step == 0:

            @pl.when(side != core)
            def _():
                there.wait_send()
        else:
            there.wait_send()
    for seat_from in range(4):
        target = x_out.at[seat_from // 2, pl.ds((seat_from % 2) * span, span)]
        pltpu.make_async_copy(x_held, target, x_recv.at[seat_from]).wait()


def spread(tokens, *weights):
    rows, span, width = tokens.shape
    count = len(weights)
    anywhere = pl.BlockSpec(memory_space=pl.ANY)
    dma = pltpu.SemaphoreType.DMA
    return pl.pallas_call(
        functools.partial(spread_kernel, count),
        in_specs=[anywhere] * (count + 1),
        out_specs=[anywhere] * (count + 1),
        out_shape=[jax.ShapeDtypeStruct((2, 2 * span, width), BF)]
        + [jax.ShapeDtypeStruct((2,) + w.shape, w.dtype) for w in weights],
        scratch_shapes=[pltpu.VMEM((span, width), BF)]
        + [pltpu.VMEM(w.shape, w.dtype) for w in weights]
        + [dma((4,)), dma((4,)), dma]
        + [dma((count,))] * 4,
        compiler_params=pltpu.CompilerParams(collective_id=0, has_side_effects=True),
        name="spread",
    )(tokens, *weights)


def gradient_groups(width, hidden):
    folds = hidden // width
    groups = []
    for layer, up, down in ((1, 0, 1), (0, 2, 3)):
        groups.append((layer, [(up, 0, hidden)]))
        groups.append((layer, [(down, i * width, width) for i in range(folds)]))
    groups.append((1, [(4, 0, width), (5, 0, 3 * width)]))
    groups.append((0, [(6, 0, width), (7, 0, 3 * width)]))
    groups.append((None, [(8, 0, width), (9, 0, width)]))
    groups.append((None, [(10, 0, 2 * width)]))
    return groups


RESULT_OF = (0, 1, 0, 1, 2, 3, 2, 3, 4, 5, 6)


def collect_kernel(groups, *refs):
    blocks = refs[:4]
    parts = refs[4:15]
    small = refs[15]
    home = refs[16:18]
    results = refs[18:25]
    small_out = refs[25]
    (
        own, got0, got1, got2, got3, got4, total, small_got,
        home_send, home_recv, own_sem, send0, recv0, send, recv, small_send, small_recv, out_sem,
    ) = refs[26:]
    core, group, depth, side, at = place()
    partner = (1 - core, group, depth)
    x_next = group + 1 - 2 * (group % 2)
    y_next = (group + 2) % 4
    first = x_next + core * (y_next - x_next)
    second = y_next + core * (x_next - y_next)
    z_next = depth + 1 - 2 * (depth % 2)
    z_far = (depth + 2) % 4
    neighbours = [
        partner,
        (core, first, depth),
        (core, second, depth),
        (core, group, z_next),
        (core, group, z_far),
    ]
    greet(row_mates(core, group, depth) + neighbours[1:3])
    bit_x, bit_y = group % 2, group // 2
    bits = [
        core,
        bit_x + core * (bit_y - bit_x),
        bit_y + core * (bit_x - bit_y),
        depth % 2,
        depth // 2,
    ]
    got = [got0, got1, got2, got3, got4]
    half = got0.shape[0]
    span = blocks[0].shape[0] // 2

    first_row = [core * half]
    count = half
    for k in range(1, 5):
        count //= 2
        first_row.append(first_row[-1] + bits[k] * count)

    starts = []
    column = 0
    for _, pieces in groups:
        starts.append(column)
        column += sum(p[2] for p in pieces)
    widths = [sum(p[2] for p in pieces) for _, pieces in groups]

    def rows(first, count):
        return pl.ds(pl.multiple_of(first, 16), count)

    def columns(g):
        return pl.ds(starts[g], widths[g])

    def step0(g):
        column = starts[g]
        copies = []
        for i, (array, row, wide) in enumerate(groups[g][1]):
            away = parts[array].at[rows(row + (1 - core) * half, half)]
            copy = remote(
                away, got0.at[:, pl.ds(column, wide)], send0.at[g, i], recv0.at[g, i], partner
            )
            copy.start()
            copies.append(copy)
            column += wide
        for copy in locals_of(g):
            copy.start()
        return copies

    def locals_of(g):
        column = starts[g]
        found = []
        for i, (array, row, wide) in enumerate(groups[g][1]):
            here = parts[array].at[rows(row + core * half, half)]
            found.append(
                pltpu.make_async_copy(here, own.at[:, pl.ds(column, wide)], own_sem.at[g, i])
            )
            column += wide
        return found

    def add(target, source, first, g):
        count = target.shape[0]
        strip = 16

        @pl.loop(0, count // strip)
        def _(i):
            r = pl.multiple_of(i * strip, strip)
            mine = source[pl.ds(pl.multiple_of(first + r, strip), strip), columns(g)]
            theirs = target[pl.ds(r, strip), columns(g)]
            target[pl.ds(r, strip), columns(g)] = (
                mine.astype(F32) + theirs.astype(F32)
            ).astype(BF)

    pending = {}

    def halving(g, k):
        count = got[k].shape[0]
        source = got[k - 1].at[rows((1 - bits[k]) * count, count), columns(g)]
        copy = remote(
            source, got[k].at[:, columns(g)], send.at[g, k], recv.at[g, k], neighbours[k]
        )
        copy.start()
        return copy

    def doubling(g, k):
        count = got[k].shape[0]
        block = total.at[rows(first_row[k], count), columns(g)]
        copy = remote(block, block, send.at[g, 4 + k], recv.at[g, 4 + k], neighbours[k])
        copy.start()
        return copy

    def joining(g):
        layer = groups[g][0]
        block = total.at[rows(core * half, half), columns(g)]
        copy = remote(block, block, send.at[g, 9], recv.at[g, 9], partner)
        if layer is None:
            copy.start()
        else:

            @pl.when(core != layer)
            def _():
                copy.start()

        return copy

    def finish_join(g, copy):
        layer, pieces = groups[g]
        if layer is None:
            copy.wait()
        else:

            @pl.when(core != layer)
            def _():
                copy.wait_send()

            @pl.when(core == layer)
            def _():
                copy.wait_recv()

    def emit(g, wait):
        layer, pieces = groups[g]
        column = starts[g]
        for i, (array, row, wide) in enumerate(pieces):
            copy = pltpu.make_async_copy(
                total.at[:, pl.ds(column, wide)],
                results[RESULT_OF[array]].at[pl.ds(row, 2 * half)],
                out_sem.at[g, i],
            )
            column += wide
            act = copy.wait if wait else copy.start
            if layer is None:
                act()
            else:

                @pl.when(core == layer)
                def _():
                    act()

    steps = 11

    def run(g, step):
        if step == 0:
            pending[g] = step0(g)
            return
        if step == 1:
            for copy in pending[g]:
                copy.wait()
            for copy in locals_of(g):
                copy.wait()
            add(got0, own, 0, g)
            pending[g] = halving(g, 1)
            return
        if step <= 5:
            pending[g].wait()
            k = step - 1
            count = got[k].shape[0]
            add(got[k], got[k - 1], bits[k] * count, g)
            if step <= 4:
                pending[g] = halving(g, step)
                return
            total[rows(first_row[4], count), columns(g)] = got4[:, columns(g)]
            pending[g] = doubling(g, 4)
            return
        if step <= 8:
            pending[g].wait()
            pending[g] = doubling(g, 9 - step)
            return
        if step == 9:
            pending[g].wait()
            pending[g] = joining(g)
            return
        finish_join(g, pending[g])
        emit(g, False)

    def home_copy(a, j):
        layer, where = j // 2, j % 2
        there = 2 * where + (core + where) % 2
        source = blocks[2 * a + layer].at[pl.ds(where * span, span)]
        target = home[a].at[depth]
        return (
            remote(
                source, target, home_send.at[a, j], home_recv.at[a, depth], (layer, group, there)
            ),
            pltpu.make_async_copy(source, target, home_recv.at[a, depth]),
            (there == depth) & (core == layer),
        )

    def home_start(a, j):
        far, near, stays = home_copy(a, j)

        @pl.when(stays)
        def _():
            near.start()

        @pl.when(jnp.logical_not(stays))
        def _():
            far.start()

    def small_step(k):
        if k > 0:
            small_copy(k - 1).wait()
            small_out[...] += small_got[k - 1]
        else:
            small_out[...] = small[...]
        if k < 5:
            small_copy(k).start()

    def small_copy(k):
        return remote(
            small_out, small_got.at[k], small_send.at[k], small_recv.at[k], neighbours[k]
        )

    number = len(groups)
    todo = [(a, j) for a in range(2) for j in range(4)]
    for slot in range(number + steps - 1):
        for g in range(number):
            if 0 <= slot - g < steps:
                run(g, slot - g)
        if todo and slot >= 1:
            home_start(*todo.pop(0))
        if slot <= 5:
            small_step(slot)
    for g in range(number):
        emit(g, True)
    for a in range(2):
        for j in range(4):
            far, near, stays = home_copy(a, j)

            @pl.when(jnp.logical_not(stays))
            def _():
                far.wait_send()

            pltpu.make_async_copy(
                blocks[0].at[pl.ds(0, span)], home[a].at[j], home_recv.at[a, j]
            ).wait()


def collect(outputs, grads, parts, small):
    size, width = outputs[0].shape
    hidden = parts[0].shape[1]
    groups = gradient_groups(width, hidden)
    wide = sum(p[2] for _, pieces in groups for p in pieces)
    number = len(groups)
    most = max(len(pieces) for _, pieces in groups)
    half = width // 2
    anywhere = pl.BlockSpec(memory_space=pl.ANY)
    resident = pl.BlockSpec(memory_space=pltpu.VMEM)
    dma = pltpu.SemaphoreType.DMA
    shapes = [parts[i].shape for i in (0, 1, 4, 5, 8, 9, 10)]
    out = pl.pallas_call(
        functools.partial(collect_kernel, groups),
        in_specs=[resident] * 4 + [anywhere] * 11 + [resident],
        out_specs=[anywhere] * 9 + [resident],
        out_shape=[jax.ShapeDtypeStruct((4, size // 2, width), BF)] * 2
        + [jax.ShapeDtypeStruct(s, BF) for s in shapes]
        + [jax.ShapeDtypeStruct(small.shape, F32)],
        scratch_shapes=[
            pltpu.VMEM((half, wide), BF),
            pltpu.VMEM((half, wide), BF),
            pltpu.VMEM((half // 2, wide), BF),
            pltpu.VMEM((half // 4, wide), BF),
            pltpu.VMEM((half // 8, wide), BF),
            pltpu.VMEM((half // 16, wide), BF),
            pltpu.VMEM((2 * half, wide), BF),
            pltpu.VMEM((5,) + small.shape, F32),
            dma((2, 4)),
            dma((2, 4)),
            dma((number, most)),
            dma((number, most)),
            dma((number, most)),
            dma((number, 10)),
            dma((number, 10)),
            dma((5,)),
            dma((5,)),
            dma((number, most)),
        ],
        compiler_params=pltpu.CompilerParams(
            collective_id=1, has_side_effects=True, vmem_limit_bytes=56 << 20
        ),
        name="collect",
    )(*outputs, *grads, *parts, small)
    return out[0], out[1], out[2:9], out[9]


def row_shards(
    inputs,
    cotangent,
    qkv_weight,
    out_weight,
    up_weight,
    down_weight,
    norm_gain,
    norm_bias,
    cross_q_weight,
    cross_kv_weight,
    cross_out_weight,
    cross_gain,
    cross_bias,
    source_segments,
    target_segments,
):
    core = lax.axis_index("section")
    depth = lax.axis_index("seq")
    span = inputs.shape[2]
    width = inputs.shape[3]
    seat = 2 * core + (depth >> 1)

    x_both, qkv_both, out_both, up_both, down_both, gain_both, bias_both = spread(
        inputs[0],
        qkv_weight[0],
        out_weight[0],
        up_weight[0],
        down_weight[0],
        norm_gain[0],
        norm_bias[0],
    )
    xs, xt = x_both[0], x_both[1]
    wqkv_e, wo_e, wu_e, wd_e, g_e, b_e = (
        w[0] for w in (qkv_both, out_both, up_both, down_both, gain_both, bias_both)
    )
    wqkv_d, wo_d, wu_d, wd_d, g_d, b_d = (
        w[1] for w in (qkv_both, out_both, up_both, down_both, gain_both, bias_both)
    )

    cots = []
    for k in range(2):
        block = lax.dynamic_index_in_dim(cotangent, seat ^ k, 0, keepdims=False)
        cots.append(swap(block, lambda c, g, z: (side_of(z), g, (2 * c + (z >> 1)) ^ k)))
    odd = (depth & 1) == 1
    cot = jnp.concatenate(
        [jnp.where(odd, cots[1], cots[0]), jnp.where(odd, cots[0], cots[1])], axis=0
    ).astype(F32)

    seg_s = lax.dynamic_index_in_dim(source_segments, depth, 0, keepdims=False).reshape(4, span)
    seg_t = lax.dynamic_index_in_dim(target_segments, depth, 0, keepdims=False).reshape(4, span)

    def in_order(seg):
        outer, inner = seg[jnp.array([0, 3])].reshape(-1), seg[jnp.array([1, 2])].reshape(-1)
        return jnp.where(core == 0, outer, inner), jnp.where(core == 0, inner, outer)

    lane = lax.broadcasted_iota(jnp.int32, (2 * span, PAIR), 1) & (DH - 1)
    late = lax.broadcasted_iota(jnp.int32, (2 * span, PAIR), 0) >= span

    def query_features(seg):
        hit = (seg[:, None] == lane) & (lane < 4)
        hit = hit | ((lane == 4) & ~late) | ((lane == 5) & late)
        return hit.astype(BF)

    def key_features(seg, barred):
        bad = ((seg[:, None] != lane) & (lane < 4)) | barred
        value = jnp.where(bad, NEGATIVE, 0.0)
        return jnp.where((lane >= STAT) & (lane < STAT + 3), 1.0, value).astype(BF)

    none = jnp.zeros(lane.shape, bool)
    seg_s0, seg_s1 = in_order(seg_s)
    seg_t0, seg_t1 = in_order(seg_t)
    qf_s, qf_t = query_features(seg_s0), query_features(seg_t0)
    kf_s0, kf_s1 = key_features(seg_s0, none), key_features(seg_s1, none)
    kf_t0 = key_features(seg_t0, (lane == 4) & late)
    kf_t1 = key_features(
        seg_t1, ((lane == 4) & (late | (core == 0))) | ((lane == 5) & late & (core == 1))
    )

    qkv_s = dot(xs, wqkv_e).astype(BF)
    kv_s1 = to_core(qkv_s[:, width:])
    qkv_t = dot(xt, wqkv_d).astype(BF)
    kv_t1 = to_core(qkv_t[:, width:])
    arg_s = ((qkv_s, 0), (qkv_s, 4), (qkv_s, 8), (kv_s1, 0), (kv_s1, 4), qf_s, kf_s0, kf_s1)
    o_s, of_s, lse_s = attend_forward(*arg_s, False)
    s1 = xs.astype(F32) + dot(o_s, wo_e)
    h_s = layer_norm(s1, g_e[0], b_e[0])
    h_s_low = h_s.astype(BF)
    u_s = dot(h_s_low, wu_e)
    gel_s = gelu_tanh(u_s).astype(BF)
    s2 = h_s + dot(gel_s, wd_e)
    memory = layer_norm(s2, g_e[1], b_e[1]).astype(BF)
    ckv = dot(memory, cross_kv_weight).astype(BF)
    ckv1 = to_core(ckv)

    arg_t = ((qkv_t, 0), (qkv_t, 4), (qkv_t, 8), (kv_t1, 0), (kv_t1, 4), qf_t, kf_t0, kf_t1)
    o_t, of_t, lse_t = attend_forward(*arg_t, True)
    t1 = xt.astype(F32) + dot(o_t, wo_d)
    h_t = layer_norm(t1, g_d[0], b_d[0])
    h_t_low = h_t.astype(BF)
    cq = dot(h_t_low, cross_q_weight).astype(BF)
    arg_c = ((cq, 0), (ckv, 0), (ckv, 4), (ckv1, 0), (ckv1, 4), qf_t, kf_s0, kf_s1)
    o_c, of_c, lse_c = attend_forward(*arg_c, False)
    t2 = h_t + dot(o_c, cross_out_weight)
    c_t = layer_norm(t2, cross_gain, cross_bias)
    c_t_low = c_t.astype(BF)
    u_t = dot(c_t_low, wu_d)
    gel_t = gelu_tanh(u_t).astype(BF)
    t3 = c_t + dot(gel_t, wd_d)
    decoded, pull_t3 = jax.vjp(layer_norm, t3, g_d[1], b_d[1])
    decoded = decoded.astype(BF)

    grad_t3, gg_d1, gb_d1 = pull_t3(cot)
    low_t3 = grad_t3.astype(BF)
    gw_down_d = dot_outer(gel_t, low_t3)
    grad_u_t = jax.vjp(gelu_tanh, u_t)[1](dot_back(low_t3, wd_d))[0].astype(BF)
    gw_up_d = dot_outer(c_t_low, grad_u_t)
    grad_c = grad_t3 + dot_back(grad_u_t, wu_d)
    grad_t2, gg_c, gb_c = jax.vjp(layer_norm, t2, cross_gain, cross_bias)[1](grad_c)
    low_t2 = grad_t2.astype(BF)
    gw_cross_out = dot_outer(o_c, low_t2)
    grad_o_c = dot_back(low_t2, cross_out_weight).astype(BF)
    grad_cq, gk, gv, gk1, gv1 = attend_backward(*arg_c, of_c, lse_c, grad_o_c, False)
    gkv1 = to_core(jnp.concatenate([gk1, gv1], axis=1))
    grad_ckv = (jnp.concatenate([gk, gv], axis=1) + gkv1.astype(F32)).astype(BF)
    gw_cross_q = dot_outer(h_t_low, grad_cq)
    grad_h = grad_t2 + dot_back(grad_cq, cross_q_weight)
    grad_t1, gg_d0, gb_d0 = jax.vjp(layer_norm, t1, g_d[0], b_d[0])[1](grad_h)
    low_t1 = grad_t1.astype(BF)
    gw_out_d = dot_outer(o_t, low_t1)
    grad_o_t = dot_back(low_t1, wo_d).astype(BF)
    gq, gk, gv, gk1, gv1 = attend_backward(*arg_t, of_t, lse_t, grad_o_t, True)
    gkv1 = to_core(jnp.concatenate([gk1, gv1], axis=1))
    grad_kv = (jnp.concatenate([gk, gv], axis=1) + gkv1.astype(F32)).astype(BF)
    grad_qkv_t = jnp.concatenate([gq, grad_kv], axis=1)
    gw_qkv_d = dot_outer(xt, grad_qkv_t)
    grad_xt = grad_t1 + dot_back(grad_qkv_t, wqkv_d)

    gw_cross_kv = dot_outer(memory, grad_ckv)
    grad_memory = dot_back(grad_ckv, cross_kv_weight).astype(BF).astype(F32)
    grad_s2, gg_e1, gb_e1 = jax.vjp(layer_norm, s2, g_e[1], b_e[1])[1](grad_memory)
    low_s2 = grad_s2.astype(BF)
    gw_down_e = dot_outer(gel_s, low_s2)
    grad_u_s = jax.vjp(gelu_tanh, u_s)[1](dot_back(low_s2, wd_e))[0].astype(BF)
    gw_up_e = dot_outer(h_s_low, grad_u_s)
    grad_h = grad_s2 + dot_back(grad_u_s, wu_e)
    grad_s1, gg_e0, gb_e0 = jax.vjp(layer_norm, s1, g_e[0], b_e[0])[1](grad_h)
    low_s1 = grad_s1.astype(BF)
    gw_out_e = dot_outer(o_s, low_s1)
    grad_o_s = dot_back(low_s1, wo_e).astype(BF)
    gq, gk, gv, gk1, gv1 = attend_backward(*arg_s, of_s, lse_s, grad_o_s, False)
    gkv1 = to_core(jnp.concatenate([gk1, gv1], axis=1))
    grad_kv = (jnp.concatenate([gk, gv], axis=1) + gkv1.astype(F32)).astype(BF)
    grad_qkv_s = jnp.concatenate([gq, grad_kv], axis=1)
    gw_qkv_e = dot_outer(xs, grad_qkv_s)
    grad_xs = grad_s1 + dot_back(grad_qkv_s, wqkv_e)

    small = jnp.stack(
        [gg_e0, gg_e1, gb_e0, gb_e1, gg_d0, gg_d1, gb_d0, gb_d1, gg_c, gb_c]
        + [jnp.zeros_like(gg_c)] * 6
    )
    parts = (
        gw_up_d, gw_down_d, gw_up_e, gw_down_e, gw_out_d, gw_qkv_d,
        gw_out_e, gw_qkv_e, gw_cross_out, gw_cross_q, gw_cross_kv,
    )
    outputs, grads, sums, small = collect(
        (memory, decoded),
        (grad_xs.astype(BF), grad_xt.astype(BF)),
        tuple(p.astype(BF) for p in parts),
        small,
    )
    g_up, g_down, g_out, g_qkv, g_cross_out, g_cross_q, g_cross_kv = (
        value.astype(F32) for value in sums
    )
    layer_small = jnp.where(core == 0, small[:4], small[4:8])
    return (
        outputs[None],
        grads.astype(F32)[None],
        g_qkv[None],
        g_out[None],
        g_up[None],
        g_down[None],
        layer_small[None, :2],
        layer_small[None, 2:],
        g_cross_q,
        g_cross_kv,
        g_cross_out,
        small[8],
        small[9],
    )


def solution(mesh):
    in_specs = (
        P("section", "dp", "seq", None),
        P("dp", "seq", None),
        P("section", None, None),
        P("section", None, None),
        P("section", None, None),
        P("section", None, None),
        P("section", None, None),
        P("section", None, None),
        P(),
        P(),
        P(),
        P(),
        P(),
        P("dp", None),
        P("dp", None),
    )
    out_specs = (
        P("section", "dp", "seq", None),
        P("section", "dp", "seq", None),
        P("section", None, None),
        P("section", None, None),
        P("section", None, None),
        P("section", None, None),
        P("section", None, None),
        P("section", None, None),
        P(),
        P(),
        P(),
        P(),
        P(),
    )
    whole_rows = mesh.shape["section"] == 2 and mesh.shape["seq"] == 4 and mesh.shape["dp"] == 4
    body = row_shards if whole_rows else shards
    return jax.shard_map(body, mesh=mesh, in_specs=in_specs, out_specs=out_specs, check_vma=False)
```

```python
import functools

import jax
import jax.numpy as jnp
from jax import lax
from jax.experimental import pallas as pl
from jax.experimental.pallas import tpu as pltpu
from jax.sharding import PartitionSpec as P

DH = 64
MICRO = 2
MB_ROWS = 2


EPSILON = 1e-05
NEGATIVE = -1e30


def from_behind(value, axis, steps):
    count = lax.axis_size(axis)
    leading, last = (max(0, -steps), min(count, count - steps))
    return lax.ppermute(value, axis, [(source, source + steps) for source in range(leading, last)])


def layer_norm(vector, gain_row, bias_row):
    centre = vector - jnp.mean(vector, axis=-1, keepdims=True)
    spread = jnp.mean(centre * centre, axis=-1, keepdims=True)
    return centre * lax.rsqrt(spread + EPSILON) * gain_row + bias_row


def gelu_tanh(vector):
    return jax.nn.gelu(vector, approximate=True)


def heads_view(vector):
    return vector.reshape(vector.shape[:-1] + (vector.shape[-1] // DH, DH))


def joined_view(vector):
    return vector.reshape(vector.shape[:-2] + (vector.shape[-2] * vector.shape[-1],))


def dense_rows(left_side, right_side):
    return jnp.einsum("rsd,de->rse", left_side, right_side, preferred_element_type=jnp.float32)


def dense_back(left_side, right_side):
    return jnp.einsum("rse,de->rsd", left_side, right_side, preferred_element_type=jnp.float32)


def outer_sum(left_side, right_side):
    return jnp.einsum("rsd,rse->de", left_side, right_side, preferred_element_type=jnp.float32)


def build_mask(query_ids, key_ids, query_places, key_places, causal):
    same_doc = query_ids[:, :, None] == key_ids[:, None, :]
    ordered = (key_places[None, :] <= query_places[:, None]) | jnp.logical_not(causal)
    return same_doc & ordered[None]


def soft_forward(queries, key_rows, value_rows, allowed):
    score_scale = DH ** (-0.5)
    scores = (
        jnp.einsum(
            "rqhe,rkhe->rhqk",
            heads_view(queries),
            heads_view(key_rows),
            preferred_element_type=jnp.float32,
        )
        * score_scale
    )
    scores = jnp.where(allowed[:, None], scores, NEGATIVE)
    highest = jnp.max(scores, axis=-1, keepdims=True)
    exp_terms = jnp.exp(scores - highest)
    totals = jnp.sum(exp_terms, axis=-1, keepdims=True)
    weights = exp_terms / totals
    log_total = (highest + jnp.log(totals))[..., 0]
    mixed_out = jnp.einsum(
        "rhqk,rkhe->rqhe",
        weights.astype(jnp.bfloat16),
        heads_view(value_rows),
        preferred_element_type=jnp.float32,
    )
    return (joined_view(mixed_out), weights, log_total)


def score_grads(grad_mixed, value_rows, weights):
    grad_weights = jnp.einsum(
        "rqhe,rkhe->rhqk",
        heads_view(grad_mixed),
        heads_view(value_rows),
        preferred_element_type=jnp.float32,
    )
    inner_sum = jnp.sum(grad_weights * weights, axis=-1, keepdims=True)
    grad_scores = (weights * (grad_weights - inner_sum)).astype(jnp.bfloat16)
    return (grad_scores, inner_sum[..., 0])


def attend_keys(queries, key_rows, value_rows, query_ids, key_ids, causal):
    span_len = key_rows.shape[1]
    offset = lax.axis_index("seq") * span_len
    whole_keys, whole_values = (
        lax.all_gather(key_rows, "seq", axis=1, tiled=True),
        lax.all_gather(value_rows, "seq", axis=1, tiled=True),
    )
    own_positions = offset + jnp.arange(span_len)
    all_positions = jnp.arange(whole_keys.shape[1])
    own_ids = lax.dynamic_slice_in_dim(query_ids, offset, span_len, 1)
    allowed = build_mask(own_ids, key_ids, own_positions, all_positions, causal)
    mixed_out, weights, log_total = soft_forward(queries, whole_keys, whole_values, allowed)
    kept_state = (
        queries,
        key_rows,
        value_rows,
        whole_keys,
        whole_values,
        weights,
        log_total,
        query_ids,
        key_ids,
        causal,
    )
    return (mixed_out, kept_state)


def attend_back(kept_state, grad_mixed):
    (
        queries,
        key_rows,
        value_rows,
        whole_keys,
        whole_values,
        weights,
        log_total,
        query_ids,
        key_ids,
        causal,
    ) = kept_state
    score_scale = DH ** (-0.5)
    grad_scores, inner_sum = score_grads(grad_mixed, whole_values, weights)
    grad_queries = (
        jnp.einsum(
            "rhqk,rkhe->rqhe",
            grad_scores,
            heads_view(whole_keys),
            preferred_element_type=jnp.float32,
        )
        * score_scale
    )
    part_keys = (
        jnp.einsum(
            "rhqk,rqhe->rkhe", grad_scores, heads_view(queries), preferred_element_type=jnp.float32
        )
        * score_scale
    )
    part_values = jnp.einsum(
        "rhqk,rqhe->rkhe",
        weights.astype(jnp.bfloat16),
        heads_view(grad_mixed),
        preferred_element_type=jnp.float32,
    )
    grad_keys, grad_values = (
        lax.psum_scatter(
            joined_view(part_keys).astype(jnp.bfloat16), "seq", scatter_dimension=1, tiled=True
        ).astype(jnp.float32),
        lax.psum_scatter(
            joined_view(part_values).astype(jnp.bfloat16), "seq", scatter_dimension=1, tiled=True
        ).astype(jnp.float32),
    )
    return (joined_view(grad_queries), grad_keys, grad_values)


def layer_forward(tokens, memory_in, own_ids, source_ids, target_ids, params, decoder):
    (
        qkv_matrix,
        out_matrix,
        up_matrix,
        down_matrix,
        norm_gains,
        norm_biases,
        query_matrix,
        pair_matrix,
        cross_matrix,
        cross_gains,
        cross_shift,
    ) = params
    residual = tokens.astype(jnp.float32)
    packed = dense_rows(tokens, qkv_matrix).astype(jnp.bfloat16)
    queries, key_rows, value_rows = jnp.split(packed, 3, axis=-1)
    mixed_out, self_state = attend_keys(queries, key_rows, value_rows, own_ids, own_ids, decoder)
    mixed_low = mixed_out.astype(jnp.bfloat16)
    first_sum = residual + dense_rows(mixed_low, out_matrix)
    first_norm = layer_norm(first_sum, norm_gains[0], norm_biases[0])
    first_low = first_norm.astype(jnp.bfloat16)
    cross_query = dense_rows(first_low, query_matrix).astype(jnp.bfloat16)
    cross_pair = dense_rows(memory_in, pair_matrix).astype(jnp.bfloat16)
    cross_keys, cross_values = jnp.split(cross_pair, 2, axis=-1)
    cross_mixed, cross_state = attend_keys(
        cross_query, cross_keys, cross_values, target_ids, source_ids, False
    )
    cross_low = cross_mixed.astype(jnp.bfloat16)
    cross_sum = first_norm + dense_rows(cross_low, cross_matrix)
    second = jnp.where(decoder, layer_norm(cross_sum, cross_gains, cross_shift), first_norm)
    second_low = second.astype(jnp.bfloat16)
    upward = dense_rows(second_low, up_matrix)
    gated_low = gelu_tanh(upward).astype(jnp.bfloat16)
    last_sum = second + dense_rows(gated_low, down_matrix)
    output = layer_norm(last_sum, norm_gains[1], norm_biases[1])
    kept_state = (
        tokens,
        self_state,
        mixed_low,
        first_sum,
        first_low,
        cross_state,
        cross_low,
        cross_sum,
        second_low,
        upward,
        gated_low,
        last_sum,
    )
    return (output, kept_state)


def layer_backward(kept_state, grad_out, params, decoder):
    (
        qkv_matrix,
        out_matrix,
        up_matrix,
        down_matrix,
        norm_gains,
        norm_biases,
        query_matrix,
        pair_matrix,
        cross_matrix,
        cross_gains,
        cross_shift,
    ) = params
    (
        tokens,
        self_state,
        mixed_low,
        first_sum,
        first_low,
        cross_state,
        cross_low,
        cross_sum,
        second_low,
        upward,
        gated_low,
        last_sum,
    ) = kept_state
    unused, pull_last = jax.vjp(layer_norm, last_sum, norm_gains[1], norm_biases[1])
    grad_last, grad_gain_last, grad_bias_last = pull_last(grad_out)
    down_in = grad_last.astype(jnp.bfloat16)
    grad_down = outer_sum(gated_low, down_in)
    grad_gated = dense_back(down_in, down_matrix)
    unused, pull_gelu = jax.vjp(gelu_tanh, upward)
    up_in = pull_gelu(grad_gated)[0].astype(jnp.bfloat16)
    grad_up = outer_sum(second_low, up_in)
    grad_second = grad_last + dense_back(up_in, up_matrix)
    unused, pull_cross = jax.vjp(layer_norm, cross_sum, cross_gains, cross_shift)
    grad_cross_sum, grad_cross_gain, grad_cross_bias = pull_cross(
        jnp.where(decoder, grad_second, 0.0)
    )
    grad_first = jnp.where(decoder, grad_cross_sum, grad_second)
    cross_in = grad_cross_sum.astype(jnp.bfloat16)
    grad_cross_out = outer_sum(cross_low, cross_in)
    grad_cross_mixed = dense_back(cross_in, cross_matrix).astype(jnp.bfloat16)
    grad_cross_query, grad_cross_keys, grad_cross_values = attend_back(
        cross_state, grad_cross_mixed
    )
    query_in = grad_cross_query.astype(jnp.bfloat16)
    grad_query_matrix = outer_sum(first_low, query_in)
    grad_first = grad_first + dense_back(query_in, query_matrix)
    pair_in = jnp.concatenate([grad_cross_keys, grad_cross_values], axis=-1).astype(jnp.bfloat16)
    unused, pull_first = jax.vjp(layer_norm, first_sum, norm_gains[0], norm_biases[0])
    grad_first_sum, grad_gain_first, grad_bias_first = pull_first(grad_first)
    out_in = grad_first_sum.astype(jnp.bfloat16)
    grad_out_matrix = outer_sum(mixed_low, out_in)
    grad_mixed = dense_back(out_in, out_matrix).astype(jnp.bfloat16)
    grad_queries, grad_keys, grad_values = attend_back(self_state, grad_mixed)
    qkv_in = jnp.concatenate([grad_queries, grad_keys, grad_values], axis=-1).astype(jnp.bfloat16)
    grad_qkv_matrix = outer_sum(tokens, qkv_in)
    grad_tokens = grad_first_sum + dense_back(qkv_in, qkv_matrix)
    grad_set = (
        grad_qkv_matrix,
        grad_out_matrix,
        grad_up,
        grad_down,
        jnp.stack([grad_gain_first, grad_gain_last]),
        jnp.stack([grad_bias_first, grad_bias_last]),
        grad_query_matrix,
        jnp.zeros(pair_matrix.shape, jnp.float32),
        grad_cross_out,
        grad_cross_gain,
        grad_cross_bias,
    )
    return (grad_tokens, pair_in, grad_set)


def shards(
    inputs,
    cotangent,
    qkv_weight,
    out_weight,
    up_weight,
    down_weight,
    norm_gain,
    norm_bias,
    cross_q_weight,
    cross_kv_weight,
    cross_out_weight,
    cross_gain,
    cross_bias,
    source_segments,
    target_segments,
):
    section_index = lax.axis_index("section")
    decoder = section_index == 1
    params = (
        qkv_weight[0],
        out_weight[0],
        up_weight[0],
        down_weight[0],
        norm_gain[0],
        norm_bias[0],
        cross_q_weight,
        cross_kv_weight,
        cross_out_weight,
        cross_gain,
        cross_bias,
    )
    tokens_all = inputs[0]
    own_all = jnp.where(decoder, target_segments, source_segments)
    span_len = tokens_all.shape[1]
    features = tokens_all.shape[2]
    memory_in = jnp.zeros((MB_ROWS, span_len, features), jnp.bfloat16)
    outputs_all = jnp.zeros(tokens_all.shape, jnp.bfloat16)
    caches = []
    sent_rows = []
    for forward_tick in range(MICRO + 1):
        micro_index = forward_tick - section_index
        active = (micro_index >= 0) & (micro_index < MICRO)
        first_row = jnp.clip(micro_index, 0, MICRO - 1) * MB_ROWS
        rows_now = lax.dynamic_slice_in_dim(tokens_all, first_row, MB_ROWS, 0)
        own_now = lax.dynamic_slice_in_dim(own_all, first_row, MB_ROWS, 0)
        source_now = lax.dynamic_slice_in_dim(source_segments, first_row, MB_ROWS, 0)
        target_now = lax.dynamic_slice_in_dim(target_segments, first_row, MB_ROWS, 0)
        output, kept_state = layer_forward(
            rows_now, memory_in, own_now, source_now, target_now, params, decoder
        )
        output_low = output.astype(jnp.bfloat16)
        current = lax.dynamic_slice_in_dim(outputs_all, first_row, MB_ROWS, 0)
        outputs_all = lax.dynamic_update_slice_in_dim(
            outputs_all, jnp.where(active, output_low, current), first_row, 0
        )
        caches.append(kept_state)
        sent_rows.append(output_low)
        if forward_tick < MICRO:
            memory_in = from_behind(output_low, "section", 1)
    grad_pair_in = jnp.zeros((MB_ROWS, span_len, 2 * features), jnp.bfloat16)
    totals = tuple((jnp.zeros(param_item.shape, jnp.float32) for param_item in params))
    input_all = jnp.zeros(tokens_all.shape, jnp.float32)
    for backward_tick in range(MICRO + 1):
        forward_tick = MICRO - backward_tick
        micro_index = forward_tick - section_index
        active = (micro_index >= 0) & (micro_index < MICRO)
        first_row = jnp.clip(micro_index, 0, MICRO - 1) * MB_ROWS
        cot_now = lax.dynamic_slice_in_dim(cotangent, first_row, MB_ROWS, 0).astype(jnp.float32)
        memory_grad = lax.optimization_barrier(
            dense_back(grad_pair_in, params[7]).astype(jnp.bfloat16)
        ).astype(jnp.float32)
        pair_term = outer_sum(sent_rows[forward_tick], grad_pair_in)
        grad_out = jnp.where(decoder, cot_now, memory_grad)
        grad_tokens, pair_in, grad_set = layer_backward(
            caches[forward_tick], grad_out, params, decoder
        )
        grad_set = grad_set[:7] + (jnp.where(decoder, 0.0, pair_term),) + grad_set[8:]
        totals = jax.tree.map(
            lambda total_sum, new_term: total_sum + jnp.where(active, new_term, 0.0),
            totals,
            grad_set,
        )
        current = lax.dynamic_slice_in_dim(input_all, first_row, MB_ROWS, 0)
        input_all = lax.dynamic_update_slice_in_dim(
            input_all, jnp.where(active, grad_tokens, current), first_row, 0
        )
        if backward_tick < MICRO:
            grad_pair_in = from_behind(pair_in, "section", -1)
    layer_part = lax.psum(
        (totals[0], totals[1], totals[2], totals[3], totals[4], totals[5]), ("dp", "seq")
    )
    cross_part = lax.psum(
        (totals[6], totals[7], totals[8], totals[9], totals[10]), ("section", "dp", "seq")
    )
    return (
        outputs_all[None],
        input_all[None],
        layer_part[0][None],
        layer_part[1][None],
        layer_part[2][None],
        layer_part[3][None],
        layer_part[4][None],
        layer_part[5][None],
        cross_part[0],
        cross_part[1],
        cross_part[2],
        cross_part[3],
        cross_part[4],
    )


BF = jnp.bfloat16
F32 = jnp.float32
AXES = ("section", "dp", "seq")
PAIR = 2 * DH
STAT = 8
Q_ROWS = 256
K_ROWS = 256
AHEAD = 2


def swap(value, move):
    pairs = []
    for core in range(2):
        for group in range(4):
            for depth in range(4):
                to = move(core, group, depth)
                if to is not None:
                    pairs.append(
                        ((core * 4 + group) * 4 + depth, (to[0] * 4 + to[1]) * 4 + to[2])
                    )
    return lax.ppermute(value, AXES, pairs)


def to_core(value):
    return swap(value, lambda core, group, depth: (1 - core, group, depth))


def replace_block(whole, block, at, axis):
    size, count = block.shape[axis], whole.shape[axis]
    parts = [lax.slice_in_dim(whole, 0, at, axis=axis)] if at > 0 else []
    parts.append(block)
    if at + size < count:
        parts.append(lax.slice_in_dim(whole, at + size, count, axis=axis))
    return jnp.concatenate(parts, axis=axis)


def attend_pair(causal, q, k, v, ko, vo, qf, kf):
    size = q.shape[0]
    half = size // 2
    lane = lax.broadcasted_iota(jnp.int32, (size, PAIR), 1)
    low_lanes = lane < DH
    q = q * jnp.array(DH ** (-0.5), BF)
    kf, kfo = kf[:size], kf[size:]
    one = jnp.ones_like(v)
    tasks = []
    for head in range(2):
        mine = low_lanes if head == 0 else jnp.logical_not(low_lanes)
        qa = jnp.where(mine, q, qf)
        ka = [jnp.where(mine, k, kf), jnp.where(mine, ko, kfo)]
        va = [jnp.where(mine, v, one), jnp.where(mine, vo, one)]
        for start in range(0, size, Q_ROWS):
            rows = slice(start, start + Q_ROWS)
            if causal and start < half:
                kk = jnp.concatenate([ka[0][:half], ka[1][:half]], axis=0)
                vv = jnp.concatenate([va[0][:half], va[1][:half]], axis=0)
                diagonal = 0
            else:
                kk = jnp.concatenate(ka, axis=0)
                vv = jnp.concatenate(va, axis=0)
                diagonal = half if causal else None
            tasks.append((qa[rows], kk, vv, diagonal, start % half))

    def scores(task):
        qq, kk, _, _, _ = task
        return lax.dot_general(qq, kk, (((1,), (1,)), ((), ())), preferred_element_type=F32)

    def finish(task, s):
        _, _, vv, diagonal, first = task
        if diagonal is not None:
            row = lax.broadcasted_iota(jnp.int32, (Q_ROWS, half), 0) + first
            col = lax.broadcasted_iota(jnp.int32, (Q_ROWS, half), 1)
            cut = jnp.where(col <= row, s[:, diagonal : diagonal + half], NEGATIVE)
            s = replace_block(s, cut, diagonal, 1)
        top = jnp.max(s, axis=1, keepdims=True)
        p = jnp.exp(s - top).astype(BF)
        o = lax.dot_general(p, vv, (((1,), (0,)), ((), ())), preferred_element_type=F32)
        return o / pltpu.roll(o, DH, 1), top + jnp.log(o)

    done = []
    ahead = [scores(t) for t in tasks[:AHEAD]]
    for i, task in enumerate(tasks):
        if i + AHEAD < len(tasks):
            ahead.append(scores(tasks[i + AHEAD]))
        done.append(finish(task, ahead[i]))
    count = size // Q_ROWS
    outs = [jnp.concatenate([d[0] for d in done[h * count :][:count]], axis=0) for h in range(2)]
    stats = [jnp.concatenate([d[1] for d in done[h * count :][:count]], axis=0) for h in range(2)]
    return jnp.where(low_lanes, outs[0], outs[1]), jnp.where(low_lanes, stats[1], stats[0])


def split3(value):
    a = value.astype(BF)
    rest = value - a.astype(F32)
    b = rest.astype(BF)
    c = (rest - b.astype(F32)).astype(BF)
    return a, b, c


def with_stat(base, value, lane):
    a, b, c = split3(-value)
    at = lane & (DH - 1)
    base = jnp.where(at == STAT, a, base)
    base = jnp.where(at == STAT + 1, b, base)
    return jnp.where(at == STAT + 2, c, base)


def attend_back_head(causal, head, q, k, v, ko, vo, qf, kf, o, lse, do):
    size = q.shape[0]
    half = size // 2
    lane = lax.broadcasted_iota(jnp.int32, (size, PAIR), 1)
    mine = (lane >= head * DH) & (lane < head * DH + DH)
    scale = DH ** (-0.5)
    q = q * jnp.array(scale, BF)
    kf, kfo = kf[:size], kf[size:]
    inner = jnp.sum(jnp.where(mine, do.astype(F32) * o, 0.0), axis=1, keepdims=True)
    dstat = with_stat(jnp.zeros_like(do), jnp.broadcast_to(inner, o.shape), lane)
    qa = jnp.where(mine, q, with_stat(qf, lse, lane))
    da = jnp.where(mine, do, dstat)
    tasks = []
    for own, keys, values, marks in ((True, k, v, kf), (False, ko, vo, kfo)):
        ka = jnp.where(mine, keys, marks)
        va = jnp.where(mine, values, marks)
        for start in range(0, size, K_ROWS):
            rows = slice(start, start + K_ROWS)
            late = causal and start >= half
            first = half if late else 0
            diagonal = (start % half) if causal and own else None
            tasks.append((ka[rows], va[rows], keys[rows], qa[first:], da[first:], first, diagonal))

    def scores(task):
        ka, va, _, qa, da, _, _ = task
        s = lax.dot_general(ka, qa, (((1,), (1,)), ((), ())), preferred_element_type=F32)
        dp = lax.dot_general(va, da, (((1,), (1,)), ((), ())), preferred_element_type=F32)
        return s, dp

    def finish(task, both):
        _, _, keys, _, _, first, diagonal = task
        s, dp = both
        if diagonal is not None:
            row = lax.broadcasted_iota(jnp.int32, (K_ROWS, half), 0) + diagonal
            col = lax.broadcasted_iota(jnp.int32, (K_ROWS, half), 1)
            cut = jnp.where(row <= col, s[:, :half], NEGATIVE)
            s = replace_block(s, cut, 0, 1)
        p = jnp.exp(s)
        ds = (p * dp).astype(BF)
        pb = p.astype(BF)
        dv = lax.dot_general(
            pb, do[first:], (((1,), (0,)), ((), ())), preferred_element_type=F32
        )
        dk = lax.dot_general(ds, q[first:], (((1,), (0,)), ((), ())), preferred_element_type=F32)
        dq = lax.dot_general(keys, ds, (((0,), (0,)), ((), ())), preferred_element_type=F32)
        return dk, dv, dq

    done = []
    ahead = [scores(t) for t in tasks[:AHEAD]]
    for i, task in enumerate(tasks):
        if i + AHEAD < len(tasks):
            ahead.append(scores(tasks[i + AHEAD]))
        done.append(finish(task, ahead[i]))
    dk = jnp.concatenate([d[0] for d in done], axis=0)
    dv = jnp.concatenate([d[1] for d in done], axis=0)
    full = sum(d[2] for d, task in zip(done, tasks) if task[5] == 0)
    late = [d[2] for d, task in zip(done, tasks) if task[5] > 0]
    if late:
        full = jnp.concatenate([full[:, :half], full[:, half:] + sum(late)], axis=1)
    return mine, full.T * scale, dk[:size], dv[:size], dk[size:], dv[size:]


MESH = pl.DeviceIdType.MESH


def place():
    core = lax.axis_index("section")
    group = lax.axis_index("dp")
    depth = lax.axis_index("seq")
    return core, group, depth, ((depth + 1) // 2) % 2, depth // 2


def greet(others):
    barrier = pltpu.get_barrier_semaphore()
    for other in others:
        pl.semaphore_signal(barrier, inc=1, device_id=other, device_id_type=MESH)
    pl.semaphore_wait(barrier, len(others))


def row_mates(core, group, depth):
    mates = [(1 - core, group, depth)]
    for step in range(1, 4):
        there = (depth + step) % 4
        mates += [(core, group, there), (1 - core, group, there)]
    return mates


def remote(source, target, send, recv, device):
    return pltpu.make_async_remote_copy(
        src_ref=source,
        dst_ref=target,
        send_sem=send,
        recv_sem=recv,
        device_id=device,
        device_id_type=MESH,
    )


def write_features(seg_ref, target_ref, queries, order, layer, core, depth):
    span = seg_ref.shape[2] // 4
    at = lax.broadcasted_iota(jnp.int32, (PAIR, span), 0)
    at = jnp.where(at >= DH, at - DH, at)
    own_core = core
    for i in range(2 if queries else 4):
        first = pl.multiple_of(order[i] * span, span)
        seg = seg_ref[layer, pl.ds(depth, 1), pl.ds(first, span)]
        seg = jnp.broadcast_to(seg, (PAIR, span))
        if queries:
            value = jnp.where((seg == at) | (at == 4 + i), 1.0, 0.0)
        else:
            bad = (seg != at) & (at < 4)
            value = jnp.where(bad, NEGATIVE, 0.0)
            if layer == 1:
                barred = [0.0, NEGATIVE, NEGATIVE * (1 - own_core).astype(F32), NEGATIVE][i]
                value = jnp.where(at == 4, barred, value)
                if i == 3:
                    value = jnp.where(at == 5, NEGATIVE * own_core.astype(F32), value)
            value = jnp.where((at >= STAT) & (at < STAT + 3), 1.0, value)
        target_ref[layer, i * span : (i + 1) * span, :] = value.T.astype(BF)


def spread_kernel(count, x_ref, seg_ref, *refs):
    weights, (x_out, *outs) = refs[:count], refs[count : 2 * count + 1]
    features = refs[2 * count + 1 : 2 * count + 3]
    refs = refs[2 * count + 3 :]
    x_held, held = refs[0], refs[1 : count + 1]
    x_send, x_recv, x_own, w_send, w_recv, w_own, w_out = refs[count + 1 :]
    core, group, depth, side, at = place()
    span = x_ref.shape[1]
    loads = [pltpu.make_async_copy(weights[i], held[i], w_own.at[i]) for i in range(count)]
    for load in loads:
        load.start()
    x_load = pltpu.make_async_copy(x_ref.at[depth], x_held, x_own)
    x_load.start()
    greet(row_mates(core, group, depth))
    seat = 2 * core + at
    copies = []
    for step in (2, 1, 3, 0):
        row = (depth + step) % 4
        target = x_out.at[core, pl.ds(pl.multiple_of(at * span, span), span)]
        if step == 0:
            there = remote(
                x_held, target, x_send.at[step], x_recv.at[seat], (side, group, row)
            )
            here = pltpu.make_async_copy(x_held, target, x_recv.at[seat])
            x_load.wait()

            @pl.when(side == core)
            def _():
                here.start()

            @pl.when(side != core)
            def _():
                there.start()
        else:
            there = remote(
                x_ref.at[row], target, x_send.at[step], x_recv.at[seat], (side, group, row)
            )
            there.start()
        copies.append((step, there))
    moves = []
    for i in range(count):
        loads[i].wait()
        own = pltpu.make_async_copy(held[i], outs[i].at[core], w_out.at[i])
        gone = remote(
            held[i], outs[i].at[core], w_send.at[i], w_recv.at[i], (1 - core, group, depth)
        )
        gone.start()
        own.start()
        moves.append((own, gone))
    order = [core, 3 - core, 1 - core, 2 + core]
    for layer in range(2):
        write_features(seg_ref, features[0], True, order, layer, core, depth)
        write_features(seg_ref, features[1], False, order, layer, core, depth)
    for own, gone in moves:
        own.wait()
        gone.wait()
    for step, there in copies:
        if step == 0:

            @pl.when(side != core)
            def _():
                there.wait_send()
        else:
            there.wait_send()
    for seat_from in range(4):
        target = x_out.at[seat_from // 2, pl.ds((seat_from % 2) * span, span)]
        pltpu.make_async_copy(x_held, target, x_recv.at[seat_from]).wait()


def spread(tokens, segments, *weights):
    rows, span, width = tokens.shape
    count = len(weights)
    anywhere = pl.BlockSpec(memory_space=pl.ANY)
    resident = pl.BlockSpec(memory_space=pltpu.VMEM)
    dma = pltpu.SemaphoreType.DMA
    out = pl.pallas_call(
        functools.partial(spread_kernel, count),
        in_specs=[anywhere, resident] + [anywhere] * count,
        out_specs=[anywhere] * (count + 1) + [resident] * 2,
        out_shape=[jax.ShapeDtypeStruct((2, 2 * span, width), BF)]
        + [jax.ShapeDtypeStruct((2,) + w.shape, w.dtype) for w in weights]
        + [jax.ShapeDtypeStruct((2, n * span, PAIR), BF) for n in (2, 4)],
        scratch_shapes=[pltpu.VMEM((span, width), BF)]
        + [pltpu.VMEM(w.shape, w.dtype) for w in weights]
        + [dma((4,)), dma((4,)), dma]
        + [dma((count,))] * 4,
        compiler_params=pltpu.CompilerParams(collective_id=0, has_side_effects=True),
        name="spread",
    )(tokens, segments, *weights)
    return out[: count + 1], out[count + 1 :]


class RowRider:
    def __init__(self, rows):
        self.array = rows
        self.shape = (2 * rows.shape[1], rows.shape[2])

    def copies(self, source, target, send, recv):
        core, group, depth, side, at = place()
        span = source.shape[1]
        slot = target.at[pl.ds(pl.multiple_of(at * span, span), span)]
        for i in range(2):
            row = 2 * core + i
            yield (
                remote(source.at[row], slot, send.at[i], recv.at[at], (side, group, row)),
                pltpu.make_async_copy(source.at[row], slot, recv.at[at]),
                (row == depth) & (side == core),
            )

    def arrivals(self, source, target, recv):
        span = source.shape[1]
        for i in range(2):
            slot = target.at[pl.ds(i * span, span)]
            yield pltpu.make_async_copy(source.at[0], slot, recv.at[i])

    def receives(self):
        return None


class HomeRider:
    def __init__(self, result, layer):
        self.array = result
        self.layer = layer
        self.shape = (4, result.shape[0] // 2, result.shape[1])

    def copies(self, source, target, send, recv):
        core, group, depth, side, at = place()
        span = source.shape[0] // 2
        slot = target.at[depth]
        for i in range(2):
            there = 2 * i + (core + i) % 2
            block = source.at[pl.ds(i * span, span)]
            yield (
                remote(block, slot, send.at[i], recv.at[depth], (self.layer, group, there)),
                pltpu.make_async_copy(block, slot, recv.at[depth]),
                (there == depth) & (core == self.layer),
            )

    def arrivals(self, source, target, recv):
        span = source.shape[0] // 2
        for i in range(4):
            yield pltpu.make_async_copy(source.at[pl.ds(0, span)], target.at[i], recv.at[i])

    def receives(self):
        return lax.axis_index("section") == self.layer


def ride_copies(rider, source, target, send, recv):
    for far, near, stays in rider.copies(source, target, send, recv):

        @pl.when(stays)
        def _():
            near.start()

        @pl.when(jnp.logical_not(stays))
        def _():
            far.start()


def ride_end(rider, source, target, send, recv):
    for far, near, stays in rider.copies(source, target, send, recv):

        @pl.when(jnp.logical_not(stays))
        def _():
            far.wait_send()

    def arrive():
        for copy in rider.arrivals(source, target, recv):
            copy.wait()

    if rider.receives() is None:
        arrive()
    else:
        pl.when(rider.receives())(arrive)


RESULT_OF = (0, 1, 0, 1, 2, 3, 2, 3, 4, 5, 6)
Z_FIRST = ()
LAG = 2
HOME_SLOT = 1
LATE = {0: 0, 3: 0, 1: 2, 2: 4}


def gradient_groups(width, hidden):
    folds = hidden // width
    groups = []
    for layer, up, down in ((1, 0, 1), (0, 2, 3)):
        groups.append((layer, [(up, 0, 0, hidden)]))
        groups.append((layer, [(down, i * width, 0, width) for i in range(folds)]))
    groups.append((None, [(8, 0, 0, width), (9, 0, 0, width), (10, 0, 0, 2 * width)]))
    for layer, o, q in ((1, 4, 5), (0, 6, 7)):
        groups.append((layer, [(o, 0, 0, width), (q, 0, 0, 3 * width)]))
    return groups


FAMILIES = ((0, 1), (2, 3), (4,), (5, 6))
CROSS_TABLE = {0: [(0, 0), (1, 0)], 1: [(0, 1), (1, 1)]}
SELF_TABLE = {
    0: [(0, 2), (1, 2), (2, 0), (3, 0)],
    2: [(0, 3), (1, 3), (2, 1), (3, 1)],
    5: [(0, 4), (1, 4)],
}


def wide(groups, chosen):
    return sum(p[3] for g in chosen for p in groups[g][1])


class Plan:
    def __init__(self, width, hidden, spans):
        self.groups = gradient_groups(width, hidden)
        self.half = width // 2
        self.spans = spans
        self.chosen = [g for f in sorted(spans) for g in FAMILIES[f]]
        self.enter = {g: spans[f][0] for f in spans for g in FAMILIES[f]}
        self.leave = {g: spans[f][1] for f in spans for g in FAMILIES[f]}
        self.final = [g for g in self.chosen if self.leave[g] == 10]
        self.arrays = sorted(
            {p[0] for g in self.chosen if self.enter[g] == 0 for p in self.groups[g][1]}
        )
        self.most = max(len(pieces) for _, pieces in self.groups)

    def columns(self, g, k):
        mates = self.level(k)
        return pl.ds(wide(self.groups, mates[: mates.index(g)]), wide(self.groups, [g]))

    def level(self, k):
        return [g for g in self.chosen if self.enter[g] <= k < min(self.leave[g], 5)]

    def family_columns(self, f, g):
        mates = FAMILIES[f]
        return pl.ds(wide(self.groups, mates[: mates.index(g)]), wide(self.groups, [g]))

    def rows(self, k):
        return self.half >> k

    def states_in(self):
        return [f for f in sorted(self.spans) if self.spans[f][0] > 0]

    def states_out(self):
        return [f for f in sorted(self.spans) if self.spans[f][1] < 10]

    def state_shape(self, f, stage):
        return jax.ShapeDtypeStruct((self.rows(stage - 1), wide(self.groups, FAMILIES[f])), BF)

    def scratch(self):
        dma = pltpu.SemaphoreType.DMA
        number = len(self.chosen)
        shapes = []
        first = self.level(0)
        shapes.append(
            pltpu.VMEM((2 * self.half, wide(self.groups, first)) if first else (16, 128), BF)
        )
        for k in range(5):
            columns = wide(self.groups, self.level(k))
            shapes.append(pltpu.VMEM((self.rows(k), columns or 128), BF))
        total = wide(self.groups, self.final)
        shapes.append(pltpu.VMEM((2 * self.half if total else 16, total or 128), BF))
        shapes += [dma((number, self.most))] * 2 + [dma((number, 1))] * 2 + [dma((number, 10))] * 2
        return shapes

    def count(self):
        return 13


class Reducer:
    def __init__(self, plan, parts, states, left, results, scratch):
        self.plan, self.parts, self.results = plan, parts, results
        self.states, self.left = states, left
        self.own, self.got, self.total = scratch[0], scratch[1:6], scratch[6]
        self.own_sem, self.out_sem, self.send0, self.recv0, self.send, self.recv = scratch[7:13]
        self.core, group, depth, _, _ = place()
        core = self.core
        partner = (1 - core, group, depth)
        x_next = group + 1 - 2 * (group % 2)
        y_next = (group + 2) % 4
        first = x_next + core * (y_next - x_next)
        second = y_next + core * (x_next - y_next)
        z_next = depth + 1 - 2 * (depth % 2)
        z_far = (depth + 2) % 4
        self.across = [(core, first, depth), (core, second, depth)]
        along = [(core, group, z_next), (core, group, z_far)]
        bit_x, bit_y = group % 2, group // 2
        across_bits = [bit_x + core * (bit_y - bit_x), bit_y + core * (bit_x - bit_y)]
        along_bits = [depth % 2, depth // 2]
        self.orders = [
            ([partner] + self.across + along, [core] + across_bits + along_bits),
            ([partner] + along + self.across, [core] + along_bits + across_bits),
        ]
        self.first_rows = []
        for _, bits in self.orders:
            held = [core * plan.half]
            for k in range(1, 5):
                held.append(held[-1] + bits[k] * plan.rows(k))
            self.first_rows.append(held)

    def family(self, g):
        return [f for f in range(4) if g in FAMILIES[f]][0]

    def order(self, g):
        return self.orders[1 if g in Z_FIRST else 0]

    def held(self, g, k):
        f = self.family(g)
        if k == self.plan.enter[g] - 1:
            return self.states[f].at[:, self.plan.family_columns(f, g)]
        if k == self.plan.leave[g] - 1:
            return self.left[f].at[:, self.plan.family_columns(f, g)]
        return self.got[k].at[:, self.plan.columns(g, k)]

    def slot(self, g, k):
        return self.got[k].at[:, self.plan.columns(g, k)]

    def rows(self, first, count):
        return pl.ds(pl.multiple_of(first, 16), count)

    def own_rows(self, half):
        count = self.plan.half
        return self.rows(half * count, count)

    def away(self, g):
        index = self.plan.chosen.index(g)
        columns = self.plan.columns(g, 0)
        return remote(
            self.own.at[self.own_rows(1 - self.core), columns],
            self.got[0].at[:, columns],
            self.send0.at[index, 0],
            self.recv0.at[index, 0],
            self.orders[0][0][0],
        )

    def stage(self, g):
        index = self.plan.chosen.index(g)
        column = self.plan.columns(g, 0).start
        for i, (array, row, col, width) in enumerate(self.plan.groups[g][1]):
            block = self.parts[array].at[pl.ds(row, 2 * self.plan.half), pl.ds(col, width)]
            yield pltpu.make_async_copy(
                block, self.own.at[:, pl.ds(column, width)], self.own_sem.at[index, i]
            )
            column += width

    def load(self):
        for g in self.plan.level(0):
            for copy in self.stage(g):
                copy.start()

    def add(self, target, arrived, source, first):
        count, strip = target.shape[0], 16

        @pl.loop(0, count // strip)
        def _(i):
            r = pl.multiple_of(i * strip, strip)
            mine = source[pl.ds(pl.multiple_of(first + r, strip), strip), :]
            target[pl.ds(r, strip), :] = mine + arrived[pl.ds(r, strip), :]

    def halving(self, g, k):
        index = self.plan.chosen.index(g)
        neighbours, bits = self.order(g)
        count = self.plan.rows(k)
        return remote(
            self.held(g, k - 1).at[self.rows((1 - bits[k]) * count, count)],
            self.slot(g, k),
            self.send.at[index, k],
            self.recv.at[index, k],
            neighbours[k],
        )

    def whole(self, g):
        mates = self.plan.final
        return pl.ds(
            wide(self.plan.groups, mates[: mates.index(g)]), wide(self.plan.groups, [g])
        )

    def doubling(self, g, k):
        index = self.plan.chosen.index(g)
        held = self.first_rows[1 if g in Z_FIRST else 0]
        block = self.total.at[self.rows(held[k], self.plan.rows(k)), self.whole(g)]
        return remote(
            block, block, self.send.at[index, 4 + k], self.recv.at[index, 4 + k], self.order(g)[0][k]
        )

    def joining(self, g):
        index = self.plan.chosen.index(g)
        half = self.plan.half
        block = self.total.at[self.rows(self.core * half, half), self.whole(g)]
        return remote(
            block, block, self.send.at[index, 9], self.recv.at[index, 9], self.orders[0][0][0]
        )

    def only(self, layer, there, act):
        if layer is None:
            act()
        else:
            pl.when((self.core == layer) if there else (self.core != layer))(act)

    def emit(self, g, wait):
        index = self.plan.chosen.index(g)
        layer, pieces = self.plan.groups[g]
        column = self.whole(g).start
        for i, (array, row, col, width) in enumerate(pieces):
            copy = pltpu.make_async_copy(
                self.total.at[:, pl.ds(column, width)],
                self.results[RESULT_OF[array]].at[
                    pl.ds(row, 2 * self.plan.half), pl.ds(col, width)
                ],
                self.out_sem.at[index, i],
            )
            column += width
            self.only(layer, True, copy.wait if wait else copy.start)

    def run(self, g, step):
        layer = self.plan.groups[g][0]
        enter, leave = self.plan.enter[g], self.plan.leave[g]
        if enter < step <= 5:
            k = step - 1
            if k == 0:
                self.away(g).wait()
                mine = self.own.at[:, self.plan.columns(g, 0)]
                self.add(self.held(g, 0), self.slot(g, 0), mine, self.core * self.plan.half)
            else:
                self.halving(g, k).wait()
                count = self.plan.rows(k)
                first = self.order(g)[1][k] * count
                self.add(self.held(g, k), self.slot(g, k), self.held(g, k - 1), first)
        if step == leave and leave < 10:
            return
        if step == 0:
            for copy in self.stage(g):
                copy.wait()
            self.away(g).start()
        elif step <= 4:
            self.halving(g, step).start()
        elif step == 5:
            held = self.first_rows[1 if g in Z_FIRST else 0]
            self.total[self.rows(held[4], self.plan.rows(4)), self.whole(g)] = self.held(g, 4)[...]
            self.doubling(g, 4).start()
        elif step <= 8:
            self.doubling(g, 10 - step).wait()
            self.doubling(g, 9 - step).start()
        elif step == 9:
            self.doubling(g, 1).wait()
            self.only(layer, False, self.joining(g).start)
        else:
            self.only(layer, False, self.joining(g).wait_send)
            self.only(layer, True, self.joining(g).wait_recv)
            self.emit(g, False)


def tail_slots(plan):
    table = {}
    late = LATE
    for f in sorted(plan.spans):
        for i, g in enumerate(FAMILIES[f]):
            for n, step in enumerate(range(plan.enter[g], 11)):
                table.setdefault(late[f] + i + LAG * n, []).append((g, step))
    return table


def collect_kernel(plan, riders, *refs):
    count = len(riders)
    homes, refs = refs[:count], refs[count:]
    parts = dict(zip(plan.arrays, refs))
    refs = refs[len(plan.arrays) :]
    states = dict(zip(plan.states_in(), refs))
    refs = refs[len(states) :]
    small, refs = refs[0], refs[1:]
    home_outs, refs = refs[:count], refs[count:]
    results, small_out, refs = refs[:7], refs[7], refs[8:]
    small_got, home_send, home_recv, small_send, small_recv = refs[:5]
    reducer = Reducer(plan, parts, states, {}, results, refs[5:])
    core, group, depth, _, _ = place()
    reducer.load()
    greet(row_mates(core, group, depth) + reducer.across)

    def small_copy(k):
        return remote(
            small_out, small_got.at[k], small_send.at[k], small_recv.at[k], reducer.orders[0][0][k]
        )

    def small_step(k):
        if k > 0:
            small_copy(k - 1).wait()
            small_out[...] += small_got[k - 1]
        else:
            small_out[...] = small[...]
        if k < 5:
            small_copy(k).start()

    table = tail_slots(plan)
    for slot in range(max(max(table), 12) + 1):
        for g, step in reversed(table.get(slot, [])):
            reducer.run(g, step)
        if slot == HOME_SLOT:
            for i, rider in enumerate(riders):
                ride_copies(rider, homes[i], home_outs[i], home_send.at[i], home_recv.at[i])
        if 2 <= slot <= 12 and slot % 2 == 0:
            small_step(slot // 2 - 1)
    for g in plan.chosen:
        reducer.emit(g, True)
    for i, rider in enumerate(riders):
        ride_end(rider, homes[i], home_outs[i], home_send.at[i], home_recv.at[i])


def collect(plan, riders, parts, states, small):
    count = len(riders)
    width = riders[0].array.shape[1]
    hidden = 4 * width
    anywhere = pl.BlockSpec(memory_space=pl.ANY)
    resident = pl.BlockSpec(memory_space=pltpu.VMEM)
    dma = pltpu.SemaphoreType.DMA
    shapes = [
        (width, hidden), (hidden, width), (width, width), (width, 3 * width),
        (width, width), (width, width), (width, 2 * width),
    ]
    out = pl.pallas_call(
        functools.partial(collect_kernel, plan, riders),
        in_specs=[resident] * count
        + [anywhere] * len(plan.arrays)
        + [resident] * (len(plan.states_in()) + 1),
        out_specs=[anywhere] * (count + 7) + [resident],
        out_shape=[jax.ShapeDtypeStruct(rider.shape, BF) for rider in riders]
        + [jax.ShapeDtypeStruct(s, BF) for s in shapes]
        + [jax.ShapeDtypeStruct(small.shape, F32)],
        scratch_shapes=[
            pltpu.VMEM((5,) + small.shape, F32),
            dma((count, 2)),
            dma((count, 4)),
            dma((5,)),
            dma((5,)),
        ]
        + plan.scratch(),
        compiler_params=pltpu.CompilerParams(
            collective_id=1, has_side_effects=True, vmem_limit_bytes=56 << 20
        ),
        name="collect",
    )(
        *[rider.array for rider in riders],
        *[parts[a] for a in plan.arrays],
        *[states[f] for f in plan.states_in()],
        small,
    )
    return out[:count], out[count : count + 7], out[count + 7]


def key_loads(offsets, source, staged, sem, layer, step):
    for t in range(2):
        first = pl.multiple_of((offsets[t] + step) * PAIR, PAIR)
        yield pltpu.make_async_copy(
            source.at[layer, :, pl.ds(first, PAIR)], staged.at[layer, step, t], sem.at[layer, step, t]
        )


def key_copies(staged, held, send, recv, layer, step):
    core, group, depth, _, _ = place()
    return [
        remote(
            staged.at[layer, step, t],
            held.at[layer, step, t],
            send.at[layer, step, t],
            recv.at[layer, step, t],
            (1 - core, group, depth),
        )
        for t in range(2)
    ]


def attend_steps(layers):
    return [(layer, step) for layer in range(layers) for step in range(4)]


def begin(layers, offsets, riders, ride, source, keys, reducer=None):
    staged, sem, held, send, recv = keys
    core, group, depth, _, _ = place()
    for layer, step in attend_steps(layers):
        for copy in key_loads(offsets, source, staged, sem, layer, step):
            copy.start()
    if reducer is not None:
        reducer.load()
    mates = row_mates(core, group, depth) if riders or reducer else [(1 - core, group, depth)]
    greet(mates + (reducer.across if reducer else []))
    for layer, step in attend_steps(layers):
        for copy in key_loads(offsets, source, staged, sem, layer, step):
            copy.wait()
        for copy in key_copies(staged, held, send, recv, layer, step):
            copy.start()
    for i, rider in enumerate(riders):
        ride_copies(rider, *[r[i] if j < 2 else r.at[i] for j, r in enumerate(ride)])


def end(layers, riders, ride, keys):
    staged, sem, held, send, recv = keys
    for layer, step in attend_steps(layers):
        for copy in key_copies(staged, held, send, recv, layer, step):
            copy.wait_send()
    for i, rider in enumerate(riders):
        ride_end(rider, *[r[i] if j < 2 else r.at[i] for j, r in enumerate(ride)])


def by_layer(causal, layer, act):
    for kind in sorted(set(causal)):
        if len(set(causal)) == 1:
            act(kind)
        else:
            pl.when(layer == causal.index(kind))(functools.partial(act, kind))


def attend_kernel(causal, offsets, riders, *refs):
    layers, count = len(causal), len(riders)
    q_ref, k_ref, v_ref, kv_ref, qf_ref, kf_ref = refs[:6]
    o_ref, of_ref, lse_ref = refs[6 + count : 9 + count]
    *keys, ride_send, ride_recv = refs[9 + 2 * count :]
    staged, _, held, send, recv = keys
    ride = (refs[6 : 6 + count], refs[9 + count : 9 + 2 * count], ride_send, ride_recv)
    layer, step = pl.program_id(0), pl.program_id(1)

    @pl.when((layer == 0) & (step == 0))
    def _():
        begin(layers, offsets, riders, ride, kv_ref, keys)

    for copy in key_copies(staged, held, send, recv, layer, step):
        copy.wait_recv()

    def work(kind):
        whole, stat = attend_pair(
            kind, q_ref[0], k_ref[0], v_ref[0], held[layer, step, 0], held[layer, step, 1],
            qf_ref[0], kf_ref[0],
        )
        o_ref[0] = whole.astype(BF)
        of_ref[0] = whole
        lse_ref[0] = stat

    by_layer(causal, layer, work)

    @pl.when((layer == layers - 1) & (step == 3))
    def _():
        end(layers, riders, ride, keys)


def grad_copies(gone, got, send, recv, layer, step):
    core, group, depth, _, _ = place()
    return [
        remote(
            gone.at[layer, step, t],
            got.at[layer, step, t],
            send.at[layer, step, t],
            recv.at[layer, step, t],
            (1 - core, group, depth),
        )
        for t in range(2)
    ]


def attend_back_kernel(causal, offsets, riders, joined, plan, table, *refs):
    layers, count = len(causal), len(riders)
    q_ref, k_ref, v_ref, kv_ref, qf_ref, kf_ref, o_ref, lse_ref, do_ref = refs[:9]
    sources, refs = refs[9 : 9 + count], refs[9 + count :]
    parts = dict(zip(plan.arrays, refs))
    refs = refs[len(parts) :]
    states = dict(zip(plan.states_in(), refs))
    refs = refs[len(states) :]
    outs = 1 if joined else 2
    dq_ref, dkv_ref, refs = refs[0], refs[outs - 1], refs[outs:]
    left = dict(zip(plan.states_out(), refs))
    refs = refs[len(left) :]
    targets, refs = refs[:count], refs[count:]
    keys, (gone, got, kept, g_send, g_recv) = refs[:5], refs[5:10]
    staged, _, held, send, recv = keys
    scratch, (ride_send, ride_recv) = refs[10:-2], refs[-2:]
    ride = (sources, targets, ride_send, ride_recv)
    layer, step = pl.program_id(0), pl.program_id(1)
    width = 4 * PAIR
    reducer = Reducer(plan, parts, states, left, [], scratch)

    @pl.when((layer == 0) & (step == 0))
    def _():
        begin(layers, offsets, riders, ride, kv_ref, keys, reducer)

    for slot in range(4 * layers):
        moves = table.get(slot, [])
        if moves:

            @pl.when((layer == slot // 4) & (step == slot % 4))
            def _():
                for g, stage in moves:
                    reducer.run(g, stage)

    for copy in key_copies(staged, held, send, recv, layer, step):
        copy.wait_recv()

    def work(kind):
        columns = pl.ds(pl.multiple_of(step * PAIR, PAIR), PAIR)

        @pl.loop(0, 2)
        def _(head):
            mine, dq, dk, dv, dko, dvo = attend_back_head(
                kind, head, q_ref[0], k_ref[0], v_ref[0], held[layer, step, 0],
                held[layer, step, 1], qf_ref[0], kf_ref[0], o_ref[0], lse_ref[0], do_ref[0],
            )
            dq_ref[layer, :, columns] = jnp.where(mine, dq.astype(BF), dq_ref[layer, :, columns])
            kept[layer, step, 0] = jnp.where(mine, dk, kept[layer, step, 0])
            kept[layer, step, 1] = jnp.where(mine, dv, kept[layer, step, 1])
            gone[layer, step, 0] = jnp.where(mine, dko.astype(BF), gone[layer, step, 0])
            gone[layer, step, 1] = jnp.where(mine, dvo.astype(BF), gone[layer, step, 1])

    by_layer(causal, layer, work)
    for copy in grad_copies(gone, got, g_send, g_recv, layer, step):
        copy.start()

    @pl.when((layer == layers - 1) & (step == 3))
    def _():
        for one, at in attend_steps(layers):
            for t, copy in enumerate(grad_copies(gone, got, g_send, g_recv, one, at)):
                copy.wait()
                first = (width if joined else 0) + t * width + at * PAIR
                dkv_ref[one, :, first : first + PAIR] = (
                    kept[one, at, t] + got[one, at, t].astype(F32)
                ).astype(BF)
        for g in plan.chosen:
            reducer.run(g, plan.leave[g])
        end(layers, riders, ride, keys)


def attend_specs(size, offsets, masks):
    def column(at):
        return pl.BlockSpec((1, size, PAIR), lambda l, p: (l, 0, at + p))

    def shared(rows, first):
        return pl.BlockSpec((1, rows, PAIR), lambda l, p: (l + first, 0, 0))

    return (
        [column(at) for at in offsets]
        + [pl.BlockSpec(memory_space=pl.ANY)]
        + [shared(size, masks[0]), shared(2 * size, masks[1])]
    ), column


def key_scratch(layers, size):
    slots = pltpu.VMEM((layers, 4, 2, size, PAIR), BF)
    sems = pltpu.SemaphoreType.DMA((layers, 4, 2))
    return [slots, sems, slots, sems, sems]


def attend_call(
    kernel, name, layers, riders, collective, in_specs, out_specs, out_shape, scratch, flops, args
):
    count = len(riders)
    dma = pltpu.SemaphoreType.DMA
    return pl.pallas_call(
        kernel,
        grid=(layers, 4),
        in_specs=in_specs,
        out_specs=out_specs + [pl.BlockSpec(memory_space=pl.ANY)] * count,
        out_shape=out_shape + [jax.ShapeDtypeStruct(rider.shape, BF) for rider in riders],
        scratch_shapes=scratch + [dma((max(count, 1), 2)), dma((max(count, 1), 4))],
        compiler_params=pltpu.CompilerParams(
            vmem_limit_bytes=56 << 20, collective_id=collective, has_side_effects=True
        ),
        cost_estimate=pl.CostEstimate(flops=flops, bytes_accessed=flops // 512, transcendentals=0),
        name=name,
    )(*args)


def attend_forward(q, kv, offsets, masks, features, causal, riders, collective):
    layers, size = len(causal), q.shape[1]
    width = 4 * PAIR
    in_specs, column = attend_specs(size, offsets, masks)
    dma = pltpu.SemaphoreType.DMA
    return attend_call(
        functools.partial(attend_kernel, causal, offsets[1:], riders),
        "attend_forward",
        layers,
        riders,
        collective,
        in_specs + [pl.BlockSpec(memory_space=pltpu.VMEM)] * len(riders),
        [column(0)] * 3,
        [jax.ShapeDtypeStruct((layers, size, width), t) for t in (BF, F32, F32)],
        key_scratch(layers, size),
        16 * layers * size * size * width,
        (q, kv, kv, kv, *features, *[rider.array for rider in riders]),
    )


def attend_backward(
    q, kv, offsets, masks, features, o, lse, do, causal, riders, collective, joined,
    plan, table, parts, states,
):
    layers, size = len(causal), q.shape[1]
    width = 4 * PAIR
    in_specs, column = attend_specs(size, offsets, masks)
    dma = pltpu.SemaphoreType.DMA
    resident = pl.BlockSpec(memory_space=pltpu.VMEM)
    anywhere = pl.BlockSpec(memory_space=pl.ANY)
    widths = [3 * width] if joined else [width, 2 * width]
    slots = (layers, 4, 2, size, PAIR)
    left = [plan.state_shape(f, plan.spans[f][1]) for f in plan.states_out()]
    return attend_call(
        functools.partial(
            attend_back_kernel, causal, offsets[1:], riders, joined, plan, table
        ),
        "attend_backward",
        layers,
        riders,
        collective,
        in_specs
        + [column(0)] * 3
        + [resident] * len(riders)
        + [anywhere] * len(plan.arrays)
        + [resident] * len(plan.states_in()),
        [resident] * (len(widths) + len(left)),
        [jax.ShapeDtypeStruct((layers, size, w), BF) for w in widths] + left,
        key_scratch(layers, size)
        + [
            pltpu.VMEM(slots, BF),
            pltpu.VMEM(slots, BF),
            pltpu.VMEM(slots, F32),
            dma((layers, 4, 2)),
            dma((layers, 4, 2)),
        ]
        + plan.scratch(),
        40 * layers * size * size * width,
        (
            q, kv, kv, kv, *features, o, lse, do,
            *[rider.array for rider in riders],
            *[parts[a] for a in plan.arrays],
            *[states[f] for f in plan.states_in()],
        ),
    )


def dot(a, b):
    return lax.dot_general(a, b, (((1,), (0,)), ((), ())), preferred_element_type=F32)


def dot_back(a, b):
    return lax.dot_general(a, b, (((1,), (1,)), ((), ())), preferred_element_type=F32)


def dot_outer(a, b):
    return lax.dot_general(a, b, (((0,), (0,)), ((), ())), preferred_element_type=F32)


def each(function, *stacked):
    return jnp.stack([function(*(s[i] for s in stacked)) for i in range(2)])


def row_shards(
    inputs,
    cotangent,
    qkv_weight,
    out_weight,
    up_weight,
    down_weight,
    norm_gain,
    norm_bias,
    cross_q_weight,
    cross_kv_weight,
    cross_out_weight,
    cross_gain,
    cross_bias,
    source_segments,
    target_segments,
):
    core = lax.axis_index("section")
    depth = lax.axis_index("seq")
    span = inputs.shape[2]
    width = inputs.shape[3]

    segments = jnp.stack([source_segments, target_segments])
    both, features = spread(
        inputs[0],
        segments,
        qkv_weight[0],
        out_weight[0],
        up_weight[0],
        down_weight[0],
        norm_gain[0],
        norm_bias[0],
    )
    x_both, qkv_both, out_both, up_both, down_both, gain_both, bias_both = both
    g_e, g_d = gain_both[0], gain_both[1]
    b_e, b_d = bias_both[0], bias_both[1]
    wu_e, wu_d = up_both[0], up_both[1]
    wd_e, wd_d = down_both[0], down_both[1]

    qkv = lax.dot_general(
        x_both, qkv_both, (((2,), (1,)), ((0,), (0,))), preferred_element_type=F32
    ).astype(BF)
    self_args = ((0, 4, 8), (0, 0), features)
    o, o_wide, lse, cot = attend_forward(
        qkv, qkv, *self_args, (False, True), [RowRider(cotangent)], 2
    )
    cot = cot.astype(F32)
    summed = x_both.astype(F32) + lax.dot_general(
        o, out_both, (((2,), (1,)), ((0,), (0,))), preferred_element_type=F32
    )
    s1, t1 = summed[0], summed[1]

    h_s = layer_norm(s1, g_e[0], b_e[0])
    h_s_low = h_s.astype(BF)
    u_s = dot(h_s_low, wu_e)
    gel_s = gelu_tanh(u_s).astype(BF)
    s2 = h_s + dot(gel_s, wd_e)
    memory = layer_norm(s2, g_e[1], b_e[1]).astype(BF)
    ckv = dot(memory, cross_kv_weight).astype(BF)

    h_t = layer_norm(t1, g_d[0], b_d[0])
    h_t_low = h_t.astype(BF)
    cq = dot(h_t_low, cross_q_weight).astype(BF)
    cross_args = ((0, 0, 4), (1, 0), features)
    o_c, oc_wide, lse_c = attend_forward(cq[None], ckv[None], *cross_args, (False,), [], 3)
    o_c = o_c[0]
    t2 = h_t + dot(o_c, cross_out_weight)
    c_t = layer_norm(t2, cross_gain, cross_bias)
    c_t_low = c_t.astype(BF)
    u_t = dot(c_t_low, wu_d)
    gel_t = gelu_tanh(u_t).astype(BF)
    t3 = c_t + dot(gel_t, wd_d)
    decoded, pull_t3 = jax.vjp(layer_norm, t3, g_d[1], b_d[1])
    decoded = decoded.astype(BF)

    grad_t3, gg_d1, gb_d1 = pull_t3(cot)
    low_t3 = grad_t3.astype(BF)
    gw_down_d = dot_outer(gel_t, low_t3).astype(BF)
    grad_u_t = jax.vjp(gelu_tanh, u_t)[1](dot_back(low_t3, wd_d))[0].astype(BF)
    gw_up_d = dot_outer(c_t_low, grad_u_t).astype(BF)
    grad_c = grad_t3 + dot_back(grad_u_t, wu_d)
    grad_t2, gg_c, gb_c = jax.vjp(layer_norm, t2, cross_gain, cross_bias)[1](grad_c)
    low_t2 = grad_t2.astype(BF)
    gw_cross_out = dot_outer(o_c, low_t2).astype(BF)
    grad_o_c = dot_back(low_t2, cross_out_weight).astype(BF)
    hidden = wu_d.shape[1]
    parts = {0: gw_up_d, 1: gw_down_d}
    plan = Plan(width, hidden, {0: (0, 2)})
    grad_cq, grad_ckv, state_d, home_memory, home_decoded = attend_backward(
        cq[None], ckv[None], *cross_args, oc_wide, lse_c, grad_o_c[None], (False,),
        [HomeRider(memory, 0), HomeRider(decoded, 1)], 4, False, plan, CROSS_TABLE, parts, {},
    )
    grad_cq, grad_ckv = grad_cq[0], grad_ckv[0]
    gw_cross_q = dot_outer(h_t_low, grad_cq).astype(BF)
    grad_h = grad_t2 + dot_back(grad_cq, cross_q_weight)
    grad_t1, gg_d0, gb_d0 = jax.vjp(layer_norm, t1, g_d[0], b_d[0])[1](grad_h)
    low_t1 = grad_t1.astype(BF)

    gw_cross_kv = dot_outer(memory, grad_ckv).astype(BF)
    grad_memory = dot_back(grad_ckv, cross_kv_weight).astype(BF).astype(F32)
    grad_s2, gg_e1, gb_e1 = jax.vjp(layer_norm, s2, g_e[1], b_e[1])[1](grad_memory)
    low_s2 = grad_s2.astype(BF)
    gw_down_e = dot_outer(gel_s, low_s2).astype(BF)
    grad_u_s = jax.vjp(gelu_tanh, u_s)[1](dot_back(low_s2, wd_e))[0].astype(BF)
    gw_up_e = dot_outer(h_s_low, grad_u_s).astype(BF)
    grad_h = grad_s2 + dot_back(grad_u_s, wu_e)
    grad_s1, gg_e0, gb_e0 = jax.vjp(layer_norm, s1, g_e[0], b_e[0])[1](grad_h)
    low_s1 = grad_s1.astype(BF)

    low_1 = jnp.stack([low_s1, low_t1])
    grad_o = lax.dot_general(
        low_1, out_both, (((2,), (2,)), ((0,), (0,))), preferred_element_type=F32
    ).astype(BF)
    parts = {2: gw_up_e, 3: gw_down_e}
    plan = Plan(width, hidden, {0: (2, 5), 1: (0, 2)})
    grad_qkv, state_d, state_e = attend_backward(
        qkv, qkv, *self_args, o_wide, lse, grad_o, (False, True), [], 5, True,
        plan, SELF_TABLE, parts, {0: state_d},
    )
    parts = {
        4: dot_outer(o[1], low_t1).astype(BF),
        5: dot_outer(x_both[1], grad_qkv[1]).astype(BF),
        6: dot_outer(o[0], low_s1).astype(BF),
        7: dot_outer(x_both[0], grad_qkv[0]).astype(BF),
        8: gw_cross_out,
        9: gw_cross_q,
        10: gw_cross_kv,
    }
    grad_x = jnp.stack([grad_s1, grad_t1]) + lax.dot_general(
        grad_qkv, qkv_both, (((2,), (2,)), ((0,), (0,))), preferred_element_type=F32
    )
    grad_x = grad_x.astype(BF)

    small = jnp.stack(
        [gg_e0, gg_e1, gb_e0, gb_e1, gg_d0, gg_d1, gb_d0, gb_d1, gg_c, gb_c]
        + [jnp.zeros_like(gg_c)] * 6
    )
    plan = Plan(width, hidden, {0: (5, 10), 1: (2, 10), 2: (0, 10), 3: (0, 10)})
    (home_xs, home_xt), sums, small = collect(
        plan,
        [HomeRider(grad_x[0], 0), HomeRider(grad_x[1], 1)],
        parts,
        {0: state_d, 1: state_e},
        small,
    )
    outputs = jnp.where(core == 0, home_memory, home_decoded)
    grads = jnp.where(core == 0, home_xs, home_xt)
    g_up, g_down, g_out, g_qkv, g_cross_out, g_cross_q, g_cross_kv = (
        value.astype(F32) for value in sums
    )
    layer_small = jnp.where(core == 0, small[:4], small[4:8])
    return (
        outputs[None],
        grads.astype(F32)[None],
        g_qkv[None],
        g_out[None],
        g_up[None],
        g_down[None],
        layer_small[None, :2],
        layer_small[None, 2:],
        g_cross_q,
        g_cross_kv,
        g_cross_out,
        small[8],
        small[9],
    )


def solution(mesh):
    in_specs = (
        P("section", "dp", "seq", None),
        P("dp", "seq", None),
        P("section", None, None),
        P("section", None, None),
        P("section", None, None),
        P("section", None, None),
        P("section", None, None),
        P("section", None, None),
        P(),
        P(),
        P(),
        P(),
        P(),
        P("dp", None),
        P("dp", None),
    )
    out_specs = (
        P("section", "dp", "seq", None),
        P("section", "dp", "seq", None),
        P("section", None, None),
        P("section", None, None),
        P("section", None, None),
        P("section", None, None),
        P("section", None, None),
        P("section", None, None),
        P(),
        P(),
        P(),
        P(),
        P(),
    )
    whole_rows = mesh.shape["section"] == 2 and mesh.shape["seq"] == 4 and mesh.shape["dp"] == 4
    body = row_shards if whole_rows else shards
    return jax.shard_map(body, mesh=mesh, in_specs=in_specs, out_specs=out_specs, check_vma=False)
```

```python
import functools

import jax
import jax.numpy as jnp
from jax import lax
from jax.experimental import pallas as pl
from jax.experimental.pallas import tpu as pltpu
from jax.sharding import PartitionSpec as P

DH = 64
MICRO = 2
MB_ROWS = 2


EPSILON = 1e-05
NEGATIVE = -1e30


def from_behind(value, axis, steps):
    count = lax.axis_size(axis)
    leading, last = (max(0, -steps), min(count, count - steps))
    return lax.ppermute(value, axis, [(source, source + steps) for source in range(leading, last)])


def layer_norm(vector, gain_row, bias_row):
    centre = vector - jnp.mean(vector, axis=-1, keepdims=True)
    spread = jnp.mean(centre * centre, axis=-1, keepdims=True)
    return centre * lax.rsqrt(spread + EPSILON) * gain_row + bias_row


def gelu_tanh(vector):
    return jax.nn.gelu(vector, approximate=True)


def heads_view(vector):
    return vector.reshape(vector.shape[:-1] + (vector.shape[-1] // DH, DH))


def joined_view(vector):
    return vector.reshape(vector.shape[:-2] + (vector.shape[-2] * vector.shape[-1],))


def dense_rows(left_side, right_side):
    return jnp.einsum("rsd,de->rse", left_side, right_side, preferred_element_type=jnp.float32)


def dense_back(left_side, right_side):
    return jnp.einsum("rse,de->rsd", left_side, right_side, preferred_element_type=jnp.float32)


def outer_sum(left_side, right_side):
    return jnp.einsum("rsd,rse->de", left_side, right_side, preferred_element_type=jnp.float32)


def build_mask(query_ids, key_ids, query_places, key_places, causal):
    same_doc = query_ids[:, :, None] == key_ids[:, None, :]
    ordered = (key_places[None, :] <= query_places[:, None]) | jnp.logical_not(causal)
    return same_doc & ordered[None]


def soft_forward(queries, key_rows, value_rows, allowed):
    score_scale = DH ** (-0.5)
    scores = (
        jnp.einsum(
            "rqhe,rkhe->rhqk",
            heads_view(queries),
            heads_view(key_rows),
            preferred_element_type=jnp.float32,
        )
        * score_scale
    )
    scores = jnp.where(allowed[:, None], scores, NEGATIVE)
    highest = jnp.max(scores, axis=-1, keepdims=True)
    exp_terms = jnp.exp(scores - highest)
    totals = jnp.sum(exp_terms, axis=-1, keepdims=True)
    weights = exp_terms / totals
    log_total = (highest + jnp.log(totals))[..., 0]
    mixed_out = jnp.einsum(
        "rhqk,rkhe->rqhe",
        weights.astype(jnp.bfloat16),
        heads_view(value_rows),
        preferred_element_type=jnp.float32,
    )
    return (joined_view(mixed_out), weights, log_total)


def score_grads(grad_mixed, value_rows, weights):
    grad_weights = jnp.einsum(
        "rqhe,rkhe->rhqk",
        heads_view(grad_mixed),
        heads_view(value_rows),
        preferred_element_type=jnp.float32,
    )
    inner_sum = jnp.sum(grad_weights * weights, axis=-1, keepdims=True)
    grad_scores = (weights * (grad_weights - inner_sum)).astype(jnp.bfloat16)
    return (grad_scores, inner_sum[..., 0])


def attend_keys(queries, key_rows, value_rows, query_ids, key_ids, causal):
    span_len = key_rows.shape[1]
    offset = lax.axis_index("seq") * span_len
    whole_keys, whole_values = (
        lax.all_gather(key_rows, "seq", axis=1, tiled=True),
        lax.all_gather(value_rows, "seq", axis=1, tiled=True),
    )
    own_positions = offset + jnp.arange(span_len)
    all_positions = jnp.arange(whole_keys.shape[1])
    own_ids = lax.dynamic_slice_in_dim(query_ids, offset, span_len, 1)
    allowed = build_mask(own_ids, key_ids, own_positions, all_positions, causal)
    mixed_out, weights, log_total = soft_forward(queries, whole_keys, whole_values, allowed)
    kept_state = (
        queries,
        key_rows,
        value_rows,
        whole_keys,
        whole_values,
        weights,
        log_total,
        query_ids,
        key_ids,
        causal,
    )
    return (mixed_out, kept_state)


def attend_back(kept_state, grad_mixed):
    (
        queries,
        key_rows,
        value_rows,
        whole_keys,
        whole_values,
        weights,
        log_total,
        query_ids,
        key_ids,
        causal,
    ) = kept_state
    score_scale = DH ** (-0.5)
    grad_scores, inner_sum = score_grads(grad_mixed, whole_values, weights)
    grad_queries = (
        jnp.einsum(
            "rhqk,rkhe->rqhe",
            grad_scores,
            heads_view(whole_keys),
            preferred_element_type=jnp.float32,
        )
        * score_scale
    )
    part_keys = (
        jnp.einsum(
            "rhqk,rqhe->rkhe", grad_scores, heads_view(queries), preferred_element_type=jnp.float32
        )
        * score_scale
    )
    part_values = jnp.einsum(
        "rhqk,rqhe->rkhe",
        weights.astype(jnp.bfloat16),
        heads_view(grad_mixed),
        preferred_element_type=jnp.float32,
    )
    grad_keys, grad_values = (
        lax.psum_scatter(
            joined_view(part_keys).astype(jnp.bfloat16), "seq", scatter_dimension=1, tiled=True
        ).astype(jnp.float32),
        lax.psum_scatter(
            joined_view(part_values).astype(jnp.bfloat16), "seq", scatter_dimension=1, tiled=True
        ).astype(jnp.float32),
    )
    return (joined_view(grad_queries), grad_keys, grad_values)


def layer_forward(tokens, memory_in, own_ids, source_ids, target_ids, params, decoder):
    (
        qkv_matrix,
        out_matrix,
        up_matrix,
        down_matrix,
        norm_gains,
        norm_biases,
        query_matrix,
        pair_matrix,
        cross_matrix,
        cross_gains,
        cross_shift,
    ) = params
    residual = tokens.astype(jnp.float32)
    packed = dense_rows(tokens, qkv_matrix).astype(jnp.bfloat16)
    queries, key_rows, value_rows = jnp.split(packed, 3, axis=-1)
    mixed_out, self_state = attend_keys(queries, key_rows, value_rows, own_ids, own_ids, decoder)
    mixed_low = mixed_out.astype(jnp.bfloat16)
    first_sum = residual + dense_rows(mixed_low, out_matrix)
    first_norm = layer_norm(first_sum, norm_gains[0], norm_biases[0])
    first_low = first_norm.astype(jnp.bfloat16)
    cross_query = dense_rows(first_low, query_matrix).astype(jnp.bfloat16)
    cross_pair = dense_rows(memory_in, pair_matrix).astype(jnp.bfloat16)
    cross_keys, cross_values = jnp.split(cross_pair, 2, axis=-1)
    cross_mixed, cross_state = attend_keys(
        cross_query, cross_keys, cross_values, target_ids, source_ids, False
    )
    cross_low = cross_mixed.astype(jnp.bfloat16)
    cross_sum = first_norm + dense_rows(cross_low, cross_matrix)
    second = jnp.where(decoder, layer_norm(cross_sum, cross_gains, cross_shift), first_norm)
    second_low = second.astype(jnp.bfloat16)
    upward = dense_rows(second_low, up_matrix)
    gated_low = gelu_tanh(upward).astype(jnp.bfloat16)
    last_sum = second + dense_rows(gated_low, down_matrix)
    output = layer_norm(last_sum, norm_gains[1], norm_biases[1])
    kept_state = (
        tokens,
        self_state,
        mixed_low,
        first_sum,
        first_low,
        cross_state,
        cross_low,
        cross_sum,
        second_low,
        upward,
        gated_low,
        last_sum,
    )
    return (output, kept_state)


def layer_backward(kept_state, grad_out, params, decoder):
    (
        qkv_matrix,
        out_matrix,
        up_matrix,
        down_matrix,
        norm_gains,
        norm_biases,
        query_matrix,
        pair_matrix,
        cross_matrix,
        cross_gains,
        cross_shift,
    ) = params
    (
        tokens,
        self_state,
        mixed_low,
        first_sum,
        first_low,
        cross_state,
        cross_low,
        cross_sum,
        second_low,
        upward,
        gated_low,
        last_sum,
    ) = kept_state
    unused, pull_last = jax.vjp(layer_norm, last_sum, norm_gains[1], norm_biases[1])
    grad_last, grad_gain_last, grad_bias_last = pull_last(grad_out)
    down_in = grad_last.astype(jnp.bfloat16)
    grad_down = outer_sum(gated_low, down_in)
    grad_gated = dense_back(down_in, down_matrix)
    unused, pull_gelu = jax.vjp(gelu_tanh, upward)
    up_in = pull_gelu(grad_gated)[0].astype(jnp.bfloat16)
    grad_up = outer_sum(second_low, up_in)
    grad_second = grad_last + dense_back(up_in, up_matrix)
    unused, pull_cross = jax.vjp(layer_norm, cross_sum, cross_gains, cross_shift)
    grad_cross_sum, grad_cross_gain, grad_cross_bias = pull_cross(
        jnp.where(decoder, grad_second, 0.0)
    )
    grad_first = jnp.where(decoder, grad_cross_sum, grad_second)
    cross_in = grad_cross_sum.astype(jnp.bfloat16)
    grad_cross_out = outer_sum(cross_low, cross_in)
    grad_cross_mixed = dense_back(cross_in, cross_matrix).astype(jnp.bfloat16)
    grad_cross_query, grad_cross_keys, grad_cross_values = attend_back(
        cross_state, grad_cross_mixed
    )
    query_in = grad_cross_query.astype(jnp.bfloat16)
    grad_query_matrix = outer_sum(first_low, query_in)
    grad_first = grad_first + dense_back(query_in, query_matrix)
    pair_in = jnp.concatenate([grad_cross_keys, grad_cross_values], axis=-1).astype(jnp.bfloat16)
    unused, pull_first = jax.vjp(layer_norm, first_sum, norm_gains[0], norm_biases[0])
    grad_first_sum, grad_gain_first, grad_bias_first = pull_first(grad_first)
    out_in = grad_first_sum.astype(jnp.bfloat16)
    grad_out_matrix = outer_sum(mixed_low, out_in)
    grad_mixed = dense_back(out_in, out_matrix).astype(jnp.bfloat16)
    grad_queries, grad_keys, grad_values = attend_back(self_state, grad_mixed)
    qkv_in = jnp.concatenate([grad_queries, grad_keys, grad_values], axis=-1).astype(jnp.bfloat16)
    grad_qkv_matrix = outer_sum(tokens, qkv_in)
    grad_tokens = grad_first_sum + dense_back(qkv_in, qkv_matrix)
    grad_set = (
        grad_qkv_matrix,
        grad_out_matrix,
        grad_up,
        grad_down,
        jnp.stack([grad_gain_first, grad_gain_last]),
        jnp.stack([grad_bias_first, grad_bias_last]),
        grad_query_matrix,
        jnp.zeros(pair_matrix.shape, jnp.float32),
        grad_cross_out,
        grad_cross_gain,
        grad_cross_bias,
    )
    return (grad_tokens, pair_in, grad_set)


def shards(
    inputs,
    cotangent,
    qkv_weight,
    out_weight,
    up_weight,
    down_weight,
    norm_gain,
    norm_bias,
    cross_q_weight,
    cross_kv_weight,
    cross_out_weight,
    cross_gain,
    cross_bias,
    source_segments,
    target_segments,
):
    section_index = lax.axis_index("section")
    decoder = section_index == 1
    params = (
        qkv_weight[0],
        out_weight[0],
        up_weight[0],
        down_weight[0],
        norm_gain[0],
        norm_bias[0],
        cross_q_weight,
        cross_kv_weight,
        cross_out_weight,
        cross_gain,
        cross_bias,
    )
    tokens_all = inputs[0]
    own_all = jnp.where(decoder, target_segments, source_segments)
    span_len = tokens_all.shape[1]
    features = tokens_all.shape[2]
    memory_in = jnp.zeros((MB_ROWS, span_len, features), jnp.bfloat16)
    outputs_all = jnp.zeros(tokens_all.shape, jnp.bfloat16)
    caches = []
    sent_rows = []
    for forward_tick in range(MICRO + 1):
        micro_index = forward_tick - section_index
        active = (micro_index >= 0) & (micro_index < MICRO)
        first_row = jnp.clip(micro_index, 0, MICRO - 1) * MB_ROWS
        rows_now = lax.dynamic_slice_in_dim(tokens_all, first_row, MB_ROWS, 0)
        own_now = lax.dynamic_slice_in_dim(own_all, first_row, MB_ROWS, 0)
        source_now = lax.dynamic_slice_in_dim(source_segments, first_row, MB_ROWS, 0)
        target_now = lax.dynamic_slice_in_dim(target_segments, first_row, MB_ROWS, 0)
        output, kept_state = layer_forward(
            rows_now, memory_in, own_now, source_now, target_now, params, decoder
        )
        output_low = output.astype(jnp.bfloat16)
        current = lax.dynamic_slice_in_dim(outputs_all, first_row, MB_ROWS, 0)
        outputs_all = lax.dynamic_update_slice_in_dim(
            outputs_all, jnp.where(active, output_low, current), first_row, 0
        )
        caches.append(kept_state)
        sent_rows.append(output_low)
        if forward_tick < MICRO:
            memory_in = from_behind(output_low, "section", 1)
    grad_pair_in = jnp.zeros((MB_ROWS, span_len, 2 * features), jnp.bfloat16)
    totals = tuple((jnp.zeros(param_item.shape, jnp.float32) for param_item in params))
    input_all = jnp.zeros(tokens_all.shape, jnp.float32)
    for backward_tick in range(MICRO + 1):
        forward_tick = MICRO - backward_tick
        micro_index = forward_tick - section_index
        active = (micro_index >= 0) & (micro_index < MICRO)
        first_row = jnp.clip(micro_index, 0, MICRO - 1) * MB_ROWS
        cot_now = lax.dynamic_slice_in_dim(cotangent, first_row, MB_ROWS, 0).astype(jnp.float32)
        memory_grad = lax.optimization_barrier(
            dense_back(grad_pair_in, params[7]).astype(jnp.bfloat16)
        ).astype(jnp.float32)
        pair_term = outer_sum(sent_rows[forward_tick], grad_pair_in)
        grad_out = jnp.where(decoder, cot_now, memory_grad)
        grad_tokens, pair_in, grad_set = layer_backward(
            caches[forward_tick], grad_out, params, decoder
        )
        grad_set = grad_set[:7] + (jnp.where(decoder, 0.0, pair_term),) + grad_set[8:]
        totals = jax.tree.map(
            lambda total_sum, new_term: total_sum + jnp.where(active, new_term, 0.0),
            totals,
            grad_set,
        )
        current = lax.dynamic_slice_in_dim(input_all, first_row, MB_ROWS, 0)
        input_all = lax.dynamic_update_slice_in_dim(
            input_all, jnp.where(active, grad_tokens, current), first_row, 0
        )
        if backward_tick < MICRO:
            grad_pair_in = from_behind(pair_in, "section", -1)
    layer_part = lax.psum(
        (totals[0], totals[1], totals[2], totals[3], totals[4], totals[5]), ("dp", "seq")
    )
    cross_part = lax.psum(
        (totals[6], totals[7], totals[8], totals[9], totals[10]), ("section", "dp", "seq")
    )
    return (
        outputs_all[None],
        input_all[None],
        layer_part[0][None],
        layer_part[1][None],
        layer_part[2][None],
        layer_part[3][None],
        layer_part[4][None],
        layer_part[5][None],
        cross_part[0],
        cross_part[1],
        cross_part[2],
        cross_part[3],
        cross_part[4],
    )


BF = jnp.bfloat16
F32 = jnp.float32
AXES = ("section", "dp", "seq")
PAIR = 2 * DH
STAT = 8
Q_ROWS = 256
K_ROWS = 256
AHEAD = 2


def swap(value, move):
    pairs = []
    for core in range(2):
        for group in range(4):
            for depth in range(4):
                to = move(core, group, depth)
                if to is not None:
                    pairs.append(
                        ((core * 4 + group) * 4 + depth, (to[0] * 4 + to[1]) * 4 + to[2])
                    )
    return lax.ppermute(value, AXES, pairs)


def to_core(value):
    return swap(value, lambda core, group, depth: (1 - core, group, depth))


def replace_block(whole, block, at, axis):
    size, count = block.shape[axis], whole.shape[axis]
    parts = [lax.slice_in_dim(whole, 0, at, axis=axis)] if at > 0 else []
    parts.append(block)
    if at + size < count:
        parts.append(lax.slice_in_dim(whole, at + size, count, axis=axis))
    return jnp.concatenate(parts, axis=axis)


def attend_pair(causal, q, k, v, ko, vo, qf, kf):
    size = q.shape[0]
    half = size // 2
    lane = lax.broadcasted_iota(jnp.int32, (size, PAIR), 1)
    low_lanes = lane < DH
    q = q * jnp.array(DH ** (-0.5), BF)
    kf, kfo = kf[:size], kf[size:]
    one = jnp.ones_like(v)
    tasks = []
    for head in range(2):
        mine = low_lanes if head == 0 else jnp.logical_not(low_lanes)
        qa = jnp.where(mine, q, qf)
        ka = [jnp.where(mine, k, kf), jnp.where(mine, ko, kfo)]
        va = [jnp.where(mine, v, one), jnp.where(mine, vo, one)]
        for start in range(0, size, Q_ROWS):
            rows = slice(start, start + Q_ROWS)
            if causal and start < half:
                kk = jnp.concatenate([ka[0][:half], ka[1][:half]], axis=0)
                vv = jnp.concatenate([va[0][:half], va[1][:half]], axis=0)
                diagonal = 0
            else:
                kk = jnp.concatenate(ka, axis=0)
                vv = jnp.concatenate(va, axis=0)
                diagonal = half if causal else None
            tasks.append((qa[rows], kk, vv, diagonal, start % half))

    def scores(task):
        qq, kk, _, _, _ = task
        return lax.dot_general(qq, kk, (((1,), (1,)), ((), ())), preferred_element_type=F32)

    def finish(task, s):
        _, _, vv, diagonal, first = task
        if diagonal is not None:
            row = lax.broadcasted_iota(jnp.int32, (Q_ROWS, half), 0) + first
            col = lax.broadcasted_iota(jnp.int32, (Q_ROWS, half), 1)
            cut = jnp.where(col <= row, s[:, diagonal : diagonal + half], NEGATIVE)
            s = replace_block(s, cut, diagonal, 1)
        top = jnp.max(s, axis=1, keepdims=True)
        p = jnp.exp(s - top).astype(BF)
        o = lax.dot_general(p, vv, (((1,), (0,)), ((), ())), preferred_element_type=F32)
        return o / pltpu.roll(o, DH, 1), top + jnp.log(o)

    done = []
    ahead = [scores(t) for t in tasks[:AHEAD]]
    for i, task in enumerate(tasks):
        if i + AHEAD < len(tasks):
            ahead.append(scores(tasks[i + AHEAD]))
        done.append(finish(task, ahead[i]))
    count = size // Q_ROWS
    outs = [jnp.concatenate([d[0] for d in done[h * count :][:count]], axis=0) for h in range(2)]
    stats = [jnp.concatenate([d[1] for d in done[h * count :][:count]], axis=0) for h in range(2)]
    return jnp.where(low_lanes, outs[0], outs[1]), jnp.where(low_lanes, stats[1], stats[0])


def split3(value):
    a = value.astype(BF)
    rest = value - a.astype(F32)
    b = rest.astype(BF)
    c = (rest - b.astype(F32)).astype(BF)
    return a, b, c


def with_stat(base, value, lane):
    a, b, c = split3(-value)
    at = lane & (DH - 1)
    base = jnp.where(at == STAT, a, base)
    base = jnp.where(at == STAT + 1, b, base)
    return jnp.where(at == STAT + 2, c, base)


def attend_back_head(causal, head, q, k, v, ko, vo, qf, kf, o, lse, do):
    size = q.shape[0]
    half = size // 2
    lane = lax.broadcasted_iota(jnp.int32, (size, PAIR), 1)
    mine = (lane >= head * DH) & (lane < head * DH + DH)
    scale = DH ** (-0.5)
    q = q * jnp.array(scale, BF)
    kf, kfo = kf[:size], kf[size:]
    inner = jnp.sum(jnp.where(mine, do.astype(F32) * o, 0.0), axis=1, keepdims=True)
    dstat = with_stat(jnp.zeros_like(do), jnp.broadcast_to(inner, o.shape), lane)
    qa = jnp.where(mine, q, with_stat(qf, lse, lane))
    da = jnp.where(mine, do, dstat)
    tasks = []
    for own, keys, values, marks in ((True, k, v, kf), (False, ko, vo, kfo)):
        ka = jnp.where(mine, keys, marks)
        va = jnp.where(mine, values, marks)
        for start in range(0, size, K_ROWS):
            rows = slice(start, start + K_ROWS)
            late = causal and start >= half
            first = half if late else 0
            diagonal = (start % half) if causal and own else None
            tasks.append((ka[rows], va[rows], keys[rows], qa[first:], da[first:], first, diagonal))

    def scores(task):
        ka, va, _, qa, da, _, _ = task
        s = lax.dot_general(ka, qa, (((1,), (1,)), ((), ())), preferred_element_type=F32)
        dp = lax.dot_general(va, da, (((1,), (1,)), ((), ())), preferred_element_type=F32)
        return s, dp

    def finish(task, both):
        _, _, keys, _, _, first, diagonal = task
        s, dp = both
        if diagonal is not None:
            row = lax.broadcasted_iota(jnp.int32, (K_ROWS, half), 0) + diagonal
            col = lax.broadcasted_iota(jnp.int32, (K_ROWS, half), 1)
            cut = jnp.where(row <= col, s[:, :half], NEGATIVE)
            s = replace_block(s, cut, 0, 1)
        p = jnp.exp(s)
        ds = (p * dp).astype(BF)
        pb = p.astype(BF)
        dv = lax.dot_general(
            pb, do[first:], (((1,), (0,)), ((), ())), preferred_element_type=F32
        )
        dk = lax.dot_general(ds, q[first:], (((1,), (0,)), ((), ())), preferred_element_type=F32)
        dq = lax.dot_general(keys, ds, (((0,), (0,)), ((), ())), preferred_element_type=F32)
        return dk, dv, dq

    done = []
    ahead = [scores(t) for t in tasks[:AHEAD]]
    for i, task in enumerate(tasks):
        if i + AHEAD < len(tasks):
            ahead.append(scores(tasks[i + AHEAD]))
        done.append(finish(task, ahead[i]))
    dk = jnp.concatenate([d[0] for d in done], axis=0)
    dv = jnp.concatenate([d[1] for d in done], axis=0)
    full = sum(d[2] for d, task in zip(done, tasks) if task[5] == 0)
    late = [d[2] for d, task in zip(done, tasks) if task[5] > 0]
    if late:
        full = jnp.concatenate([full[:, :half], full[:, half:] + sum(late)], axis=1)
    return mine, full.T * scale, dk[:size], dv[:size], dk[size:], dv[size:]


MESH = pl.DeviceIdType.MESH


def place():
    core = lax.axis_index("section")
    group = lax.axis_index("dp")
    depth = lax.axis_index("seq")
    return core, group, depth, ((depth + 1) // 2) % 2, depth // 2


def greet(others):
    barrier = pltpu.get_barrier_semaphore()
    for other in others:
        pl.semaphore_signal(barrier, inc=1, device_id=other, device_id_type=MESH)
    pl.semaphore_wait(barrier, len(others))


def row_mates(core, group, depth):
    mates = [(1 - core, group, depth)]
    for step in range(1, 4):
        there = (depth + step) % 4
        mates += [(core, group, there), (1 - core, group, there)]
    return mates


def remote(source, target, send, recv, device):
    return pltpu.make_async_remote_copy(
        src_ref=source,
        dst_ref=target,
        send_sem=send,
        recv_sem=recv,
        device_id=device,
        device_id_type=MESH,
    )


def write_features(seg_ref, target_ref, queries, order, layer, core, depth):
    span = seg_ref.shape[2] // 4
    at = lax.broadcasted_iota(jnp.int32, (PAIR, span), 0)
    at = jnp.where(at >= DH, at - DH, at)
    own_core = core
    for i in range(2 if queries else 4):
        first = pl.multiple_of(order[i] * span, span)
        seg = seg_ref[layer, pl.ds(depth, 1), pl.ds(first, span)]
        seg = jnp.broadcast_to(seg, (PAIR, span))
        if queries:
            value = jnp.where((seg == at) | (at == 4 + i), 1.0, 0.0)
        else:
            bad = (seg != at) & (at < 4)
            value = jnp.where(bad, NEGATIVE, 0.0)
            if layer == 1:
                barred = [0.0, NEGATIVE, NEGATIVE * (1 - own_core).astype(F32), NEGATIVE][i]
                value = jnp.where(at == 4, barred, value)
                if i == 3:
                    value = jnp.where(at == 5, NEGATIVE * own_core.astype(F32), value)
            value = jnp.where((at >= STAT) & (at < STAT + 3), 1.0, value)
        target_ref[layer, i * span : (i + 1) * span, :] = value.T.astype(BF)


def spread_kernel(count, x_ref, seg_ref, *refs):
    weights, (x_out, *outs) = refs[:count], refs[count : 2 * count + 1]
    features = refs[2 * count + 1 : 2 * count + 3]
    refs = refs[2 * count + 3 :]
    x_held, held = refs[0], refs[1 : count + 1]
    x_send, x_recv, x_own, w_send, w_recv, w_own, w_out = refs[count + 1 :]
    core, group, depth, side, at = place()
    span = x_ref.shape[1]
    loads = [pltpu.make_async_copy(weights[i], held[i], w_own.at[i]) for i in range(count)]
    for load in loads:
        load.start()
    x_load = pltpu.make_async_copy(x_ref.at[depth], x_held, x_own)
    x_load.start()
    greet(row_mates(core, group, depth))
    seat = 2 * core + at
    copies = []
    for step in (2, 1, 3, 0):
        row = (depth + step) % 4
        target = x_out.at[core, pl.ds(pl.multiple_of(at * span, span), span)]
        if step == 0:
            there = remote(
                x_held, target, x_send.at[step], x_recv.at[seat], (side, group, row)
            )
            here = pltpu.make_async_copy(x_held, target, x_recv.at[seat])
            x_load.wait()

            @pl.when(side == core)
            def _():
                here.start()

            @pl.when(side != core)
            def _():
                there.start()
        else:
            there = remote(
                x_ref.at[row], target, x_send.at[step], x_recv.at[seat], (side, group, row)
            )
            there.start()
        copies.append((step, there))
    moves = []
    for i in range(count):
        loads[i].wait()
        own = pltpu.make_async_copy(held[i], outs[i].at[core], w_out.at[i])
        gone = remote(
            held[i], outs[i].at[core], w_send.at[i], w_recv.at[i], (1 - core, group, depth)
        )
        gone.start()
        own.start()
        moves.append((own, gone))
    order = [core, 3 - core, 1 - core, 2 + core]
    for layer in range(2):
        write_features(seg_ref, features[0], True, order, layer, core, depth)
        write_features(seg_ref, features[1], False, order, layer, core, depth)
    for own, gone in moves:
        own.wait()
        gone.wait()
    for step, there in copies:
        if step == 0:

            @pl.when(side != core)
            def _():
                there.wait_send()
        else:
            there.wait_send()
    for seat_from in range(4):
        target = x_out.at[seat_from // 2, pl.ds((seat_from % 2) * span, span)]
        pltpu.make_async_copy(x_held, target, x_recv.at[seat_from]).wait()


def spread(tokens, segments, *weights):
    rows, span, width = tokens.shape
    count = len(weights)
    anywhere = pl.BlockSpec(memory_space=pl.ANY)
    resident = pl.BlockSpec(memory_space=pltpu.VMEM)
    dma = pltpu.SemaphoreType.DMA
    out = pl.pallas_call(
        functools.partial(spread_kernel, count),
        in_specs=[anywhere, resident] + [anywhere] * count,
        out_specs=[anywhere] * (count + 1) + [resident] * 2,
        out_shape=[jax.ShapeDtypeStruct((2, 2 * span, width), BF)]
        + [jax.ShapeDtypeStruct((2,) + w.shape, w.dtype) for w in weights]
        + [jax.ShapeDtypeStruct((2, n * span, PAIR), BF) for n in (2, 4)],
        scratch_shapes=[pltpu.VMEM((span, width), BF)]
        + [pltpu.VMEM(w.shape, w.dtype) for w in weights]
        + [dma((4,)), dma((4,)), dma]
        + [dma((count,))] * 4,
        compiler_params=pltpu.CompilerParams(collective_id=0, has_side_effects=True),
        name="spread",
    )(tokens, segments, *weights)
    return out[: count + 1], out[count + 1 :]


class RowRider:
    def __init__(self, rows):
        self.array = rows
        self.shape = (2 * rows.shape[1], rows.shape[2])

    def copies(self, source, target, send, recv):
        core, group, depth, side, at = place()
        span = source.shape[1]
        slot = target.at[pl.ds(pl.multiple_of(at * span, span), span)]
        for i in range(2):
            row = 2 * core + i
            yield (
                remote(source.at[row], slot, send.at[i], recv.at[at], (side, group, row)),
                pltpu.make_async_copy(source.at[row], slot, recv.at[at]),
                (row == depth) & (side == core),
            )

    def arrivals(self, source, target, recv):
        span = source.shape[1]
        for i in range(2):
            slot = target.at[pl.ds(i * span, span)]
            yield pltpu.make_async_copy(source.at[0], slot, recv.at[i])

    def receives(self):
        return None


class HomeRider:
    def __init__(self, result, layer):
        self.array = result
        self.layer = layer
        self.shape = (4, result.shape[0] // 2, result.shape[1])

    def copies(self, source, target, send, recv):
        core, group, depth, side, at = place()
        span = source.shape[0] // 2
        slot = target.at[depth]
        for i in range(2):
            there = 2 * i + (core + i) % 2
            block = source.at[pl.ds(i * span, span)]
            yield (
                remote(block, slot, send.at[i], recv.at[depth], (self.layer, group, there)),
                pltpu.make_async_copy(block, slot, recv.at[depth]),
                (there == depth) & (core == self.layer),
            )

    def arrivals(self, source, target, recv):
        span = source.shape[0] // 2
        for i in range(4):
            yield pltpu.make_async_copy(source.at[pl.ds(0, span)], target.at[i], recv.at[i])

    def receives(self):
        return lax.axis_index("section") == self.layer


def ride_copies(rider, source, target, send, recv):
    for far, near, stays in rider.copies(source, target, send, recv):

        @pl.when(stays)
        def _():
            near.start()

        @pl.when(jnp.logical_not(stays))
        def _():
            far.start()


def ride_end(rider, source, target, send, recv):
    for far, near, stays in rider.copies(source, target, send, recv):

        @pl.when(jnp.logical_not(stays))
        def _():
            far.wait_send()

    def arrive():
        for copy in rider.arrivals(source, target, recv):
            copy.wait()

    if rider.receives() is None:
        arrive()
    else:
        pl.when(rider.receives())(arrive)


RESULT_OF = (0, 1, 0, 1, 2, 3, 2, 3, 4, 5, 6)
Z_FIRST = ()
LAG = 2
HOME_SLOT = 14
LATE = {0: 3, 3: 0, 1: 1, 2: 2}


def gradient_groups(width, hidden):
    folds = hidden // width
    groups = []
    for layer, up, down in ((1, 0, 1), (0, 2, 3)):
        groups.append((layer, [(up, 0, 0, hidden)]))
        groups.append((layer, [(down, i * width, 0, width) for i in range(folds)]))
    groups.append((None, [(8, 0, 0, width), (9, 0, 0, width), (10, 0, 0, 2 * width)]))
    for layer, o, q in ((1, 4, 5), (0, 6, 7)):
        groups.append((layer, [(o, 0, 0, width), (q, 0, 0, 3 * width)]))
    return groups


FAMILIES = ((0, 1), (2, 3), (4,), (5, 6))
CROSS_TABLE = {0: [(0, 0), (1, 0)], 1: [(0, 1), (1, 1)]}
SELF_TABLE = {
    0: [(0, 2), (1, 2), (2, 0), (3, 0)],
    2: [(0, 3), (1, 3), (2, 1), (3, 1)],
    5: [(0, 4), (1, 4)],
}


def wide(groups, chosen):
    return sum(p[3] for g in chosen for p in groups[g][1])


class Plan:
    def __init__(self, width, hidden, spans, made=()):
        self.groups = gradient_groups(width, hidden)
        self.half = width // 2
        self.spans = spans
        self.chosen = [g for f in sorted(spans) for g in FAMILIES[f]]
        self.enter = {g: spans[f][0] for f in spans for g in FAMILIES[f]}
        self.leave = {g: spans[f][1] for f in spans for g in FAMILIES[f]}
        self.final = [g for g in self.chosen if self.leave[g] == 10]
        self.arrays = sorted(
            {p[0] for g in self.chosen if self.enter[g] == 0 for p in self.groups[g][1]} - set(made)
        )
        self.made = made
        self.most = max(len(pieces) for _, pieces in self.groups)

    def columns(self, g, k):
        mates = self.level(k)
        return pl.ds(wide(self.groups, mates[: mates.index(g)]), wide(self.groups, [g]))

    def level(self, k):
        return [g for g in self.chosen if self.enter[g] <= k < min(self.leave[g], 5)]

    def family_columns(self, f, g):
        mates = FAMILIES[f]
        return pl.ds(wide(self.groups, mates[: mates.index(g)]), wide(self.groups, [g]))

    def rows(self, k):
        return self.half >> k

    def states_in(self):
        return [f for f in sorted(self.spans) if self.spans[f][0] > 0]

    def states_out(self):
        return [f for f in sorted(self.spans) if self.spans[f][1] < 10]

    def state_shape(self, f, stage):
        return jax.ShapeDtypeStruct((self.rows(stage - 1), wide(self.groups, FAMILIES[f])), BF)

    def scratch(self):
        dma = pltpu.SemaphoreType.DMA
        number = len(self.chosen)
        shapes = []
        first = self.level(0)
        shapes.append(
            pltpu.VMEM((2 * self.half, wide(self.groups, first)) if first else (16, 128), BF)
        )
        for k in range(5):
            columns = wide(self.groups, self.level(k))
            shapes.append(pltpu.VMEM((self.rows(k), columns or 128), BF))
        total = wide(self.groups, self.final)
        shapes.append(pltpu.VMEM((2 * self.half if total else 16, total or 128), BF))
        shapes += [dma((number, self.most))] * 2 + [dma((number, 1))] * 2 + [dma((number, 10))] * 2
        return shapes

    def count(self):
        return 13


class Reducer:
    def __init__(self, plan, parts, states, left, results, scratch, makers=None):
        self.makers = makers or {}
        self.plan, self.parts, self.results = plan, parts, results
        self.states, self.left = states, left
        self.own, self.got, self.total = scratch[0], scratch[1:6], scratch[6]
        self.own_sem, self.out_sem, self.send0, self.recv0, self.send, self.recv = scratch[7:13]
        self.core, group, depth, _, _ = place()
        core = self.core
        partner = (1 - core, group, depth)
        x_next = group + 1 - 2 * (group % 2)
        y_next = (group + 2) % 4
        first = x_next + core * (y_next - x_next)
        second = y_next + core * (x_next - y_next)
        z_next = depth + 1 - 2 * (depth % 2)
        z_far = (depth + 2) % 4
        self.across = [(core, first, depth), (core, second, depth)]
        along = [(core, group, z_next), (core, group, z_far)]
        bit_x, bit_y = group % 2, group // 2
        across_bits = [bit_x + core * (bit_y - bit_x), bit_y + core * (bit_x - bit_y)]
        along_bits = [depth % 2, depth // 2]
        self.orders = [
            ([partner] + self.across + along, [core] + across_bits + along_bits),
            ([partner] + along + self.across, [core] + along_bits + across_bits),
        ]
        self.first_rows = []
        for _, bits in self.orders:
            held = [core * plan.half]
            for k in range(1, 5):
                held.append(held[-1] + bits[k] * plan.rows(k))
            self.first_rows.append(held)

    def family(self, g):
        return [f for f in range(4) if g in FAMILIES[f]][0]

    def order(self, g):
        return self.orders[1 if g in Z_FIRST else 0]

    def held(self, g, k):
        f = self.family(g)
        if k == self.plan.enter[g] - 1:
            return self.states[f].at[:, self.plan.family_columns(f, g)]
        if k == self.plan.leave[g] - 1:
            return self.left[f].at[:, self.plan.family_columns(f, g)]
        return self.got[k].at[:, self.plan.columns(g, k)]

    def slot(self, g, k):
        return self.got[k].at[:, self.plan.columns(g, k)]

    def rows(self, first, count):
        return pl.ds(pl.multiple_of(first, 16), count)

    def own_rows(self, half):
        count = self.plan.half
        return self.rows(half * count, count)

    def away(self, g):
        index = self.plan.chosen.index(g)
        columns = self.plan.columns(g, 0)
        return remote(
            self.own.at[self.own_rows(1 - self.core), columns],
            self.got[0].at[:, columns],
            self.send0.at[index, 0],
            self.recv0.at[index, 0],
            self.orders[0][0][0],
        )

    def stage(self, g):
        index = self.plan.chosen.index(g)
        column = self.plan.columns(g, 0).start
        for i, (array, row, col, width) in enumerate(self.plan.groups[g][1]):
            if array in self.makers:
                column += width
                continue
            block = self.parts[array].at[pl.ds(row, 2 * self.plan.half), pl.ds(col, width)]
            yield pltpu.make_async_copy(
                block, self.own.at[:, pl.ds(column, width)], self.own_sem.at[index, i]
            )
            column += width

    def make(self, g):
        column = self.plan.columns(g, 0).start
        for array, row, col, width in self.plan.groups[g][1]:
            if array in self.makers:
                tokens, ready, grads, grads_ready = self.makers[array]
                ready()
                grads_ready()
                tile = tokens.shape[1]

                @pl.loop(0, width // tile)
                def _(i):
                    at = pl.multiple_of(i * tile, tile)
                    self.own[:, pl.ds(pl.multiple_of(column + at, tile), tile)] = dot_outer(
                        tokens[...], grads[:, pl.ds(at, tile)]
                    ).astype(BF)

            column += width

    def load(self):
        for g in self.plan.level(0):
            for copy in self.stage(g):
                copy.start()

    def add(self, target, arrived, source, first):
        count, strip = target.shape[0], 16

        @pl.loop(0, count // strip)
        def _(i):
            r = pl.multiple_of(i * strip, strip)
            mine = source[pl.ds(pl.multiple_of(first + r, strip), strip), :]
            target[pl.ds(r, strip), :] = mine + arrived[pl.ds(r, strip), :]

    def halving(self, g, k):
        index = self.plan.chosen.index(g)
        neighbours, bits = self.order(g)
        count = self.plan.rows(k)
        return remote(
            self.held(g, k - 1).at[self.rows((1 - bits[k]) * count, count)],
            self.slot(g, k),
            self.send.at[index, k],
            self.recv.at[index, k],
            neighbours[k],
        )

    def whole(self, g):
        mates = self.plan.final
        return pl.ds(
            wide(self.plan.groups, mates[: mates.index(g)]), wide(self.plan.groups, [g])
        )

    def doubling(self, g, k):
        index = self.plan.chosen.index(g)
        held = self.first_rows[1 if g in Z_FIRST else 0]
        block = self.total.at[self.rows(held[k], self.plan.rows(k)), self.whole(g)]
        return remote(
            block, block, self.send.at[index, 4 + k], self.recv.at[index, 4 + k], self.order(g)[0][k]
        )

    def joining(self, g):
        index = self.plan.chosen.index(g)
        half = self.plan.half
        block = self.total.at[self.rows(self.core * half, half), self.whole(g)]
        return remote(
            block, block, self.send.at[index, 9], self.recv.at[index, 9], self.orders[0][0][0]
        )

    def only(self, layer, there, act):
        if layer is None:
            act()
        else:
            pl.when((self.core == layer) if there else (self.core != layer))(act)

    def emit(self, g, wait):
        index = self.plan.chosen.index(g)
        layer, pieces = self.plan.groups[g]
        column = self.whole(g).start
        for i, (array, row, col, width) in enumerate(pieces):
            copy = pltpu.make_async_copy(
                self.total.at[:, pl.ds(column, width)],
                self.results[RESULT_OF[array]].at[
                    pl.ds(row, 2 * self.plan.half), pl.ds(col, width)
                ],
                self.out_sem.at[index, i],
            )
            column += width
            self.only(layer, True, copy.wait if wait else copy.start)

    def run(self, g, step):
        layer = self.plan.groups[g][0]
        enter, leave = self.plan.enter[g], self.plan.leave[g]
        if enter < step <= 5:
            k = step - 1
            if k == 0:
                self.away(g).wait()
                mine = self.own.at[:, self.plan.columns(g, 0)]
                self.add(self.held(g, 0), self.slot(g, 0), mine, self.core * self.plan.half)
            else:
                self.halving(g, k).wait()
                count = self.plan.rows(k)
                first = self.order(g)[1][k] * count
                self.add(self.held(g, k), self.slot(g, k), self.held(g, k - 1), first)
        if step == leave and leave < 10:
            return
        if step == 0:
            for copy in self.stage(g):
                copy.wait()
            self.make(g)
            self.away(g).start()
        elif step <= 4:
            self.halving(g, step).start()
        elif step == 5:
            held = self.first_rows[1 if g in Z_FIRST else 0]
            self.total[self.rows(held[4], self.plan.rows(4)), self.whole(g)] = self.held(g, 4)[...]
            self.doubling(g, 4).start()
        elif step <= 8:
            self.doubling(g, 10 - step).wait()
            self.doubling(g, 9 - step).start()
        elif step == 9:
            self.doubling(g, 1).wait()
            self.only(layer, False, self.joining(g).start)
        else:
            self.only(layer, False, self.joining(g).wait_send)
            self.only(layer, True, self.joining(g).wait_recv)
            self.emit(g, False)


def tail_slots(plan):
    table = {}
    late = LATE
    for f in sorted(plan.spans):
        for i, g in enumerate(FAMILIES[f]):
            for n, step in enumerate(range(plan.enter[g], 11)):
                table.setdefault(late[f] + i + LAG * n, []).append((g, step))
    return table


def collect_kernel(plan, riders, recipe, *refs):
    count = len(riders)
    homes, refs = refs[:count], refs[count:]
    number = len({i for entry in recipe.values() for i, _ in entry})
    sources, refs = refs[:number], refs[number:]
    parts = dict(zip(plan.arrays, refs))
    refs = refs[len(plan.arrays) :]
    states = dict(zip(plan.states_in(), refs))
    refs = refs[len(states) :]
    small, refs = refs[0], refs[1:]
    home_outs, refs = refs[:count], refs[count:]
    results, small_out, refs = refs[:7], refs[7], refs[8:]
    small_got, home_send, home_recv, small_send, small_recv, source_sem = refs[:6]
    held, refs = refs[6 : 6 + number], refs[6 + number :]
    loads = [
        pltpu.make_async_copy(source, target, source_sem.at[i])
        for i, (source, target) in enumerate(zip(sources, held))
    ]
    waited = set()

    def ready(i):
        def act():
            if i not in waited:
                waited.add(i)
                loads[i].wait()

        return act

    makers = {}
    for array, entry in recipe.items():
        made = []
        for i, layer in entry:
            made += [held[i] if layer is None else held[i].at[layer], ready(i)]
        makers[array] = made
    reducer = Reducer(plan, parts, states, {}, results, refs, makers)
    core, group, depth, _, _ = place()
    for copy in loads:
        copy.start()
    reducer.load()
    greet(row_mates(core, group, depth) + reducer.across)

    def small_copy(k):
        return remote(
            small_out, small_got.at[k], small_send.at[k], small_recv.at[k], reducer.orders[0][0][k]
        )

    def small_step(k):
        if k > 0:
            small_copy(k - 1).wait()
            small_out[...] += small_got[k - 1]
        else:
            small_out[...] = small[...]
        if k < 5:
            small_copy(k).start()

    table = tail_slots(plan)
    for slot in range(max(max(table), 12) + 1):
        for g, step in sorted(reversed(table.get(slot, [])), key=lambda item: item[1] == 0):
            reducer.run(g, step)
        if slot == HOME_SLOT:
            for i, rider in enumerate(riders):
                ride_copies(rider, homes[i], home_outs[i], home_send.at[i], home_recv.at[i])
        if 2 <= slot <= 12 and slot % 2 == 0:
            small_step(slot // 2 - 1)
    for g in plan.chosen:
        reducer.emit(g, True)
    for i, rider in enumerate(riders):
        ride_end(rider, homes[i], home_outs[i], home_send.at[i], home_recv.at[i])


def collect(plan, riders, parts, states, small, products):
    sources = []
    recipe = {}
    for array, entry in products.items():
        recipe[array] = []
        for value, layer in entry:
            at = [i for i, known in enumerate(sources) if known is value]
            if not at:
                at = [len(sources)]
                sources.append(value)
            recipe[array].append((at[0], layer))
    count = len(riders)
    width = riders[0].array.shape[1]
    hidden = 4 * width
    anywhere = pl.BlockSpec(memory_space=pl.ANY)
    resident = pl.BlockSpec(memory_space=pltpu.VMEM)
    dma = pltpu.SemaphoreType.DMA
    shapes = [
        (width, hidden), (hidden, width), (width, width), (width, 3 * width),
        (width, width), (width, width), (width, 2 * width),
    ]
    out = pl.pallas_call(
        functools.partial(collect_kernel, plan, riders, recipe),
        in_specs=[resident] * count
        + [anywhere] * (len(sources) + len(plan.arrays))
        + [resident] * (len(plan.states_in()) + 1),
        out_specs=[anywhere] * (count + 7) + [resident],
        out_shape=[jax.ShapeDtypeStruct(rider.shape, BF) for rider in riders]
        + [jax.ShapeDtypeStruct(s, BF) for s in shapes]
        + [jax.ShapeDtypeStruct(small.shape, F32)],
        scratch_shapes=[
            pltpu.VMEM((5,) + small.shape, F32),
            dma((count, 2)),
            dma((count, 4)),
            dma((5,)),
            dma((5,)),
            dma((len(sources),)),
        ]
        + [pltpu.VMEM(v.shape, v.dtype) for v in sources]
        + plan.scratch(),
        compiler_params=pltpu.CompilerParams(
            collective_id=1, has_side_effects=True, vmem_limit_bytes=56 << 20
        ),
        name="collect",
    )(
        *[rider.array for rider in riders],
        *sources,
        *[parts[a] for a in plan.arrays],
        *[states[f] for f in plan.states_in()],
        small,
    )
    return out[:count], out[count : count + 7], out[count + 7]


def key_loads(offsets, source, staged, sem, layer, step):
    for t in range(2):
        first = pl.multiple_of((offsets[t] + step) * PAIR, PAIR)
        yield pltpu.make_async_copy(
            source.at[layer, :, pl.ds(first, PAIR)], staged.at[layer, step, t], sem.at[layer, step, t]
        )


def key_copies(staged, held, send, recv, layer, step):
    core, group, depth, _, _ = place()
    return [
        remote(
            staged.at[layer, step, t],
            held.at[layer, step, t],
            send.at[layer, step, t],
            recv.at[layer, step, t],
            (1 - core, group, depth),
        )
        for t in range(2)
    ]


def attend_steps(layers):
    return [(layer, step) for layer in range(layers) for step in range(4)]


def begin(layers, offsets, riders, ride, source, keys, reducer=None):
    staged, sem, held, send, recv = keys
    core, group, depth, _, _ = place()
    for layer, step in attend_steps(layers):
        for copy in key_loads(offsets, source, staged, sem, layer, step):
            copy.start()
    if reducer is not None:
        reducer.load()
    mates = row_mates(core, group, depth) if riders or reducer else [(1 - core, group, depth)]
    greet(mates + (reducer.across if reducer else []))
    for layer, step in attend_steps(layers):
        for copy in key_loads(offsets, source, staged, sem, layer, step):
            copy.wait()
        for copy in key_copies(staged, held, send, recv, layer, step):
            copy.start()
    for i, rider in enumerate(riders):
        ride_copies(rider, *[r[i] if j < 2 else r.at[i] for j, r in enumerate(ride)])


def end(layers, riders, ride, keys):
    staged, sem, held, send, recv = keys
    for layer, step in attend_steps(layers):
        for copy in key_copies(staged, held, send, recv, layer, step):
            copy.wait_send()
    for i, rider in enumerate(riders):
        ride_end(rider, *[r[i] if j < 2 else r.at[i] for j, r in enumerate(ride)])


def by_layer(causal, layer, act):
    for kind in sorted(set(causal)):
        if len(set(causal)) == 1:
            act(kind)
        else:
            pl.when(layer == causal.index(kind))(functools.partial(act, kind))


def attend_kernel(causal, offsets, riders, *refs):
    layers, count = len(causal), len(riders)
    q_ref, k_ref, v_ref, kv_ref, qf_ref, kf_ref = refs[:6]
    o_ref, of_ref, lse_ref = refs[6 + count : 9 + count]
    *keys, ride_send, ride_recv = refs[9 + 2 * count :]
    staged, _, held, send, recv = keys
    ride = (refs[6 : 6 + count], refs[9 + count : 9 + 2 * count], ride_send, ride_recv)
    layer, step = pl.program_id(0), pl.program_id(1)

    @pl.when((layer == 0) & (step == 0))
    def _():
        begin(layers, offsets, riders, ride, kv_ref, keys)

    for copy in key_copies(staged, held, send, recv, layer, step):
        copy.wait_recv()

    def work(kind):
        whole, stat = attend_pair(
            kind, q_ref[0], k_ref[0], v_ref[0], held[layer, step, 0], held[layer, step, 1],
            qf_ref[0], kf_ref[0],
        )
        o_ref[0] = whole.astype(BF)
        of_ref[0] = whole
        lse_ref[0] = stat

    by_layer(causal, layer, work)

    @pl.when((layer == layers - 1) & (step == 3))
    def _():
        end(layers, riders, ride, keys)


def grad_copies(gone, got, send, recv, layer, step):
    core, group, depth, _, _ = place()
    return [
        remote(
            gone.at[layer, step, t],
            got.at[layer, step, t],
            send.at[layer, step, t],
            recv.at[layer, step, t],
            (1 - core, group, depth),
        )
        for t in range(2)
    ]


def attend_back_kernel(causal, offsets, riders, joined, plan, table, *refs):
    layers, count = len(causal), len(riders)
    q_ref, k_ref, v_ref, kv_ref, qf_ref, kf_ref, o_ref, lse_ref, do_ref = refs[:9]
    sources, refs = refs[9 : 9 + count], refs[9 + count :]
    parts = dict(zip(plan.arrays, refs))
    refs = refs[len(parts) :]
    states = dict(zip(plan.states_in(), refs))
    refs = refs[len(states) :]
    outs = 1 if joined else 2
    dq_ref, dkv_ref, refs = refs[0], refs[outs - 1], refs[outs:]
    left = dict(zip(plan.states_out(), refs))
    refs = refs[len(left) :]
    targets, refs = refs[:count], refs[count:]
    keys, (gone, got, kept, g_send, g_recv) = refs[:5], refs[5:10]
    staged, _, held, send, recv = keys
    scratch, (ride_send, ride_recv) = refs[10:-2], refs[-2:]
    ride = (sources, targets, ride_send, ride_recv)
    layer, step = pl.program_id(0), pl.program_id(1)
    width = 4 * PAIR
    reducer = Reducer(plan, parts, states, left, [], scratch)

    @pl.when((layer == 0) & (step == 0))
    def _():
        begin(layers, offsets, riders, ride, kv_ref, keys, reducer)

    for slot in range(4 * layers):
        moves = table.get(slot, [])
        if moves:

            @pl.when((layer == slot // 4) & (step == slot % 4))
            def _():
                for g, stage in moves:
                    reducer.run(g, stage)

    for copy in key_copies(staged, held, send, recv, layer, step):
        copy.wait_recv()

    def work(kind):
        columns = pl.ds(pl.multiple_of(step * PAIR, PAIR), PAIR)

        @pl.loop(0, 2)
        def _(head):
            mine, dq, dk, dv, dko, dvo = attend_back_head(
                kind, head, q_ref[0], k_ref[0], v_ref[0], held[layer, step, 0],
                held[layer, step, 1], qf_ref[0], kf_ref[0], o_ref[0], lse_ref[0], do_ref[0],
            )
            dq_ref[layer, :, columns] = jnp.where(mine, dq.astype(BF), dq_ref[layer, :, columns])
            kept[layer, step, 0] = jnp.where(mine, dk, kept[layer, step, 0])
            kept[layer, step, 1] = jnp.where(mine, dv, kept[layer, step, 1])
            gone[layer, step, 0] = jnp.where(mine, dko.astype(BF), gone[layer, step, 0])
            gone[layer, step, 1] = jnp.where(mine, dvo.astype(BF), gone[layer, step, 1])

    by_layer(causal, layer, work)
    for copy in grad_copies(gone, got, g_send, g_recv, layer, step):
        copy.start()

    @pl.when((layer == layers - 1) & (step == 3))
    def _():
        for one, at in attend_steps(layers):
            for t, copy in enumerate(grad_copies(gone, got, g_send, g_recv, one, at)):
                copy.wait()
                first = (width if joined else 0) + t * width + at * PAIR
                dkv_ref[one, :, first : first + PAIR] = (
                    kept[one, at, t] + got[one, at, t].astype(F32)
                ).astype(BF)
        for g in plan.chosen:
            reducer.run(g, plan.leave[g])
        end(layers, riders, ride, keys)


def attend_specs(size, offsets, masks):
    def column(at):
        return pl.BlockSpec((1, size, PAIR), lambda l, p: (l, 0, at + p))

    def shared(rows, first):
        return pl.BlockSpec((1, rows, PAIR), lambda l, p: (l + first, 0, 0))

    return (
        [column(at) for at in offsets]
        + [pl.BlockSpec(memory_space=pl.ANY)]
        + [shared(size, masks[0]), shared(2 * size, masks[1])]
    ), column


def key_scratch(layers, size):
    slots = pltpu.VMEM((layers, 4, 2, size, PAIR), BF)
    sems = pltpu.SemaphoreType.DMA((layers, 4, 2))
    return [slots, sems, slots, sems, sems]


def attend_call(
    kernel, name, layers, riders, collective, in_specs, out_specs, out_shape, scratch, flops, args
):
    count = len(riders)
    dma = pltpu.SemaphoreType.DMA
    return pl.pallas_call(
        kernel,
        grid=(layers, 4),
        in_specs=in_specs,
        out_specs=out_specs + [pl.BlockSpec(memory_space=pl.ANY)] * count,
        out_shape=out_shape + [jax.ShapeDtypeStruct(rider.shape, BF) for rider in riders],
        scratch_shapes=scratch + [dma((max(count, 1), 2)), dma((max(count, 1), 4))],
        compiler_params=pltpu.CompilerParams(
            vmem_limit_bytes=56 << 20, collective_id=collective, has_side_effects=True
        ),
        cost_estimate=pl.CostEstimate(flops=flops, bytes_accessed=flops // 512, transcendentals=0),
        name=name,
    )(*args)


def attend_forward(q, kv, offsets, masks, features, causal, riders, collective):
    layers, size = len(causal), q.shape[1]
    width = 4 * PAIR
    in_specs, column = attend_specs(size, offsets, masks)
    dma = pltpu.SemaphoreType.DMA
    return attend_call(
        functools.partial(attend_kernel, causal, offsets[1:], riders),
        "attend_forward",
        layers,
        riders,
        collective,
        in_specs + [pl.BlockSpec(memory_space=pltpu.VMEM)] * len(riders),
        [column(0)] * 3,
        [jax.ShapeDtypeStruct((layers, size, width), t) for t in (BF, F32, F32)],
        key_scratch(layers, size),
        16 * layers * size * size * width,
        (q, kv, kv, kv, *features, *[rider.array for rider in riders]),
    )


def attend_backward(
    q, kv, offsets, masks, features, o, lse, do, causal, riders, collective, joined,
    plan, table, parts, states,
):
    layers, size = len(causal), q.shape[1]
    width = 4 * PAIR
    in_specs, column = attend_specs(size, offsets, masks)
    dma = pltpu.SemaphoreType.DMA
    resident = pl.BlockSpec(memory_space=pltpu.VMEM)
    anywhere = pl.BlockSpec(memory_space=pl.ANY)
    widths = [3 * width] if joined else [width, 2 * width]
    slots = (layers, 4, 2, size, PAIR)
    left = [plan.state_shape(f, plan.spans[f][1]) for f in plan.states_out()]
    return attend_call(
        functools.partial(
            attend_back_kernel, causal, offsets[1:], riders, joined, plan, table
        ),
        "attend_backward",
        layers,
        riders,
        collective,
        in_specs
        + [column(0)] * 3
        + [resident] * len(riders)
        + [anywhere] * len(plan.arrays)
        + [resident] * len(plan.states_in()),
        [resident] * (len(widths) + len(left)),
        [jax.ShapeDtypeStruct((layers, size, w), BF) for w in widths] + left,
        key_scratch(layers, size)
        + [
            pltpu.VMEM(slots, BF),
            pltpu.VMEM(slots, BF),
            pltpu.VMEM(slots, F32),
            dma((layers, 4, 2)),
            dma((layers, 4, 2)),
        ]
        + plan.scratch(),
        40 * layers * size * size * width,
        (
            q, kv, kv, kv, *features, o, lse, do,
            *[rider.array for rider in riders],
            *[parts[a] for a in plan.arrays],
            *[states[f] for f in plan.states_in()],
        ),
    )


def dot(a, b):
    return lax.dot_general(a, b, (((1,), (0,)), ((), ())), preferred_element_type=F32)


def dot_back(a, b):
    return lax.dot_general(a, b, (((1,), (1,)), ((), ())), preferred_element_type=F32)


def dot_outer(a, b):
    return lax.dot_general(a, b, (((0,), (0,)), ((), ())), preferred_element_type=F32)


def each(function, *stacked):
    return jnp.stack([function(*(s[i] for s in stacked)) for i in range(2)])


def widen_kernel(count, *refs):
    sums, homes, refs = refs[:count], refs[count : count + 4], refs[count + 4 :]
    wide, tokens, grads = refs[:count], refs[count], refs[count + 1]
    for source, target in zip(sums, wide):
        target[...] = source[...].astype(F32)
    core = lax.axis_index("section")

    @pl.when(core == 0)
    def _():
        tokens[...] = homes[0][...]
        grads[...] = homes[2][...].astype(F32)

    @pl.when(core != 0)
    def _():
        tokens[...] = homes[1][...]
        grads[...] = homes[3][...].astype(F32)


def widen(sums, homes, steps=8):
    def rows(shape):
        return pl.BlockSpec((shape[0] // steps,) + shape[1:], lambda i: (i, 0))

    homes = [h.reshape(-1, h.shape[-1]) for h in homes]
    shapes = [v.shape for v in sums] + [homes[0].shape] * 2
    types = [F32] * len(sums) + [BF, F32]
    return pl.pallas_call(
        functools.partial(widen_kernel, len(sums)),
        grid=(steps,),
        in_specs=[rows(v.shape) for v in (*sums, *homes)],
        out_specs=[rows(s) for s in shapes],
        out_shape=[jax.ShapeDtypeStruct(s, t) for s, t in zip(shapes, types)],
        name="widen",
    )(*sums, *homes)


def row_shards(
    inputs,
    cotangent,
    qkv_weight,
    out_weight,
    up_weight,
    down_weight,
    norm_gain,
    norm_bias,
    cross_q_weight,
    cross_kv_weight,
    cross_out_weight,
    cross_gain,
    cross_bias,
    source_segments,
    target_segments,
):
    core = lax.axis_index("section")
    depth = lax.axis_index("seq")
    span = inputs.shape[2]
    width = inputs.shape[3]

    segments = jnp.stack([source_segments, target_segments])
    both, features = spread(
        inputs[0],
        segments,
        qkv_weight[0],
        out_weight[0],
        up_weight[0],
        down_weight[0],
        norm_gain[0],
        norm_bias[0],
    )
    x_both, qkv_both, out_both, up_both, down_both, gain_both, bias_both = both
    g_e, g_d = gain_both[0], gain_both[1]
    b_e, b_d = bias_both[0], bias_both[1]
    wu_e, wu_d = up_both[0], up_both[1]
    wd_e, wd_d = down_both[0], down_both[1]

    qkv = lax.dot_general(
        x_both, qkv_both, (((2,), (1,)), ((0,), (0,))), preferred_element_type=F32
    ).astype(BF)
    self_args = ((0, 4, 8), (0, 0), features)
    o, o_wide, lse, cot = attend_forward(
        qkv, qkv, *self_args, (False, True), [RowRider(cotangent)], 2
    )
    cot = cot.astype(F32)
    summed = x_both.astype(F32) + lax.dot_general(
        o, out_both, (((2,), (1,)), ((0,), (0,))), preferred_element_type=F32
    )
    s1, t1 = summed[0], summed[1]

    h_s = layer_norm(s1, g_e[0], b_e[0])
    h_s_low = h_s.astype(BF)
    u_s = dot(h_s_low, wu_e)
    gel_s = gelu_tanh(u_s).astype(BF)
    s2 = h_s + dot(gel_s, wd_e)
    memory = layer_norm(s2, g_e[1], b_e[1]).astype(BF)
    ckv = dot(memory, cross_kv_weight).astype(BF)

    h_t = layer_norm(t1, g_d[0], b_d[0])
    h_t_low = h_t.astype(BF)
    cq = dot(h_t_low, cross_q_weight).astype(BF)
    cross_args = ((0, 0, 4), (1, 0), features)
    o_c, oc_wide, lse_c = attend_forward(cq[None], ckv[None], *cross_args, (False,), [], 3)
    o_c = o_c[0]
    t2 = h_t + dot(o_c, cross_out_weight)
    c_t = layer_norm(t2, cross_gain, cross_bias)
    c_t_low = c_t.astype(BF)
    u_t = dot(c_t_low, wu_d)
    gel_t = gelu_tanh(u_t).astype(BF)
    t3 = c_t + dot(gel_t, wd_d)
    decoded, pull_t3 = jax.vjp(layer_norm, t3, g_d[1], b_d[1])
    decoded = decoded.astype(BF)

    grad_t3, gg_d1, gb_d1 = pull_t3(cot)
    low_t3 = grad_t3.astype(BF)
    gw_down_d = dot_outer(gel_t, low_t3).astype(BF)
    grad_u_t = jax.vjp(gelu_tanh, u_t)[1](dot_back(low_t3, wd_d))[0].astype(BF)
    gw_up_d = dot_outer(c_t_low, grad_u_t).astype(BF)
    grad_c = grad_t3 + dot_back(grad_u_t, wu_d)
    grad_t2, gg_c, gb_c = jax.vjp(layer_norm, t2, cross_gain, cross_bias)[1](grad_c)
    low_t2 = grad_t2.astype(BF)
    grad_o_c = dot_back(low_t2, cross_out_weight).astype(BF)
    hidden = wu_d.shape[1]
    parts = {0: gw_up_d, 1: gw_down_d}
    plan = Plan(width, hidden, {0: (0, 2)})
    grad_cq, grad_ckv, state_d, home_memory, home_decoded = attend_backward(
        cq[None], ckv[None], *cross_args, oc_wide, lse_c, grad_o_c[None], (False,),
        [HomeRider(memory, 0), HomeRider(decoded, 1)], 4, False, plan, CROSS_TABLE, parts, {},
    )
    grad_cq, grad_ckv = grad_cq[0], grad_ckv[0]
    grad_h = grad_t2 + dot_back(grad_cq, cross_q_weight)
    grad_t1, gg_d0, gb_d0 = jax.vjp(layer_norm, t1, g_d[0], b_d[0])[1](grad_h)
    low_t1 = grad_t1.astype(BF)

    grad_memory = dot_back(grad_ckv, cross_kv_weight).astype(BF).astype(F32)
    grad_s2, gg_e1, gb_e1 = jax.vjp(layer_norm, s2, g_e[1], b_e[1])[1](grad_memory)
    low_s2 = grad_s2.astype(BF)
    gw_down_e = dot_outer(gel_s, low_s2).astype(BF)
    grad_u_s = jax.vjp(gelu_tanh, u_s)[1](dot_back(low_s2, wd_e))[0].astype(BF)
    gw_up_e = dot_outer(h_s_low, grad_u_s).astype(BF)
    grad_h = grad_s2 + dot_back(grad_u_s, wu_e)
    grad_s1, gg_e0, gb_e0 = jax.vjp(layer_norm, s1, g_e[0], b_e[0])[1](grad_h)
    low_s1 = grad_s1.astype(BF)

    low_1 = jnp.stack([low_s1, low_t1])
    grad_o = lax.dot_general(
        low_1, out_both, (((2,), (2,)), ((0,), (0,))), preferred_element_type=F32
    ).astype(BF)
    parts = {2: gw_up_e, 3: gw_down_e}
    plan = Plan(width, hidden, {0: (2, 5), 1: (0, 2)})
    grad_qkv, state_d, state_e = attend_backward(
        qkv, qkv, *self_args, o_wide, lse, grad_o, (False, True), [], 5, True,
        plan, SELF_TABLE, parts, {0: state_d},
    )
    low_cross = low_t2
    products = {
        4: ((o, 1), (low_1, 1)),
        5: ((x_both, 1), (grad_qkv, 1)),
        6: ((o, 0), (low_1, 0)),
        7: ((x_both, 0), (grad_qkv, 0)),
        8: ((o_c, None), (low_cross, None)),
        9: ((h_t_low, None), (grad_cq, None)),
        10: ((memory, None), (grad_ckv, None)),
    }
    grad_x = jnp.stack([grad_s1, grad_t1]) + lax.dot_general(
        grad_qkv, qkv_both, (((2,), (2,)), ((0,), (0,))), preferred_element_type=F32
    )
    grad_x = grad_x.astype(BF)

    small = jnp.stack(
        [gg_e0, gg_e1, gb_e0, gb_e1, gg_d0, gg_d1, gb_d0, gb_d1, gg_c, gb_c]
        + [jnp.zeros_like(gg_c)] * 6
    )
    plan = Plan(width, hidden, {0: (5, 10), 1: (2, 10), 2: (0, 10), 3: (0, 10)}, tuple(products))
    (home_xs, home_xt), sums, small = collect(
        plan,
        [HomeRider(grad_x[0], 0), HomeRider(grad_x[1], 1)],
        {},
        {0: state_d, 1: state_e},
        small,
        products,
    )
    *wide_sums, outputs, grads = widen(sums, [home_memory, home_decoded, home_xs, home_xt])
    g_up, g_down, g_out, g_qkv, g_cross_out, g_cross_q, g_cross_kv = wide_sums
    local = (1, -1) + inputs.shape[2:]
    layer_small = jnp.where(core == 0, small[:4], small[4:8])
    return (
        outputs.reshape(local),
        grads.reshape(local),
        g_qkv[None],
        g_out[None],
        g_up[None],
        g_down[None],
        layer_small[None, :2],
        layer_small[None, 2:],
        g_cross_q,
        g_cross_kv,
        g_cross_out,
        small[8],
        small[9],
    )


def solution(mesh):
    in_specs = (
        P("section", "dp", "seq", None),
        P("dp", "seq", None),
        P("section", None, None),
        P("section", None, None),
        P("section", None, None),
        P("section", None, None),
        P("section", None, None),
        P("section", None, None),
        P(),
        P(),
        P(),
        P(),
        P(),
        P("dp", None),
        P("dp", None),
    )
    out_specs = (
        P("section", "dp", "seq", None),
        P("section", "dp", "seq", None),
        P("section", None, None),
        P("section", None, None),
        P("section", None, None),
        P("section", None, None),
        P("section", None, None),
        P("section", None, None),
        P(),
        P(),
        P(),
        P(),
        P(),
    )
    whole_rows = mesh.shape["section"] == 2 and mesh.shape["seq"] == 4 and mesh.shape["dp"] == 4
    body = row_shards if whole_rows else shards
    return jax.shard_map(body, mesh=mesh, in_specs=in_specs, out_specs=out_specs, check_vma=False)
```

```python
import functools

import jax
import jax.numpy as jnp
from jax import lax
from jax.experimental import pallas as pl
from jax.experimental.pallas import tpu as pltpu
from jax.sharding import PartitionSpec as P

DH = 64
MICRO = 2
MB_ROWS = 2


EPSILON = 1e-05
NEGATIVE = -1e30


def from_behind(value, axis, steps):
    count = lax.axis_size(axis)
    leading, last = (max(0, -steps), min(count, count - steps))
    return lax.ppermute(value, axis, [(source, source + steps) for source in range(leading, last)])


def layer_norm(vector, gain_row, bias_row):
    centre = vector - jnp.mean(vector, axis=-1, keepdims=True)
    spread = jnp.mean(centre * centre, axis=-1, keepdims=True)
    return centre * lax.rsqrt(spread + EPSILON) * gain_row + bias_row


def gelu_tanh(vector):
    return jax.nn.gelu(vector, approximate=True)


def heads_view(vector):
    return vector.reshape(vector.shape[:-1] + (vector.shape[-1] // DH, DH))


def joined_view(vector):
    return vector.reshape(vector.shape[:-2] + (vector.shape[-2] * vector.shape[-1],))


def dense_rows(left_side, right_side):
    return jnp.einsum("rsd,de->rse", left_side, right_side, preferred_element_type=jnp.float32)


def dense_back(left_side, right_side):
    return jnp.einsum("rse,de->rsd", left_side, right_side, preferred_element_type=jnp.float32)


def outer_sum(left_side, right_side):
    return jnp.einsum("rsd,rse->de", left_side, right_side, preferred_element_type=jnp.float32)


def build_mask(query_ids, key_ids, query_places, key_places, causal):
    same_doc = query_ids[:, :, None] == key_ids[:, None, :]
    ordered = (key_places[None, :] <= query_places[:, None]) | jnp.logical_not(causal)
    return same_doc & ordered[None]


def soft_forward(queries, key_rows, value_rows, allowed):
    score_scale = DH ** (-0.5)
    scores = (
        jnp.einsum(
            "rqhe,rkhe->rhqk",
            heads_view(queries),
            heads_view(key_rows),
            preferred_element_type=jnp.float32,
        )
        * score_scale
    )
    scores = jnp.where(allowed[:, None], scores, NEGATIVE)
    highest = jnp.max(scores, axis=-1, keepdims=True)
    exp_terms = jnp.exp(scores - highest)
    totals = jnp.sum(exp_terms, axis=-1, keepdims=True)
    weights = exp_terms / totals
    log_total = (highest + jnp.log(totals))[..., 0]
    mixed_out = jnp.einsum(
        "rhqk,rkhe->rqhe",
        weights.astype(jnp.bfloat16),
        heads_view(value_rows),
        preferred_element_type=jnp.float32,
    )
    return (joined_view(mixed_out), weights, log_total)


def score_grads(grad_mixed, value_rows, weights):
    grad_weights = jnp.einsum(
        "rqhe,rkhe->rhqk",
        heads_view(grad_mixed),
        heads_view(value_rows),
        preferred_element_type=jnp.float32,
    )
    inner_sum = jnp.sum(grad_weights * weights, axis=-1, keepdims=True)
    grad_scores = (weights * (grad_weights - inner_sum)).astype(jnp.bfloat16)
    return (grad_scores, inner_sum[..., 0])


def attend_keys(queries, key_rows, value_rows, query_ids, key_ids, causal):
    span_len = key_rows.shape[1]
    offset = lax.axis_index("seq") * span_len
    whole_keys, whole_values = (
        lax.all_gather(key_rows, "seq", axis=1, tiled=True),
        lax.all_gather(value_rows, "seq", axis=1, tiled=True),
    )
    own_positions = offset + jnp.arange(span_len)
    all_positions = jnp.arange(whole_keys.shape[1])
    own_ids = lax.dynamic_slice_in_dim(query_ids, offset, span_len, 1)
    allowed = build_mask(own_ids, key_ids, own_positions, all_positions, causal)
    mixed_out, weights, log_total = soft_forward(queries, whole_keys, whole_values, allowed)
    kept_state = (
        queries,
        key_rows,
        value_rows,
        whole_keys,
        whole_values,
        weights,
        log_total,
        query_ids,
        key_ids,
        causal,
    )
    return (mixed_out, kept_state)


def attend_back(kept_state, grad_mixed):
    (
        queries,
        key_rows,
        value_rows,
        whole_keys,
        whole_values,
        weights,
        log_total,
        query_ids,
        key_ids,
        causal,
    ) = kept_state
    score_scale = DH ** (-0.5)
    grad_scores, inner_sum = score_grads(grad_mixed, whole_values, weights)
    grad_queries = (
        jnp.einsum(
            "rhqk,rkhe->rqhe",
            grad_scores,
            heads_view(whole_keys),
            preferred_element_type=jnp.float32,
        )
        * score_scale
    )
    part_keys = (
        jnp.einsum(
            "rhqk,rqhe->rkhe", grad_scores, heads_view(queries), preferred_element_type=jnp.float32
        )
        * score_scale
    )
    part_values = jnp.einsum(
        "rhqk,rqhe->rkhe",
        weights.astype(jnp.bfloat16),
        heads_view(grad_mixed),
        preferred_element_type=jnp.float32,
    )
    grad_keys, grad_values = (
        lax.psum_scatter(
            joined_view(part_keys).astype(jnp.bfloat16), "seq", scatter_dimension=1, tiled=True
        ).astype(jnp.float32),
        lax.psum_scatter(
            joined_view(part_values).astype(jnp.bfloat16), "seq", scatter_dimension=1, tiled=True
        ).astype(jnp.float32),
    )
    return (joined_view(grad_queries), grad_keys, grad_values)


def layer_forward(tokens, memory_in, own_ids, source_ids, target_ids, params, decoder):
    (
        qkv_matrix,
        out_matrix,
        up_matrix,
        down_matrix,
        norm_gains,
        norm_biases,
        query_matrix,
        pair_matrix,
        cross_matrix,
        cross_gains,
        cross_shift,
    ) = params
    residual = tokens.astype(jnp.float32)
    packed = dense_rows(tokens, qkv_matrix).astype(jnp.bfloat16)
    queries, key_rows, value_rows = jnp.split(packed, 3, axis=-1)
    mixed_out, self_state = attend_keys(queries, key_rows, value_rows, own_ids, own_ids, decoder)
    mixed_low = mixed_out.astype(jnp.bfloat16)
    first_sum = residual + dense_rows(mixed_low, out_matrix)
    first_norm = layer_norm(first_sum, norm_gains[0], norm_biases[0])
    first_low = first_norm.astype(jnp.bfloat16)
    cross_query = dense_rows(first_low, query_matrix).astype(jnp.bfloat16)
    cross_pair = dense_rows(memory_in, pair_matrix).astype(jnp.bfloat16)
    cross_keys, cross_values = jnp.split(cross_pair, 2, axis=-1)
    cross_mixed, cross_state = attend_keys(
        cross_query, cross_keys, cross_values, target_ids, source_ids, False
    )
    cross_low = cross_mixed.astype(jnp.bfloat16)
    cross_sum = first_norm + dense_rows(cross_low, cross_matrix)
    second = jnp.where(decoder, layer_norm(cross_sum, cross_gains, cross_shift), first_norm)
    second_low = second.astype(jnp.bfloat16)
    upward = dense_rows(second_low, up_matrix)
    gated_low = gelu_tanh(upward).astype(jnp.bfloat16)
    last_sum = second + dense_rows(gated_low, down_matrix)
    output = layer_norm(last_sum, norm_gains[1], norm_biases[1])
    kept_state = (
        tokens,
        self_state,
        mixed_low,
        first_sum,
        first_low,
        cross_state,
        cross_low,
        cross_sum,
        second_low,
        upward,
        gated_low,
        last_sum,
    )
    return (output, kept_state)


def layer_backward(kept_state, grad_out, params, decoder):
    (
        qkv_matrix,
        out_matrix,
        up_matrix,
        down_matrix,
        norm_gains,
        norm_biases,
        query_matrix,
        pair_matrix,
        cross_matrix,
        cross_gains,
        cross_shift,
    ) = params
    (
        tokens,
        self_state,
        mixed_low,
        first_sum,
        first_low,
        cross_state,
        cross_low,
        cross_sum,
        second_low,
        upward,
        gated_low,
        last_sum,
    ) = kept_state
    unused, pull_last = jax.vjp(layer_norm, last_sum, norm_gains[1], norm_biases[1])
    grad_last, grad_gain_last, grad_bias_last = pull_last(grad_out)
    down_in = grad_last.astype(jnp.bfloat16)
    grad_down = outer_sum(gated_low, down_in)
    grad_gated = dense_back(down_in, down_matrix)
    unused, pull_gelu = jax.vjp(gelu_tanh, upward)
    up_in = pull_gelu(grad_gated)[0].astype(jnp.bfloat16)
    grad_up = outer_sum(second_low, up_in)
    grad_second = grad_last + dense_back(up_in, up_matrix)
    unused, pull_cross = jax.vjp(layer_norm, cross_sum, cross_gains, cross_shift)
    grad_cross_sum, grad_cross_gain, grad_cross_bias = pull_cross(
        jnp.where(decoder, grad_second, 0.0)
    )
    grad_first = jnp.where(decoder, grad_cross_sum, grad_second)
    cross_in = grad_cross_sum.astype(jnp.bfloat16)
    grad_cross_out = outer_sum(cross_low, cross_in)
    grad_cross_mixed = dense_back(cross_in, cross_matrix).astype(jnp.bfloat16)
    grad_cross_query, grad_cross_keys, grad_cross_values = attend_back(
        cross_state, grad_cross_mixed
    )
    query_in = grad_cross_query.astype(jnp.bfloat16)
    grad_query_matrix = outer_sum(first_low, query_in)
    grad_first = grad_first + dense_back(query_in, query_matrix)
    pair_in = jnp.concatenate([grad_cross_keys, grad_cross_values], axis=-1).astype(jnp.bfloat16)
    unused, pull_first = jax.vjp(layer_norm, first_sum, norm_gains[0], norm_biases[0])
    grad_first_sum, grad_gain_first, grad_bias_first = pull_first(grad_first)
    out_in = grad_first_sum.astype(jnp.bfloat16)
    grad_out_matrix = outer_sum(mixed_low, out_in)
    grad_mixed = dense_back(out_in, out_matrix).astype(jnp.bfloat16)
    grad_queries, grad_keys, grad_values = attend_back(self_state, grad_mixed)
    qkv_in = jnp.concatenate([grad_queries, grad_keys, grad_values], axis=-1).astype(jnp.bfloat16)
    grad_qkv_matrix = outer_sum(tokens, qkv_in)
    grad_tokens = grad_first_sum + dense_back(qkv_in, qkv_matrix)
    grad_set = (
        grad_qkv_matrix,
        grad_out_matrix,
        grad_up,
        grad_down,
        jnp.stack([grad_gain_first, grad_gain_last]),
        jnp.stack([grad_bias_first, grad_bias_last]),
        grad_query_matrix,
        jnp.zeros(pair_matrix.shape, jnp.float32),
        grad_cross_out,
        grad_cross_gain,
        grad_cross_bias,
    )
    return (grad_tokens, pair_in, grad_set)


def shards(
    inputs,
    cotangent,
    qkv_weight,
    out_weight,
    up_weight,
    down_weight,
    norm_gain,
    norm_bias,
    cross_q_weight,
    cross_kv_weight,
    cross_out_weight,
    cross_gain,
    cross_bias,
    source_segments,
    target_segments,
):
    section_index = lax.axis_index("section")
    decoder = section_index == 1
    params = (
        qkv_weight[0],
        out_weight[0],
        up_weight[0],
        down_weight[0],
        norm_gain[0],
        norm_bias[0],
        cross_q_weight,
        cross_kv_weight,
        cross_out_weight,
        cross_gain,
        cross_bias,
    )
    tokens_all = inputs[0]
    own_all = jnp.where(decoder, target_segments, source_segments)
    span_len = tokens_all.shape[1]
    features = tokens_all.shape[2]
    memory_in = jnp.zeros((MB_ROWS, span_len, features), jnp.bfloat16)
    outputs_all = jnp.zeros(tokens_all.shape, jnp.bfloat16)
    caches = []
    sent_rows = []
    for forward_tick in range(MICRO + 1):
        micro_index = forward_tick - section_index
        active = (micro_index >= 0) & (micro_index < MICRO)
        first_row = jnp.clip(micro_index, 0, MICRO - 1) * MB_ROWS
        rows_now = lax.dynamic_slice_in_dim(tokens_all, first_row, MB_ROWS, 0)
        own_now = lax.dynamic_slice_in_dim(own_all, first_row, MB_ROWS, 0)
        source_now = lax.dynamic_slice_in_dim(source_segments, first_row, MB_ROWS, 0)
        target_now = lax.dynamic_slice_in_dim(target_segments, first_row, MB_ROWS, 0)
        output, kept_state = layer_forward(
            rows_now, memory_in, own_now, source_now, target_now, params, decoder
        )
        output_low = output.astype(jnp.bfloat16)
        current = lax.dynamic_slice_in_dim(outputs_all, first_row, MB_ROWS, 0)
        outputs_all = lax.dynamic_update_slice_in_dim(
            outputs_all, jnp.where(active, output_low, current), first_row, 0
        )
        caches.append(kept_state)
        sent_rows.append(output_low)
        if forward_tick < MICRO:
            memory_in = from_behind(output_low, "section", 1)
    grad_pair_in = jnp.zeros((MB_ROWS, span_len, 2 * features), jnp.bfloat16)
    totals = tuple((jnp.zeros(param_item.shape, jnp.float32) for param_item in params))
    input_all = jnp.zeros(tokens_all.shape, jnp.float32)
    for backward_tick in range(MICRO + 1):
        forward_tick = MICRO - backward_tick
        micro_index = forward_tick - section_index
        active = (micro_index >= 0) & (micro_index < MICRO)
        first_row = jnp.clip(micro_index, 0, MICRO - 1) * MB_ROWS
        cot_now = lax.dynamic_slice_in_dim(cotangent, first_row, MB_ROWS, 0).astype(jnp.float32)
        memory_grad = lax.optimization_barrier(
            dense_back(grad_pair_in, params[7]).astype(jnp.bfloat16)
        ).astype(jnp.float32)
        pair_term = outer_sum(sent_rows[forward_tick], grad_pair_in)
        grad_out = jnp.where(decoder, cot_now, memory_grad)
        grad_tokens, pair_in, grad_set = layer_backward(
            caches[forward_tick], grad_out, params, decoder
        )
        grad_set = grad_set[:7] + (jnp.where(decoder, 0.0, pair_term),) + grad_set[8:]
        totals = jax.tree.map(
            lambda total_sum, new_term: total_sum + jnp.where(active, new_term, 0.0),
            totals,
            grad_set,
        )
        current = lax.dynamic_slice_in_dim(input_all, first_row, MB_ROWS, 0)
        input_all = lax.dynamic_update_slice_in_dim(
            input_all, jnp.where(active, grad_tokens, current), first_row, 0
        )
        if backward_tick < MICRO:
            grad_pair_in = from_behind(pair_in, "section", -1)
    layer_part = lax.psum(
        (totals[0], totals[1], totals[2], totals[3], totals[4], totals[5]), ("dp", "seq")
    )
    cross_part = lax.psum(
        (totals[6], totals[7], totals[8], totals[9], totals[10]), ("section", "dp", "seq")
    )
    return (
        outputs_all[None],
        input_all[None],
        layer_part[0][None],
        layer_part[1][None],
        layer_part[2][None],
        layer_part[3][None],
        layer_part[4][None],
        layer_part[5][None],
        cross_part[0],
        cross_part[1],
        cross_part[2],
        cross_part[3],
        cross_part[4],
    )


BF = jnp.bfloat16
F32 = jnp.float32
AXES = ("section", "dp", "seq")
PAIR = 2 * DH
STAT = 8
Q_ROWS = 256
K_ROWS = 256
AHEAD = 2


def swap(value, move):
    pairs = []
    for core in range(2):
        for group in range(4):
            for depth in range(4):
                to = move(core, group, depth)
                if to is not None:
                    pairs.append(
                        ((core * 4 + group) * 4 + depth, (to[0] * 4 + to[1]) * 4 + to[2])
                    )
    return lax.ppermute(value, AXES, pairs)


def to_core(value):
    return swap(value, lambda core, group, depth: (1 - core, group, depth))


def replace_block(whole, block, at, axis):
    size, count = block.shape[axis], whole.shape[axis]
    parts = [lax.slice_in_dim(whole, 0, at, axis=axis)] if at > 0 else []
    parts.append(block)
    if at + size < count:
        parts.append(lax.slice_in_dim(whole, at + size, count, axis=axis))
    return jnp.concatenate(parts, axis=axis)


def attend_pair(causal, q, k, v, ko, vo, qf, kf):
    size = q.shape[0]
    half = size // 2
    lane = lax.broadcasted_iota(jnp.int32, (size, PAIR), 1)
    low_lanes = lane < DH
    q = q * jnp.array(DH ** (-0.5), BF)
    kf, kfo = kf[:size], kf[size:]
    one = jnp.ones_like(v)
    tasks = []
    for head in range(2):
        mine = low_lanes if head == 0 else jnp.logical_not(low_lanes)
        qa = jnp.where(mine, q, qf)
        ka = [jnp.where(mine, k, kf), jnp.where(mine, ko, kfo)]
        va = [jnp.where(mine, v, one), jnp.where(mine, vo, one)]
        for start in range(0, size, Q_ROWS):
            rows = slice(start, start + Q_ROWS)
            if causal and start < half:
                kk = jnp.concatenate([ka[0][:half], ka[1][:half]], axis=0)
                vv = jnp.concatenate([va[0][:half], va[1][:half]], axis=0)
                diagonal = 0
            else:
                kk = jnp.concatenate(ka, axis=0)
                vv = jnp.concatenate(va, axis=0)
                diagonal = half if causal else None
            tasks.append((qa[rows], kk, vv, diagonal, start % half))

    def scores(task):
        qq, kk, _, _, _ = task
        return lax.dot_general(qq, kk, (((1,), (1,)), ((), ())), preferred_element_type=F32)

    def finish(task, s):
        _, _, vv, diagonal, first = task
        if diagonal is not None:
            row = lax.broadcasted_iota(jnp.int32, (Q_ROWS, half), 0) + first
            col = lax.broadcasted_iota(jnp.int32, (Q_ROWS, half), 1)
            cut = jnp.where(col <= row, s[:, diagonal : diagonal + half], NEGATIVE)
            s = replace_block(s, cut, diagonal, 1)
        top = jnp.max(s, axis=1, keepdims=True)
        p = jnp.exp(s - top).astype(BF)
        o = lax.dot_general(p, vv, (((1,), (0,)), ((), ())), preferred_element_type=F32)
        return o / pltpu.roll(o, DH, 1), top + jnp.log(o)

    done = []
    ahead = [scores(t) for t in tasks[:AHEAD]]
    for i, task in enumerate(tasks):
        if i + AHEAD < len(tasks):
            ahead.append(scores(tasks[i + AHEAD]))
        done.append(finish(task, ahead[i]))
    count = size // Q_ROWS
    outs = [jnp.concatenate([d[0] for d in done[h * count :][:count]], axis=0) for h in range(2)]
    stats = [jnp.concatenate([d[1] for d in done[h * count :][:count]], axis=0) for h in range(2)]
    return jnp.where(low_lanes, outs[0], outs[1]), jnp.where(low_lanes, stats[1], stats[0])


def split3(value):
    a = value.astype(BF)
    rest = value - a.astype(F32)
    b = rest.astype(BF)
    c = (rest - b.astype(F32)).astype(BF)
    return a, b, c


def with_stat(base, value, lane):
    a, b, c = split3(-value)
    at = lane & (DH - 1)
    base = jnp.where(at == STAT, a, base)
    base = jnp.where(at == STAT + 1, b, base)
    return jnp.where(at == STAT + 2, c, base)


def attend_back_head(causal, head, q, k, v, ko, vo, qf, kf, o, lse, do):
    size = q.shape[0]
    half = size // 2
    lane = lax.broadcasted_iota(jnp.int32, (size, PAIR), 1)
    mine = (lane >= head * DH) & (lane < head * DH + DH)
    scale = DH ** (-0.5)
    q = q * jnp.array(scale, BF)
    kf, kfo = kf[:size], kf[size:]
    inner = jnp.sum(jnp.where(mine, do.astype(F32) * o, 0.0), axis=1, keepdims=True)
    dstat = with_stat(jnp.zeros_like(do), jnp.broadcast_to(inner, o.shape), lane)
    qa = jnp.where(mine, q, with_stat(qf, lse, lane))
    da = jnp.where(mine, do, dstat)
    tasks = []
    for own, keys, values, marks in ((True, k, v, kf), (False, ko, vo, kfo)):
        ka = jnp.where(mine, keys, marks)
        va = jnp.where(mine, values, marks)
        for start in range(0, size, K_ROWS):
            rows = slice(start, start + K_ROWS)
            late = causal and start >= half
            first = half if late else 0
            diagonal = (start % half) if causal and own else None
            tasks.append((ka[rows], va[rows], keys[rows], qa[first:], da[first:], first, diagonal))

    def scores(task):
        ka, va, _, qa, da, _, _ = task
        s = lax.dot_general(ka, qa, (((1,), (1,)), ((), ())), preferred_element_type=F32)
        dp = lax.dot_general(va, da, (((1,), (1,)), ((), ())), preferred_element_type=F32)
        return s, dp

    def finish(task, both):
        _, _, keys, _, _, first, diagonal = task
        s, dp = both
        if diagonal is not None:
            row = lax.broadcasted_iota(jnp.int32, (K_ROWS, half), 0) + diagonal
            col = lax.broadcasted_iota(jnp.int32, (K_ROWS, half), 1)
            cut = jnp.where(row <= col, s[:, :half], NEGATIVE)
            s = replace_block(s, cut, 0, 1)
        p = jnp.exp(s)
        ds = (p * dp).astype(BF)
        pb = p.astype(BF)
        dv = lax.dot_general(
            pb, do[first:], (((1,), (0,)), ((), ())), preferred_element_type=F32
        )
        dk = lax.dot_general(ds, q[first:], (((1,), (0,)), ((), ())), preferred_element_type=F32)
        dq = lax.dot_general(keys, ds, (((0,), (0,)), ((), ())), preferred_element_type=F32)
        return dk, dv, dq

    done = []
    ahead = [scores(t) for t in tasks[:AHEAD]]
    for i, task in enumerate(tasks):
        if i + AHEAD < len(tasks):
            ahead.append(scores(tasks[i + AHEAD]))
        done.append(finish(task, ahead[i]))
    dk = jnp.concatenate([d[0] for d in done], axis=0)
    dv = jnp.concatenate([d[1] for d in done], axis=0)
    full = sum(d[2] for d, task in zip(done, tasks) if task[5] == 0)
    late = [d[2] for d, task in zip(done, tasks) if task[5] > 0]
    if late:
        full = jnp.concatenate([full[:, :half], full[:, half:] + sum(late)], axis=1)
    return mine, full.T * scale, dk[:size], dv[:size], dk[size:], dv[size:]


MESH = pl.DeviceIdType.MESH


def place():
    core = lax.axis_index("section")
    group = lax.axis_index("dp")
    depth = lax.axis_index("seq")
    return core, group, depth, ((depth + 1) // 2) % 2, depth // 2


def greet(others):
    barrier = pltpu.get_barrier_semaphore()
    for other in others:
        pl.semaphore_signal(barrier, inc=1, device_id=other, device_id_type=MESH)
    pl.semaphore_wait(barrier, len(others))


def row_mates(core, group, depth):
    mates = [(1 - core, group, depth)]
    for step in range(1, 4):
        there = (depth + step) % 4
        mates += [(core, group, there), (1 - core, group, there)]
    return mates


def remote(source, target, send, recv, device):
    return pltpu.make_async_remote_copy(
        src_ref=source,
        dst_ref=target,
        send_sem=send,
        recv_sem=recv,
        device_id=device,
        device_id_type=MESH,
    )


def write_features(seg_ref, target_ref, queries, order, layer, core, depth):
    span = seg_ref.shape[1] // 4
    at = lax.broadcasted_iota(jnp.int32, (PAIR, span), 0)
    at = jnp.where(at >= DH, at - DH, at)
    own_core = core
    for i in range(2 if queries else 4):
        first = pl.multiple_of(order[i] * span, span)
        seg = seg_ref[pl.ds(depth, 1), pl.ds(first, span)]
        seg = jnp.broadcast_to(seg, (PAIR, span))
        if queries:
            value = jnp.where((seg == at) | (at == 4 + i), 1.0, 0.0)
        else:
            bad = (seg != at) & (at < 4)
            value = jnp.where(bad, NEGATIVE, 0.0)
            if layer == 1:
                barred = [0.0, NEGATIVE, NEGATIVE * (1 - own_core).astype(F32), NEGATIVE][i]
                value = jnp.where(at == 4, barred, value)
                if i == 3:
                    value = jnp.where(at == 5, NEGATIVE * own_core.astype(F32), value)
            value = jnp.where((at >= STAT) & (at < STAT + 3), 1.0, value)
        target_ref[layer, i * span : (i + 1) * span, :] = value.T.astype(BF)


def spread_kernel(count, x_ref, source_seg, target_seg, *refs):
    weights, (x_out, qkv_out, *outs) = refs[:count], refs[count : 2 * count + 2]
    features = refs[2 * count + 2 : 2 * count + 4]
    refs = refs[2 * count + 4 :]
    x_held, x_got, w_both, qkv_got, *held = refs[: count + 3]
    x_send, x_recv, x_own, x_home, qkv_home, w_send, w_recv, w_own, w_out = refs[count + 3 :]
    core, group, depth, side, at = place()
    span = x_ref.shape[1]
    holders = [w_both.at[core]] + held
    loads = [pltpu.make_async_copy(weights[i], holders[i], w_own.at[i]) for i in range(count)]
    for load in loads:
        load.start()
    x_load = pltpu.make_async_copy(x_ref.at[depth], x_held, x_own)
    x_load.start()
    greet(row_mates(core, group, depth))
    seat = 2 * core + at
    copies = []
    for step in (2, 1, 3, 0):
        row = (depth + step) % 4
        target = x_got.at[core, pl.ds(pl.multiple_of(at * span, span), span)]
        if step == 0:
            there = remote(
                x_held, target, x_send.at[step], x_recv.at[seat], (side, group, row)
            )
            here = pltpu.make_async_copy(x_held, target, x_recv.at[seat])
            x_load.wait()

            @pl.when(side == core)
            def _():
                here.start()

            @pl.when(side != core)
            def _():
                there.start()
        else:
            there = remote(
                x_ref.at[row], target, x_send.at[step], x_recv.at[seat], (side, group, row)
            )
            there.start()
        copies.append((step, there))
    moves = []
    for i in range(count):
        loads[i].wait()
        landing = w_both.at[core] if i == 0 else outs[i].at[core]
        gone = remote(
            holders[i], landing, w_send.at[i], w_recv.at[i], (1 - core, group, depth)
        )
        gone.start()
        if i > 0:
            own = pltpu.make_async_copy(held[i - 1], outs[i].at[core], w_out.at[i])
            own.start()
            moves.append(own)
        moves.append(gone)
    order = [core, 3 - core, 1 - core, 2 + core]
    for layer, seg_ref in enumerate((source_seg, target_seg)):
        write_features(seg_ref, features[0], True, order, layer, core, depth)
        write_features(seg_ref, features[1], False, order, layer, core, depth)
    for move in moves:
        move.wait()
    own = pltpu.make_async_copy(w_both, outs[0], w_out.at[0])
    own.start()
    local = [own]
    for step, there in copies:
        if step == 0:

            @pl.when(side != core)
            def _():
                there.wait_send()
        else:
            there.wait_send()
    tile = x_ref.shape[2]
    for seat_from in range(4):
        layer = seat_from // 2
        rows = pl.ds((seat_from % 2) * span, span)
        block = x_got.at[layer, rows]
        pltpu.make_async_copy(x_held, block, x_recv.at[seat_from]).wait()
        local.append(pltpu.make_async_copy(block, x_out.at[layer, rows], x_home.at[seat_from]))
        local[-1].start()

        @pl.loop(0, 3)
        def _(i):
            columns = pl.ds(pl.multiple_of(i * tile, tile), tile)
            qkv_got[layer, rows, columns] = dot(
                x_got[layer, rows, :], w_both[layer, :, columns]
            ).astype(BF)

        local.append(
            pltpu.make_async_copy(
                qkv_got.at[layer, rows], qkv_out.at[layer, rows], qkv_home.at[seat_from]
            )
        )
        local[-1].start()
    for copy in local:
        copy.wait()


def spread(tokens, source_segments, target_segments, *weights):
    rows, span, width = tokens.shape
    count = len(weights)
    anywhere = pl.BlockSpec(memory_space=pl.ANY)
    resident = pl.BlockSpec(memory_space=pltpu.VMEM)
    dma = pltpu.SemaphoreType.DMA
    out = pl.pallas_call(
        functools.partial(spread_kernel, count),
        in_specs=[anywhere, resident, resident] + [anywhere] * count,
        out_specs=[anywhere] * (count + 2) + [resident] * 2,
        out_shape=[
            jax.ShapeDtypeStruct((2, 2 * span, width), BF),
            jax.ShapeDtypeStruct((2, 2 * span, 3 * width), BF),
        ]
        + [jax.ShapeDtypeStruct((2,) + w.shape, w.dtype) for w in weights]
        + [jax.ShapeDtypeStruct((2, n * span, PAIR), BF) for n in (2, 4)],
        scratch_shapes=[
            pltpu.VMEM((span, width), BF),
            pltpu.VMEM((2, 2 * span, width), BF),
            pltpu.VMEM((2,) + weights[0].shape, BF),
            pltpu.VMEM((2, 2 * span, 3 * width), BF),
        ]
        + [pltpu.VMEM(w.shape, w.dtype) for w in weights[1:]]
        + [dma((4,)), dma((4,)), dma, dma((4,)), dma((4,))]
        + [dma((count,))] * 4,
        compiler_params=pltpu.CompilerParams(
            collective_id=0, has_side_effects=True, vmem_limit_bytes=60 << 20
        ),
        name="spread",
    )(tokens, source_segments, target_segments, *weights)
    return out[0], out[1], out[2 : count + 2], out[count + 2 :]


class RowRider:
    def __init__(self, rows):
        self.array = rows
        self.shape = (2 * rows.shape[1], rows.shape[2])

    def copies(self, source, target, send, recv):
        core, group, depth, side, at = place()
        span = source.shape[1]
        slot = target.at[pl.ds(pl.multiple_of(at * span, span), span)]
        for i in range(2):
            row = 2 * core + i
            yield (
                remote(source.at[row], slot, send.at[i], recv.at[at], (side, group, row)),
                pltpu.make_async_copy(source.at[row], slot, recv.at[at]),
                (row == depth) & (side == core),
            )

    def arrivals(self, source, target, recv):
        span = source.shape[1]
        for i in range(2):
            slot = target.at[pl.ds(i * span, span)]
            yield pltpu.make_async_copy(source.at[0], slot, recv.at[i])

    def receives(self):
        return None


class HomeRider:
    def __init__(self, result, layer):
        self.array = result
        self.layer = layer
        self.shape = (4, result.shape[0] // 2, result.shape[1])

    def copies(self, source, target, send, recv):
        core, group, depth, side, at = place()
        span = source.shape[0] // 2
        slot = target.at[depth]
        for i in range(2):
            there = 2 * i + (core + i) % 2
            block = source.at[pl.ds(i * span, span)]
            yield (
                remote(block, slot, send.at[i], recv.at[depth], (self.layer, group, there)),
                pltpu.make_async_copy(block, slot, recv.at[depth]),
                (there == depth) & (core == self.layer),
            )

    def arrivals(self, source, target, recv):
        span = source.shape[0] // 2
        for i in range(4):
            yield pltpu.make_async_copy(source.at[pl.ds(0, span)], target.at[i], recv.at[i])

    def receives(self):
        return lax.axis_index("section") == self.layer


def ride_copies(rider, source, target, send, recv):
    for far, near, stays in rider.copies(source, target, send, recv):

        @pl.when(stays)
        def _():
            near.start()

        @pl.when(jnp.logical_not(stays))
        def _():
            far.start()


def ride_end(rider, source, target, send, recv):
    for far, near, stays in rider.copies(source, target, send, recv):

        @pl.when(jnp.logical_not(stays))
        def _():
            far.wait_send()

    def arrive():
        for copy in rider.arrivals(source, target, recv):
            copy.wait()

    if rider.receives() is None:
        arrive()
    else:
        pl.when(rider.receives())(arrive)


RESULT_OF = (0, 1, 0, 1, 2, 3, 2, 3, 4, 5, 6)
Z_FIRST = ()
LAG = 2
HOME_SLOT = 14
LATE = {0: 3, 3: 0, 1: 1, 2: 2}


def gradient_groups(width, hidden):
    folds = hidden // width
    groups = []
    for layer, up, down in ((1, 0, 1), (0, 2, 3)):
        groups.append((layer, [(up, 0, 0, hidden)]))
        groups.append((layer, [(down, i * width, 0, width) for i in range(folds)]))
    groups.append((None, [(8, 0, 0, width), (9, 0, 0, width), (10, 0, 0, 2 * width)]))
    for layer, o, q in ((1, 4, 5), (0, 6, 7)):
        groups.append((layer, [(o, 0, 0, width), (q, 0, 0, 3 * width)]))
    return groups


FAMILIES = ((0, 1), (2, 3), (4,), (5, 6))
CROSS_TABLE = {0: [(0, 0), (1, 0)], 1: [(0, 1), (1, 1)]}
SELF_TABLE = {
    0: [(0, 2), (1, 2), (2, 0), (3, 0)],
    2: [(0, 3), (1, 3), (2, 1), (3, 1)],
    5: [(0, 4), (1, 4)],
}


def wide(groups, chosen):
    return sum(p[3] for g in chosen for p in groups[g][1])


class Plan:
    def __init__(self, width, hidden, spans, made=()):
        self.groups = gradient_groups(width, hidden)
        self.half = width // 2
        self.spans = spans
        self.chosen = [g for f in sorted(spans) for g in FAMILIES[f]]
        self.enter = {g: spans[f][0] for f in spans for g in FAMILIES[f]}
        self.leave = {g: spans[f][1] for f in spans for g in FAMILIES[f]}
        self.final = [g for g in self.chosen if self.leave[g] == 10]
        self.arrays = sorted(
            {p[0] for g in self.chosen if self.enter[g] == 0 for p in self.groups[g][1]} - set(made)
        )
        self.made = made
        self.most = max(len(pieces) for _, pieces in self.groups)

    def columns(self, g, k):
        mates = self.level(k)
        return pl.ds(wide(self.groups, mates[: mates.index(g)]), wide(self.groups, [g]))

    def level(self, k):
        return [g for g in self.chosen if self.enter[g] <= k < min(self.leave[g], 5)]

    def family_columns(self, f, g):
        mates = FAMILIES[f]
        return pl.ds(wide(self.groups, mates[: mates.index(g)]), wide(self.groups, [g]))

    def rows(self, k):
        return self.half >> k

    def states_in(self):
        return [f for f in sorted(self.spans) if self.spans[f][0] > 0]

    def states_out(self):
        return [f for f in sorted(self.spans) if self.spans[f][1] < 10]

    def state_shape(self, f, stage):
        return jax.ShapeDtypeStruct((self.rows(stage - 1), wide(self.groups, FAMILIES[f])), BF)

    def scratch(self):
        dma = pltpu.SemaphoreType.DMA
        number = len(self.chosen)
        shapes = []
        first = self.level(0)
        shapes.append(
            pltpu.VMEM((2 * self.half, wide(self.groups, first)) if first else (16, 128), BF)
        )
        for k in range(5):
            columns = wide(self.groups, self.level(k))
            shapes.append(pltpu.VMEM((self.rows(k), columns or 128), BF))
        total = wide(self.groups, self.final)
        shapes.append(pltpu.VMEM((2 * self.half if total else 16, total or 128), BF))
        shapes += [dma((number, self.most))] * 2 + [dma((number, 1))] * 2 + [dma((number, 10))] * 2
        return shapes

    def count(self):
        return 13


class Reducer:
    def __init__(self, plan, parts, states, left, results, scratch, makers=None):
        self.makers = makers or {}
        self.plan, self.parts, self.results = plan, parts, results
        self.states, self.left = states, left
        self.own, self.got, self.total = scratch[0], scratch[1:6], scratch[6]
        self.own_sem, self.out_sem, self.send0, self.recv0, self.send, self.recv = scratch[7:13]
        self.core, group, depth, _, _ = place()
        core = self.core
        partner = (1 - core, group, depth)
        x_next = group + 1 - 2 * (group % 2)
        y_next = (group + 2) % 4
        first = x_next + core * (y_next - x_next)
        second = y_next + core * (x_next - y_next)
        z_next = depth + 1 - 2 * (depth % 2)
        z_far = (depth + 2) % 4
        self.across = [(core, first, depth), (core, second, depth)]
        along = [(core, group, z_next), (core, group, z_far)]
        bit_x, bit_y = group % 2, group // 2
        across_bits = [bit_x + core * (bit_y - bit_x), bit_y + core * (bit_x - bit_y)]
        along_bits = [depth % 2, depth // 2]
        self.orders = [
            ([partner] + self.across + along, [core] + across_bits + along_bits),
            ([partner] + along + self.across, [core] + along_bits + across_bits),
        ]
        self.first_rows = []
        for _, bits in self.orders:
            held = [core * plan.half]
            for k in range(1, 5):
                held.append(held[-1] + bits[k] * plan.rows(k))
            self.first_rows.append(held)

    def family(self, g):
        return [f for f in range(4) if g in FAMILIES[f]][0]

    def order(self, g):
        return self.orders[1 if g in Z_FIRST else 0]

    def held(self, g, k):
        f = self.family(g)
        if k == self.plan.enter[g] - 1:
            return self.states[f].at[:, self.plan.family_columns(f, g)]
        if k == self.plan.leave[g] - 1:
            return self.left[f].at[:, self.plan.family_columns(f, g)]
        return self.got[k].at[:, self.plan.columns(g, k)]

    def slot(self, g, k):
        return self.got[k].at[:, self.plan.columns(g, k)]

    def rows(self, first, count):
        return pl.ds(pl.multiple_of(first, 16), count)

    def own_rows(self, half):
        count = self.plan.half
        return self.rows(half * count, count)

    def away(self, g):
        index = self.plan.chosen.index(g)
        columns = self.plan.columns(g, 0)
        return remote(
            self.own.at[self.own_rows(1 - self.core), columns],
            self.got[0].at[:, columns],
            self.send0.at[index, 0],
            self.recv0.at[index, 0],
            self.orders[0][0][0],
        )

    def stage(self, g):
        index = self.plan.chosen.index(g)
        column = self.plan.columns(g, 0).start
        for i, (array, row, col, width) in enumerate(self.plan.groups[g][1]):
            if array in self.makers:
                column += width
                continue
            block = self.parts[array].at[pl.ds(row, 2 * self.plan.half), pl.ds(col, width)]
            yield pltpu.make_async_copy(
                block, self.own.at[:, pl.ds(column, width)], self.own_sem.at[index, i]
            )
            column += width

    def make(self, g):
        column = self.plan.columns(g, 0).start
        for array, row, col, width in self.plan.groups[g][1]:
            if array in self.makers:
                tokens, ready, grads, grads_ready = self.makers[array]
                ready()
                grads_ready()
                tile = tokens.shape[1]

                @pl.loop(0, width // tile)
                def _(i):
                    at = pl.multiple_of(i * tile, tile)
                    self.own[:, pl.ds(pl.multiple_of(column + at, tile), tile)] = dot_outer(
                        tokens[...], grads[:, pl.ds(at, tile)]
                    ).astype(BF)

            column += width

    def load(self):
        for g in self.plan.level(0):
            for copy in self.stage(g):
                copy.start()

    def add(self, target, arrived, source, first):
        count, strip = target.shape[0], 16

        @pl.loop(0, count // strip)
        def _(i):
            r = pl.multiple_of(i * strip, strip)
            mine = source[pl.ds(pl.multiple_of(first + r, strip), strip), :]
            target[pl.ds(r, strip), :] = mine + arrived[pl.ds(r, strip), :]

    def halving(self, g, k):
        index = self.plan.chosen.index(g)
        neighbours, bits = self.order(g)
        count = self.plan.rows(k)
        return remote(
            self.held(g, k - 1).at[self.rows((1 - bits[k]) * count, count)],
            self.slot(g, k),
            self.send.at[index, k],
            self.recv.at[index, k],
            neighbours[k],
        )

    def whole(self, g):
        mates = self.plan.final
        return pl.ds(
            wide(self.plan.groups, mates[: mates.index(g)]), wide(self.plan.groups, [g])
        )

    def doubling(self, g, k):
        index = self.plan.chosen.index(g)
        held = self.first_rows[1 if g in Z_FIRST else 0]
        block = self.total.at[self.rows(held[k], self.plan.rows(k)), self.whole(g)]
        return remote(
            block, block, self.send.at[index, 4 + k], self.recv.at[index, 4 + k], self.order(g)[0][k]
        )

    def joining(self, g):
        index = self.plan.chosen.index(g)
        half = self.plan.half
        block = self.total.at[self.rows(self.core * half, half), self.whole(g)]
        return remote(
            block, block, self.send.at[index, 9], self.recv.at[index, 9], self.orders[0][0][0]
        )

    def only(self, layer, there, act):
        if layer is None:
            act()
        else:
            pl.when((self.core == layer) if there else (self.core != layer))(act)

    def emit(self, g, wait):
        index = self.plan.chosen.index(g)
        layer, pieces = self.plan.groups[g]
        column = self.whole(g).start
        for i, (array, row, col, width) in enumerate(pieces):
            copy = pltpu.make_async_copy(
                self.total.at[:, pl.ds(column, width)],
                self.results[RESULT_OF[array]].at[
                    pl.ds(row, 2 * self.plan.half), pl.ds(col, width)
                ],
                self.out_sem.at[index, i],
            )
            column += width
            self.only(layer, True, copy.wait if wait else copy.start)

    def run(self, g, step):
        layer = self.plan.groups[g][0]
        enter, leave = self.plan.enter[g], self.plan.leave[g]
        if enter < step <= 5:
            k = step - 1
            if k == 0:
                self.away(g).wait()
                mine = self.own.at[:, self.plan.columns(g, 0)]
                self.add(self.held(g, 0), self.slot(g, 0), mine, self.core * self.plan.half)
            else:
                self.halving(g, k).wait()
                count = self.plan.rows(k)
                first = self.order(g)[1][k] * count
                self.add(self.held(g, k), self.slot(g, k), self.held(g, k - 1), first)
        if step == leave and leave < 10:
            return
        if step == 0:
            for copy in self.stage(g):
                copy.wait()
            self.make(g)
            self.away(g).start()
        elif step <= 4:
            self.halving(g, step).start()
        elif step == 5:
            held = self.first_rows[1 if g in Z_FIRST else 0]
            self.total[self.rows(held[4], self.plan.rows(4)), self.whole(g)] = self.held(g, 4)[...]
            self.doubling(g, 4).start()
        elif step <= 8:
            self.doubling(g, 10 - step).wait()
            self.doubling(g, 9 - step).start()
        elif step == 9:
            self.doubling(g, 1).wait()
            self.only(layer, False, self.joining(g).start)
        else:
            self.only(layer, False, self.joining(g).wait_send)
            self.only(layer, True, self.joining(g).wait_recv)
            self.emit(g, False)


def tail_slots(plan):
    table = {}
    late = LATE
    for f in sorted(plan.spans):
        for i, g in enumerate(FAMILIES[f]):
            for n, step in enumerate(range(plan.enter[g], 11)):
                table.setdefault(late[f] + i + LAG * n, []).append((g, step))
    return table


def collect_kernel(plan, riders, recipe, *refs):
    count = len(riders)
    homes, refs = refs[:count], refs[count:]
    number = len({i for entry in recipe.values() for i, _ in entry})
    sources, refs = refs[:number], refs[number:]
    parts = dict(zip(plan.arrays, refs))
    refs = refs[len(plan.arrays) :]
    states = dict(zip(plan.states_in(), refs))
    refs = refs[len(states) :]
    small, refs = refs[0], refs[1:]
    home_outs, refs = refs[:count], refs[count:]
    results, small_out, refs = refs[:7], refs[7], refs[8:]
    small_got, home_send, home_recv, small_send, small_recv, source_sem = refs[:6]
    held, refs = refs[6 : 6 + number], refs[6 + number :]
    loads = [
        pltpu.make_async_copy(source, target, source_sem.at[i])
        for i, (source, target) in enumerate(zip(sources, held))
    ]
    waited = set()

    def ready(i):
        def act():
            if i not in waited:
                waited.add(i)
                loads[i].wait()

        return act

    makers = {}
    for array, entry in recipe.items():
        made = []
        for i, layer in entry:
            made += [held[i] if layer is None else held[i].at[layer], ready(i)]
        makers[array] = made
    reducer = Reducer(plan, parts, states, {}, results, refs, makers)
    core, group, depth, _, _ = place()
    for copy in loads:
        copy.start()
    reducer.load()
    greet(row_mates(core, group, depth) + reducer.across)

    def small_copy(k):
        return remote(
            small_out, small_got.at[k], small_send.at[k], small_recv.at[k], reducer.orders[0][0][k]
        )

    def small_step(k):
        if k > 0:
            small_copy(k - 1).wait()
            small_out[...] += small_got[k - 1]
        else:
            small_out[...] = small[...]
        if k < 5:
            small_copy(k).start()

    table = tail_slots(plan)
    for slot in range(max(max(table), 12) + 1):
        for g, step in sorted(reversed(table.get(slot, [])), key=lambda item: item[1] == 0):
            reducer.run(g, step)
        if slot == HOME_SLOT:
            for i, rider in enumerate(riders):
                ride_copies(rider, homes[i], home_outs[i], home_send.at[i], home_recv.at[i])
        if 2 <= slot <= 12 and slot % 2 == 0:
            small_step(slot // 2 - 1)
    for g in plan.chosen:
        reducer.emit(g, True)
    for i, rider in enumerate(riders):
        ride_end(rider, homes[i], home_outs[i], home_send.at[i], home_recv.at[i])


def collect(plan, riders, parts, states, small, products):
    sources = []
    recipe = {}
    for array, entry in products.items():
        recipe[array] = []
        for value, layer in entry:
            at = [i for i, known in enumerate(sources) if known is value]
            if not at:
                at = [len(sources)]
                sources.append(value)
            recipe[array].append((at[0], layer))
    count = len(riders)
    width = riders[0].array.shape[1]
    hidden = 4 * width
    anywhere = pl.BlockSpec(memory_space=pl.ANY)
    resident = pl.BlockSpec(memory_space=pltpu.VMEM)
    dma = pltpu.SemaphoreType.DMA
    shapes = [
        (width, hidden), (hidden, width), (width, width), (width, 3 * width),
        (width, width), (width, width), (width, 2 * width),
    ]
    out = pl.pallas_call(
        functools.partial(collect_kernel, plan, riders, recipe),
        in_specs=[resident] * count
        + [anywhere] * (len(sources) + len(plan.arrays))
        + [resident] * (len(plan.states_in()) + 1),
        out_specs=[anywhere] * (count + 7) + [resident],
        out_shape=[jax.ShapeDtypeStruct(rider.shape, BF) for rider in riders]
        + [jax.ShapeDtypeStruct(s, BF) for s in shapes]
        + [jax.ShapeDtypeStruct(small.shape, F32)],
        scratch_shapes=[
            pltpu.VMEM((5,) + small.shape, F32),
            dma((count, 2)),
            dma((count, 4)),
            dma((5,)),
            dma((5,)),
            dma((len(sources),)),
        ]
        + [pltpu.VMEM(v.shape, v.dtype) for v in sources]
        + plan.scratch(),
        compiler_params=pltpu.CompilerParams(
            collective_id=1, has_side_effects=True, vmem_limit_bytes=56 << 20
        ),
        name="collect",
    )(
        *[rider.array for rider in riders],
        *sources,
        *[parts[a] for a in plan.arrays],
        *[states[f] for f in plan.states_in()],
        small,
    )
    return out[:count], out[count : count + 7], out[count + 7]


def key_loads(offsets, source, staged, sem, layer, step):
    for t in range(2):
        first = pl.multiple_of((offsets[t] + step) * PAIR, PAIR)
        yield pltpu.make_async_copy(
            source.at[layer, :, pl.ds(first, PAIR)], staged.at[layer, step, t], sem.at[layer, step, t]
        )


def key_copies(staged, held, send, recv, layer, step):
    core, group, depth, _, _ = place()
    return [
        remote(
            staged.at[layer, step, t],
            held.at[layer, step, t],
            send.at[layer, step, t],
            recv.at[layer, step, t],
            (1 - core, group, depth),
        )
        for t in range(2)
    ]


def attend_steps(layers):
    return [(layer, step) for layer in range(layers) for step in range(4)]


def begin(layers, offsets, riders, ride, source, keys, reducer=None):
    staged, sem, held, send, recv = keys
    core, group, depth, _, _ = place()
    for layer, step in attend_steps(layers):
        for copy in key_loads(offsets, source, staged, sem, layer, step):
            copy.start()
    if reducer is not None:
        reducer.load()
    mates = row_mates(core, group, depth) if riders or reducer else [(1 - core, group, depth)]
    greet(mates + (reducer.across if reducer else []))
    for layer, step in attend_steps(layers):
        for copy in key_loads(offsets, source, staged, sem, layer, step):
            copy.wait()
        for copy in key_copies(staged, held, send, recv, layer, step):
            copy.start()
    for i, rider in enumerate(riders):
        ride_copies(rider, *[r[i] if j < 2 else r.at[i] for j, r in enumerate(ride)])


def end(layers, riders, ride, keys):
    staged, sem, held, send, recv = keys
    for layer, step in attend_steps(layers):
        for copy in key_copies(staged, held, send, recv, layer, step):
            copy.wait_send()
    for i, rider in enumerate(riders):
        ride_end(rider, *[r[i] if j < 2 else r.at[i] for j, r in enumerate(ride)])


def by_layer(causal, layer, act):
    for kind in sorted(set(causal)):
        if len(set(causal)) == 1:
            act(kind)
        else:
            pl.when(layer == causal.index(kind))(functools.partial(act, kind))


def attend_kernel(causal, offsets, riders, *refs):
    layers, count = len(causal), len(riders)
    q_ref, k_ref, v_ref, kv_ref, qf_ref, kf_ref = refs[:6]
    o_ref, of_ref, lse_ref = refs[6 + count : 9 + count]
    *keys, ride_send, ride_recv = refs[9 + 2 * count :]
    staged, _, held, send, recv = keys
    ride = (refs[6 : 6 + count], refs[9 + count : 9 + 2 * count], ride_send, ride_recv)
    layer, step = pl.program_id(0), pl.program_id(1)

    @pl.when((layer == 0) & (step == 0))
    def _():
        begin(layers, offsets, riders, ride, kv_ref, keys)

    for copy in key_copies(staged, held, send, recv, layer, step):
        copy.wait_recv()

    def work(kind):
        whole, stat = attend_pair(
            kind, q_ref[0], k_ref[0], v_ref[0], held[layer, step, 0], held[layer, step, 1],
            qf_ref[0], kf_ref[0],
        )
        o_ref[0] = whole.astype(BF)
        of_ref[0] = whole
        lse_ref[0] = stat

    by_layer(causal, layer, work)

    @pl.when((layer == layers - 1) & (step == 3))
    def _():
        end(layers, riders, ride, keys)


def grad_copies(gone, got, send, recv, layer, step):
    core, group, depth, _, _ = place()
    return [
        remote(
            gone.at[layer, step, t],
            got.at[layer, step, t],
            send.at[layer, step, t],
            recv.at[layer, step, t],
            (1 - core, group, depth),
        )
        for t in range(2)
    ]


def attend_back_kernel(causal, offsets, riders, joined, plan, table, *refs):
    layers, count = len(causal), len(riders)
    q_ref, k_ref, v_ref, kv_ref, qf_ref, kf_ref, o_ref, lse_ref, do_ref = refs[:9]
    sources, refs = refs[9 : 9 + count], refs[9 + count :]
    parts = dict(zip(plan.arrays, refs))
    refs = refs[len(parts) :]
    states = dict(zip(plan.states_in(), refs))
    refs = refs[len(states) :]
    outs = 1 if joined else 2
    dq_ref, dkv_ref, refs = refs[0], refs[outs - 1], refs[outs:]
    left = dict(zip(plan.states_out(), refs))
    refs = refs[len(left) :]
    targets, refs = refs[:count], refs[count:]
    keys, (gone, got, kept, g_send, g_recv) = refs[:5], refs[5:10]
    staged, _, held, send, recv = keys
    scratch, (ride_send, ride_recv) = refs[10:-2], refs[-2:]
    ride = (sources, targets, ride_send, ride_recv)
    layer, step = pl.program_id(0), pl.program_id(1)
    width = 4 * PAIR
    reducer = Reducer(plan, parts, states, left, [], scratch)

    @pl.when((layer == 0) & (step == 0))
    def _():
        begin(layers, offsets, riders, ride, kv_ref, keys, reducer)

    for slot in range(4 * layers):
        moves = table.get(slot, [])
        if moves:

            @pl.when((layer == slot // 4) & (step == slot % 4))
            def _():
                for g, stage in moves:
                    reducer.run(g, stage)

    for copy in key_copies(staged, held, send, recv, layer, step):
        copy.wait_recv()

    def work(kind):
        columns = pl.ds(pl.multiple_of(step * PAIR, PAIR), PAIR)

        @pl.loop(0, 2)
        def _(head):
            mine, dq, dk, dv, dko, dvo = attend_back_head(
                kind, head, q_ref[0], k_ref[0], v_ref[0], held[layer, step, 0],
                held[layer, step, 1], qf_ref[0], kf_ref[0], o_ref[0], lse_ref[0], do_ref[0],
            )
            dq_ref[layer, :, columns] = jnp.where(mine, dq.astype(BF), dq_ref[layer, :, columns])
            kept[layer, step, 0] = jnp.where(mine, dk, kept[layer, step, 0])
            kept[layer, step, 1] = jnp.where(mine, dv, kept[layer, step, 1])
            gone[layer, step, 0] = jnp.where(mine, dko.astype(BF), gone[layer, step, 0])
            gone[layer, step, 1] = jnp.where(mine, dvo.astype(BF), gone[layer, step, 1])

    by_layer(causal, layer, work)
    for copy in grad_copies(gone, got, g_send, g_recv, layer, step):
        copy.start()

    @pl.when((layer == layers - 1) & (step == 3))
    def _():
        for one, at in attend_steps(layers):
            for t, copy in enumerate(grad_copies(gone, got, g_send, g_recv, one, at)):
                copy.wait()
                first = (width if joined else 0) + t * width + at * PAIR
                dkv_ref[one, :, first : first + PAIR] = (
                    kept[one, at, t] + got[one, at, t].astype(F32)
                ).astype(BF)
        for g in plan.chosen:
            reducer.run(g, plan.leave[g])
        end(layers, riders, ride, keys)


def attend_specs(size, offsets, masks):
    def column(at):
        return pl.BlockSpec((1, size, PAIR), lambda l, p: (l, 0, at + p))

    def shared(rows, first):
        return pl.BlockSpec((1, rows, PAIR), lambda l, p: (l + first, 0, 0))

    return (
        [column(at) for at in offsets]
        + [pl.BlockSpec(memory_space=pl.ANY)]
        + [shared(size, masks[0]), shared(2 * size, masks[1])]
    ), column


def key_scratch(layers, size):
    slots = pltpu.VMEM((layers, 4, 2, size, PAIR), BF)
    sems = pltpu.SemaphoreType.DMA((layers, 4, 2))
    return [slots, sems, slots, sems, sems]


def attend_call(
    kernel, name, layers, riders, collective, in_specs, out_specs, out_shape, scratch, flops, args
):
    count = len(riders)
    dma = pltpu.SemaphoreType.DMA
    return pl.pallas_call(
        kernel,
        grid=(layers, 4),
        in_specs=in_specs,
        out_specs=out_specs + [pl.BlockSpec(memory_space=pl.ANY)] * count,
        out_shape=out_shape + [jax.ShapeDtypeStruct(rider.shape, BF) for rider in riders],
        scratch_shapes=scratch + [dma((max(count, 1), 2)), dma((max(count, 1), 4))],
        compiler_params=pltpu.CompilerParams(
            vmem_limit_bytes=56 << 20, collective_id=collective, has_side_effects=True
        ),
        cost_estimate=pl.CostEstimate(flops=flops, bytes_accessed=flops // 512, transcendentals=0),
        name=name,
    )(*args)


def attend_forward(q, kv, offsets, masks, features, causal, riders, collective):
    layers, size = len(causal), q.shape[1]
    width = 4 * PAIR
    in_specs, column = attend_specs(size, offsets, masks)
    dma = pltpu.SemaphoreType.DMA
    return attend_call(
        functools.partial(attend_kernel, causal, offsets[1:], riders),
        "attend_forward",
        layers,
        riders,
        collective,
        in_specs + [pl.BlockSpec(memory_space=pltpu.VMEM)] * len(riders),
        [column(0)] * 3,
        [jax.ShapeDtypeStruct((layers, size, width), t) for t in (BF, F32, F32)],
        key_scratch(layers, size),
        16 * layers * size * size * width,
        (q, kv, kv, kv, *features, *[rider.array for rider in riders]),
    )


def attend_backward(
    q, kv, offsets, masks, features, o, lse, do, causal, riders, collective, joined,
    plan, table, parts, states,
):
    layers, size = len(causal), q.shape[1]
    width = 4 * PAIR
    in_specs, column = attend_specs(size, offsets, masks)
    dma = pltpu.SemaphoreType.DMA
    resident = pl.BlockSpec(memory_space=pltpu.VMEM)
    anywhere = pl.BlockSpec(memory_space=pl.ANY)
    widths = [3 * width] if joined else [width, 2 * width]
    slots = (layers, 4, 2, size, PAIR)
    left = [plan.state_shape(f, plan.spans[f][1]) for f in plan.states_out()]
    return attend_call(
        functools.partial(
            attend_back_kernel, causal, offsets[1:], riders, joined, plan, table
        ),
        "attend_backward",
        layers,
        riders,
        collective,
        in_specs
        + [column(0)] * 3
        + [resident] * len(riders)
        + [anywhere] * len(plan.arrays)
        + [resident] * len(plan.states_in()),
        [resident] * (len(widths) + len(left)),
        [jax.ShapeDtypeStruct((layers, size, w), BF) for w in widths] + left,
        key_scratch(layers, size)
        + [
            pltpu.VMEM(slots, BF),
            pltpu.VMEM(slots, BF),
            pltpu.VMEM(slots, F32),
            dma((layers, 4, 2)),
            dma((layers, 4, 2)),
        ]
        + plan.scratch(),
        40 * layers * size * size * width,
        (
            q, kv, kv, kv, *features, o, lse, do,
            *[rider.array for rider in riders],
            *[parts[a] for a in plan.arrays],
            *[states[f] for f in plan.states_in()],
        ),
    )


def dot(a, b):
    return lax.dot_general(a, b, (((1,), (0,)), ((), ())), preferred_element_type=F32)


def dot_back(a, b):
    return lax.dot_general(a, b, (((1,), (1,)), ((), ())), preferred_element_type=F32)


def dot_outer(a, b):
    return lax.dot_general(a, b, (((0,), (0,)), ((), ())), preferred_element_type=F32)


def each(function, *stacked):
    return jnp.stack([function(*(s[i] for s in stacked)) for i in range(2)])


def widen_kernel(count, *refs):
    sums, homes, refs = refs[:count], refs[count : count + 4], refs[count + 4 :]
    wide, tokens, grads = refs[:count], refs[count], refs[count + 1]
    for source, target in zip(sums, wide):
        target[...] = source[...].astype(F32)
    core = lax.axis_index("section")

    @pl.when(core == 0)
    def _():
        tokens[...] = homes[0][...]
        grads[...] = homes[2][...].astype(F32)

    @pl.when(core != 0)
    def _():
        tokens[...] = homes[1][...]
        grads[...] = homes[3][...].astype(F32)


def widen(sums, homes, steps=4):
    def rows(shape):
        return pl.BlockSpec((shape[0] // steps,) + shape[1:], lambda i: (i, 0))

    homes = [h.reshape(-1, h.shape[-1]) for h in homes]
    shapes = [v.shape for v in sums] + [homes[0].shape] * 2
    types = [F32] * len(sums) + [BF, F32]
    return pl.pallas_call(
        functools.partial(widen_kernel, len(sums)),
        grid=(steps,),
        in_specs=[rows(v.shape) for v in (*sums, *homes)],
        out_specs=[rows(s) for s in shapes],
        out_shape=[jax.ShapeDtypeStruct(s, t) for s, t in zip(shapes, types)],
        name="widen",
    )(*sums, *homes)


def row_shards(
    inputs,
    cotangent,
    qkv_weight,
    out_weight,
    up_weight,
    down_weight,
    norm_gain,
    norm_bias,
    cross_q_weight,
    cross_kv_weight,
    cross_out_weight,
    cross_gain,
    cross_bias,
    source_segments,
    target_segments,
):
    core = lax.axis_index("section")
    depth = lax.axis_index("seq")
    span = inputs.shape[2]
    width = inputs.shape[3]

    x_both, qkv, both, features = spread(
        inputs[0],
        source_segments,
        target_segments,
        qkv_weight[0],
        out_weight[0],
        up_weight[0],
        down_weight[0],
        norm_gain[0],
        norm_bias[0],
    )
    qkv_both, out_both, up_both, down_both, gain_both, bias_both = both
    g_e, g_d = gain_both[0], gain_both[1]
    b_e, b_d = bias_both[0], bias_both[1]
    wu_e, wu_d = up_both[0], up_both[1]
    wd_e, wd_d = down_both[0], down_both[1]

    self_args = ((0, 4, 8), (0, 0), features)
    o, o_wide, lse, cot = attend_forward(
        qkv, qkv, *self_args, (False, True), [RowRider(cotangent)], 2
    )
    cot = cot.astype(F32)
    summed = x_both.astype(F32) + lax.dot_general(
        o, out_both, (((2,), (1,)), ((0,), (0,))), preferred_element_type=F32
    )
    s1, t1 = summed[0], summed[1]

    h_s = layer_norm(s1, g_e[0], b_e[0])
    h_s_low = h_s.astype(BF)
    u_s = dot(h_s_low, wu_e)
    gel_s = gelu_tanh(u_s).astype(BF)
    s2 = h_s + dot(gel_s, wd_e)
    memory = layer_norm(s2, g_e[1], b_e[1]).astype(BF)
    ckv = dot(memory, cross_kv_weight).astype(BF)

    h_t = layer_norm(t1, g_d[0], b_d[0])
    h_t_low = h_t.astype(BF)
    cq = dot(h_t_low, cross_q_weight).astype(BF)
    cross_args = ((0, 0, 4), (1, 0), features)
    o_c, oc_wide, lse_c = attend_forward(cq[None], ckv[None], *cross_args, (False,), [], 3)
    o_c = o_c[0]
    t2 = h_t + dot(o_c, cross_out_weight)
    c_t = layer_norm(t2, cross_gain, cross_bias)
    c_t_low = c_t.astype(BF)
    u_t = dot(c_t_low, wu_d)
    gel_t = gelu_tanh(u_t).astype(BF)
    t3 = c_t + dot(gel_t, wd_d)
    decoded, pull_t3 = jax.vjp(layer_norm, t3, g_d[1], b_d[1])
    decoded = decoded.astype(BF)

    grad_t3, gg_d1, gb_d1 = pull_t3(cot)
    low_t3 = grad_t3.astype(BF)
    gw_down_d = dot_outer(gel_t, low_t3).astype(BF)
    grad_u_t = jax.vjp(gelu_tanh, u_t)[1](dot_back(low_t3, wd_d))[0].astype(BF)
    gw_up_d = dot_outer(c_t_low, grad_u_t).astype(BF)
    grad_c = grad_t3 + dot_back(grad_u_t, wu_d)
    grad_t2, gg_c, gb_c = jax.vjp(layer_norm, t2, cross_gain, cross_bias)[1](grad_c)
    low_t2 = grad_t2.astype(BF)
    grad_o_c = dot_back(low_t2, cross_out_weight).astype(BF)
    hidden = wu_d.shape[1]
    parts = {0: gw_up_d, 1: gw_down_d}
    plan = Plan(width, hidden, {0: (0, 2)})
    grad_cq, grad_ckv, state_d, home_decoded = attend_backward(
        cq[None], ckv[None], *cross_args, oc_wide, lse_c, grad_o_c[None], (False,),
        [HomeRider(decoded, 1)], 4, False, plan, CROSS_TABLE, parts, {},
    )
    grad_cq, grad_ckv = grad_cq[0], grad_ckv[0]
    grad_h = grad_t2 + dot_back(grad_cq, cross_q_weight)
    grad_t1, gg_d0, gb_d0 = jax.vjp(layer_norm, t1, g_d[0], b_d[0])[1](grad_h)
    low_t1 = grad_t1.astype(BF)

    grad_memory = dot_back(grad_ckv, cross_kv_weight).astype(BF).astype(F32)
    grad_s2, gg_e1, gb_e1 = jax.vjp(layer_norm, s2, g_e[1], b_e[1])[1](grad_memory)
    low_s2 = grad_s2.astype(BF)
    gw_down_e = dot_outer(gel_s, low_s2).astype(BF)
    grad_u_s = jax.vjp(gelu_tanh, u_s)[1](dot_back(low_s2, wd_e))[0].astype(BF)
    gw_up_e = dot_outer(h_s_low, grad_u_s).astype(BF)
    grad_h = grad_s2 + dot_back(grad_u_s, wu_e)
    grad_s1, gg_e0, gb_e0 = jax.vjp(layer_norm, s1, g_e[0], b_e[0])[1](grad_h)
    low_s1 = grad_s1.astype(BF)

    low_1 = jnp.stack([low_s1, low_t1])
    grad_o = lax.dot_general(
        low_1, out_both, (((2,), (2,)), ((0,), (0,))), preferred_element_type=F32
    ).astype(BF)
    parts = {2: gw_up_e, 3: gw_down_e}
    plan = Plan(width, hidden, {0: (2, 5), 1: (0, 2)})
    grad_qkv, state_d, state_e, home_memory = attend_backward(
        qkv, qkv, *self_args, o_wide, lse, grad_o, (False, True), [HomeRider(memory, 0)], 5, True,
        plan, SELF_TABLE, parts, {0: state_d},
    )
    low_cross = low_t2
    products = {
        4: ((o, 1), (low_1, 1)),
        5: ((x_both, 1), (grad_qkv, 1)),
        6: ((o, 0), (low_1, 0)),
        7: ((x_both, 0), (grad_qkv, 0)),
        8: ((o_c, None), (low_cross, None)),
        9: ((h_t_low, None), (grad_cq, None)),
        10: ((memory, None), (grad_ckv, None)),
    }
    grad_x = jnp.stack([grad_s1, grad_t1]) + lax.dot_general(
        grad_qkv, qkv_both, (((2,), (2,)), ((0,), (0,))), preferred_element_type=F32
    )
    grad_x = grad_x.astype(BF)

    small = jnp.stack(
        [gg_e0, gg_e1, gb_e0, gb_e1, gg_d0, gg_d1, gb_d0, gb_d1, gg_c, gb_c]
        + [jnp.zeros_like(gg_c)] * 6
    )
    plan = Plan(width, hidden, {0: (5, 10), 1: (2, 10), 2: (0, 10), 3: (0, 10)}, tuple(products))
    (home_xs, home_xt), sums, small = collect(
        plan,
        [HomeRider(grad_x[0], 0), HomeRider(grad_x[1], 1)],
        {},
        {0: state_d, 1: state_e},
        small,
        products,
    )
    *wide_sums, outputs, grads = widen(sums, [home_memory, home_decoded, home_xs, home_xt])
    g_up, g_down, g_out, g_qkv, g_cross_out, g_cross_q, g_cross_kv = wide_sums
    local = (1, -1) + inputs.shape[2:]
    layer_small = jnp.where(core == 0, small[:4], small[4:8])
    return (
        outputs.reshape(local),
        grads.reshape(local),
        g_qkv[None],
        g_out[None],
        g_up[None],
        g_down[None],
        layer_small[None, :2],
        layer_small[None, 2:],
        g_cross_q,
        g_cross_kv,
        g_cross_out,
        small[8],
        small[9],
    )


def solution(mesh):
    in_specs = (
        P("section", "dp", "seq", None),
        P("dp", "seq", None),
        P("section", None, None),
        P("section", None, None),
        P("section", None, None),
        P("section", None, None),
        P("section", None, None),
        P("section", None, None),
        P(),
        P(),
        P(),
        P(),
        P(),
        P("dp", None),
        P("dp", None),
    )
    out_specs = (
        P("section", "dp", "seq", None),
        P("section", "dp", "seq", None),
        P("section", None, None),
        P("section", None, None),
        P("section", None, None),
        P("section", None, None),
        P("section", None, None),
        P("section", None, None),
        P(),
        P(),
        P(),
        P(),
        P(),
    )
    whole_rows = mesh.shape["section"] == 2 and mesh.shape["seq"] == 4 and mesh.shape["dp"] == 4
    body = row_shards if whole_rows else shards
    return jax.shard_map(body, mesh=mesh, in_specs=in_specs, out_specs=out_specs, check_vma=False)
```

```python
import functools

import jax
import jax.numpy as jnp
from jax import lax
from jax.experimental import pallas as pl
from jax.experimental.pallas import tpu as pltpu
from jax.sharding import PartitionSpec as P

DH = 64
MICRO = 2
MB_ROWS = 2


EPSILON = 1e-05
NEGATIVE = -1e30


def from_behind(value, axis, steps):
    count = lax.axis_size(axis)
    leading, last = (max(0, -steps), min(count, count - steps))
    return lax.ppermute(value, axis, [(source, source + steps) for source in range(leading, last)])


def layer_norm(vector, gain_row, bias_row):
    centre = vector - jnp.mean(vector, axis=-1, keepdims=True)
    spread = jnp.mean(centre * centre, axis=-1, keepdims=True)
    return centre * lax.rsqrt(spread + EPSILON) * gain_row + bias_row


def gelu_tanh(vector):
    return jax.nn.gelu(vector, approximate=True)


def heads_view(vector):
    return vector.reshape(vector.shape[:-1] + (vector.shape[-1] // DH, DH))


def joined_view(vector):
    return vector.reshape(vector.shape[:-2] + (vector.shape[-2] * vector.shape[-1],))


def dense_rows(left_side, right_side):
    return jnp.einsum("rsd,de->rse", left_side, right_side, preferred_element_type=jnp.float32)


def dense_back(left_side, right_side):
    return jnp.einsum("rse,de->rsd", left_side, right_side, preferred_element_type=jnp.float32)


def outer_sum(left_side, right_side):
    return jnp.einsum("rsd,rse->de", left_side, right_side, preferred_element_type=jnp.float32)


def build_mask(query_ids, key_ids, query_places, key_places, causal):
    same_doc = query_ids[:, :, None] == key_ids[:, None, :]
    ordered = (key_places[None, :] <= query_places[:, None]) | jnp.logical_not(causal)
    return same_doc & ordered[None]


def soft_forward(queries, key_rows, value_rows, allowed):
    score_scale = DH ** (-0.5)
    scores = (
        jnp.einsum(
            "rqhe,rkhe->rhqk",
            heads_view(queries),
            heads_view(key_rows),
            preferred_element_type=jnp.float32,
        )
        * score_scale
    )
    scores = jnp.where(allowed[:, None], scores, NEGATIVE)
    highest = jnp.max(scores, axis=-1, keepdims=True)
    exp_terms = jnp.exp(scores - highest)
    totals = jnp.sum(exp_terms, axis=-1, keepdims=True)
    weights = exp_terms / totals
    log_total = (highest + jnp.log(totals))[..., 0]
    mixed_out = jnp.einsum(
        "rhqk,rkhe->rqhe",
        weights.astype(jnp.bfloat16),
        heads_view(value_rows),
        preferred_element_type=jnp.float32,
    )
    return (joined_view(mixed_out), weights, log_total)


def score_grads(grad_mixed, value_rows, weights):
    grad_weights = jnp.einsum(
        "rqhe,rkhe->rhqk",
        heads_view(grad_mixed),
        heads_view(value_rows),
        preferred_element_type=jnp.float32,
    )
    inner_sum = jnp.sum(grad_weights * weights, axis=-1, keepdims=True)
    grad_scores = (weights * (grad_weights - inner_sum)).astype(jnp.bfloat16)
    return (grad_scores, inner_sum[..., 0])


def attend_keys(queries, key_rows, value_rows, query_ids, key_ids, causal):
    span_len = key_rows.shape[1]
    offset = lax.axis_index("seq") * span_len
    whole_keys, whole_values = (
        lax.all_gather(key_rows, "seq", axis=1, tiled=True),
        lax.all_gather(value_rows, "seq", axis=1, tiled=True),
    )
    own_positions = offset + jnp.arange(span_len)
    all_positions = jnp.arange(whole_keys.shape[1])
    own_ids = lax.dynamic_slice_in_dim(query_ids, offset, span_len, 1)
    allowed = build_mask(own_ids, key_ids, own_positions, all_positions, causal)
    mixed_out, weights, log_total = soft_forward(queries, whole_keys, whole_values, allowed)
    kept_state = (
        queries,
        key_rows,
        value_rows,
        whole_keys,
        whole_values,
        weights,
        log_total,
        query_ids,
        key_ids,
        causal,
    )
    return (mixed_out, kept_state)


def attend_back(kept_state, grad_mixed):
    (
        queries,
        key_rows,
        value_rows,
        whole_keys,
        whole_values,
        weights,
        log_total,
        query_ids,
        key_ids,
        causal,
    ) = kept_state
    score_scale = DH ** (-0.5)
    grad_scores, inner_sum = score_grads(grad_mixed, whole_values, weights)
    grad_queries = (
        jnp.einsum(
            "rhqk,rkhe->rqhe",
            grad_scores,
            heads_view(whole_keys),
            preferred_element_type=jnp.float32,
        )
        * score_scale
    )
    part_keys = (
        jnp.einsum(
            "rhqk,rqhe->rkhe", grad_scores, heads_view(queries), preferred_element_type=jnp.float32
        )
        * score_scale
    )
    part_values = jnp.einsum(
        "rhqk,rqhe->rkhe",
        weights.astype(jnp.bfloat16),
        heads_view(grad_mixed),
        preferred_element_type=jnp.float32,
    )
    grad_keys, grad_values = (
        lax.psum_scatter(
            joined_view(part_keys).astype(jnp.bfloat16), "seq", scatter_dimension=1, tiled=True
        ).astype(jnp.float32),
        lax.psum_scatter(
            joined_view(part_values).astype(jnp.bfloat16), "seq", scatter_dimension=1, tiled=True
        ).astype(jnp.float32),
    )
    return (joined_view(grad_queries), grad_keys, grad_values)


def layer_forward(tokens, memory_in, own_ids, source_ids, target_ids, params, decoder):
    (
        qkv_matrix,
        out_matrix,
        up_matrix,
        down_matrix,
        norm_gains,
        norm_biases,
        query_matrix,
        pair_matrix,
        cross_matrix,
        cross_gains,
        cross_shift,
    ) = params
    residual = tokens.astype(jnp.float32)
    packed = dense_rows(tokens, qkv_matrix).astype(jnp.bfloat16)
    queries, key_rows, value_rows = jnp.split(packed, 3, axis=-1)
    mixed_out, self_state = attend_keys(queries, key_rows, value_rows, own_ids, own_ids, decoder)
    mixed_low = mixed_out.astype(jnp.bfloat16)
    first_sum = residual + dense_rows(mixed_low, out_matrix)
    first_norm = layer_norm(first_sum, norm_gains[0], norm_biases[0])
    first_low = first_norm.astype(jnp.bfloat16)
    cross_query = dense_rows(first_low, query_matrix).astype(jnp.bfloat16)
    cross_pair = dense_rows(memory_in, pair_matrix).astype(jnp.bfloat16)
    cross_keys, cross_values = jnp.split(cross_pair, 2, axis=-1)
    cross_mixed, cross_state = attend_keys(
        cross_query, cross_keys, cross_values, target_ids, source_ids, False
    )
    cross_low = cross_mixed.astype(jnp.bfloat16)
    cross_sum = first_norm + dense_rows(cross_low, cross_matrix)
    second = jnp.where(decoder, layer_norm(cross_sum, cross_gains, cross_shift), first_norm)
    second_low = second.astype(jnp.bfloat16)
    upward = dense_rows(second_low, up_matrix)
    gated_low = gelu_tanh(upward).astype(jnp.bfloat16)
    last_sum = second + dense_rows(gated_low, down_matrix)
    output = layer_norm(last_sum, norm_gains[1], norm_biases[1])
    kept_state = (
        tokens,
        self_state,
        mixed_low,
        first_sum,
        first_low,
        cross_state,
        cross_low,
        cross_sum,
        second_low,
        upward,
        gated_low,
        last_sum,
    )
    return (output, kept_state)


def layer_backward(kept_state, grad_out, params, decoder):
    (
        qkv_matrix,
        out_matrix,
        up_matrix,
        down_matrix,
        norm_gains,
        norm_biases,
        query_matrix,
        pair_matrix,
        cross_matrix,
        cross_gains,
        cross_shift,
    ) = params
    (
        tokens,
        self_state,
        mixed_low,
        first_sum,
        first_low,
        cross_state,
        cross_low,
        cross_sum,
        second_low,
        upward,
        gated_low,
        last_sum,
    ) = kept_state
    unused, pull_last = jax.vjp(layer_norm, last_sum, norm_gains[1], norm_biases[1])
    grad_last, grad_gain_last, grad_bias_last = pull_last(grad_out)
    down_in = grad_last.astype(jnp.bfloat16)
    grad_down = outer_sum(gated_low, down_in)
    grad_gated = dense_back(down_in, down_matrix)
    unused, pull_gelu = jax.vjp(gelu_tanh, upward)
    up_in = pull_gelu(grad_gated)[0].astype(jnp.bfloat16)
    grad_up = outer_sum(second_low, up_in)
    grad_second = grad_last + dense_back(up_in, up_matrix)
    unused, pull_cross = jax.vjp(layer_norm, cross_sum, cross_gains, cross_shift)
    grad_cross_sum, grad_cross_gain, grad_cross_bias = pull_cross(
        jnp.where(decoder, grad_second, 0.0)
    )
    grad_first = jnp.where(decoder, grad_cross_sum, grad_second)
    cross_in = grad_cross_sum.astype(jnp.bfloat16)
    grad_cross_out = outer_sum(cross_low, cross_in)
    grad_cross_mixed = dense_back(cross_in, cross_matrix).astype(jnp.bfloat16)
    grad_cross_query, grad_cross_keys, grad_cross_values = attend_back(
        cross_state, grad_cross_mixed
    )
    query_in = grad_cross_query.astype(jnp.bfloat16)
    grad_query_matrix = outer_sum(first_low, query_in)
    grad_first = grad_first + dense_back(query_in, query_matrix)
    pair_in = jnp.concatenate([grad_cross_keys, grad_cross_values], axis=-1).astype(jnp.bfloat16)
    unused, pull_first = jax.vjp(layer_norm, first_sum, norm_gains[0], norm_biases[0])
    grad_first_sum, grad_gain_first, grad_bias_first = pull_first(grad_first)
    out_in = grad_first_sum.astype(jnp.bfloat16)
    grad_out_matrix = outer_sum(mixed_low, out_in)
    grad_mixed = dense_back(out_in, out_matrix).astype(jnp.bfloat16)
    grad_queries, grad_keys, grad_values = attend_back(self_state, grad_mixed)
    qkv_in = jnp.concatenate([grad_queries, grad_keys, grad_values], axis=-1).astype(jnp.bfloat16)
    grad_qkv_matrix = outer_sum(tokens, qkv_in)
    grad_tokens = grad_first_sum + dense_back(qkv_in, qkv_matrix)
    grad_set = (
        grad_qkv_matrix,
        grad_out_matrix,
        grad_up,
        grad_down,
        jnp.stack([grad_gain_first, grad_gain_last]),
        jnp.stack([grad_bias_first, grad_bias_last]),
        grad_query_matrix,
        jnp.zeros(pair_matrix.shape, jnp.float32),
        grad_cross_out,
        grad_cross_gain,
        grad_cross_bias,
    )
    return (grad_tokens, pair_in, grad_set)


def shards(
    inputs,
    cotangent,
    qkv_weight,
    out_weight,
    up_weight,
    down_weight,
    norm_gain,
    norm_bias,
    cross_q_weight,
    cross_kv_weight,
    cross_out_weight,
    cross_gain,
    cross_bias,
    source_segments,
    target_segments,
):
    section_index = lax.axis_index("section")
    decoder = section_index == 1
    params = (
        qkv_weight[0],
        out_weight[0],
        up_weight[0],
        down_weight[0],
        norm_gain[0],
        norm_bias[0],
        cross_q_weight,
        cross_kv_weight,
        cross_out_weight,
        cross_gain,
        cross_bias,
    )
    tokens_all = inputs[0]
    own_all = jnp.where(decoder, target_segments, source_segments)
    span_len = tokens_all.shape[1]
    features = tokens_all.shape[2]
    memory_in = jnp.zeros((MB_ROWS, span_len, features), jnp.bfloat16)
    outputs_all = jnp.zeros(tokens_all.shape, jnp.bfloat16)
    caches = []
    sent_rows = []
    for forward_tick in range(MICRO + 1):
        micro_index = forward_tick - section_index
        active = (micro_index >= 0) & (micro_index < MICRO)
        first_row = jnp.clip(micro_index, 0, MICRO - 1) * MB_ROWS
        rows_now = lax.dynamic_slice_in_dim(tokens_all, first_row, MB_ROWS, 0)
        own_now = lax.dynamic_slice_in_dim(own_all, first_row, MB_ROWS, 0)
        source_now = lax.dynamic_slice_in_dim(source_segments, first_row, MB_ROWS, 0)
        target_now = lax.dynamic_slice_in_dim(target_segments, first_row, MB_ROWS, 0)
        output, kept_state = layer_forward(
            rows_now, memory_in, own_now, source_now, target_now, params, decoder
        )
        output_low = output.astype(jnp.bfloat16)
        current = lax.dynamic_slice_in_dim(outputs_all, first_row, MB_ROWS, 0)
        outputs_all = lax.dynamic_update_slice_in_dim(
            outputs_all, jnp.where(active, output_low, current), first_row, 0
        )
        caches.append(kept_state)
        sent_rows.append(output_low)
        if forward_tick < MICRO:
            memory_in = from_behind(output_low, "section", 1)
    grad_pair_in = jnp.zeros((MB_ROWS, span_len, 2 * features), jnp.bfloat16)
    totals = tuple((jnp.zeros(param_item.shape, jnp.float32) for param_item in params))
    input_all = jnp.zeros(tokens_all.shape, jnp.float32)
    for backward_tick in range(MICRO + 1):
        forward_tick = MICRO - backward_tick
        micro_index = forward_tick - section_index
        active = (micro_index >= 0) & (micro_index < MICRO)
        first_row = jnp.clip(micro_index, 0, MICRO - 1) * MB_ROWS
        cot_now = lax.dynamic_slice_in_dim(cotangent, first_row, MB_ROWS, 0).astype(jnp.float32)
        memory_grad = lax.optimization_barrier(
            dense_back(grad_pair_in, params[7]).astype(jnp.bfloat16)
        ).astype(jnp.float32)
        pair_term = outer_sum(sent_rows[forward_tick], grad_pair_in)
        grad_out = jnp.where(decoder, cot_now, memory_grad)
        grad_tokens, pair_in, grad_set = layer_backward(
            caches[forward_tick], grad_out, params, decoder
        )
        grad_set = grad_set[:7] + (jnp.where(decoder, 0.0, pair_term),) + grad_set[8:]
        totals = jax.tree.map(
            lambda total_sum, new_term: total_sum + jnp.where(active, new_term, 0.0),
            totals,
            grad_set,
        )
        current = lax.dynamic_slice_in_dim(input_all, first_row, MB_ROWS, 0)
        input_all = lax.dynamic_update_slice_in_dim(
            input_all, jnp.where(active, grad_tokens, current), first_row, 0
        )
        if backward_tick < MICRO:
            grad_pair_in = from_behind(pair_in, "section", -1)
    layer_part = lax.psum(
        (totals[0], totals[1], totals[2], totals[3], totals[4], totals[5]), ("dp", "seq")
    )
    cross_part = lax.psum(
        (totals[6], totals[7], totals[8], totals[9], totals[10]), ("section", "dp", "seq")
    )
    return (
        outputs_all[None],
        input_all[None],
        layer_part[0][None],
        layer_part[1][None],
        layer_part[2][None],
        layer_part[3][None],
        layer_part[4][None],
        layer_part[5][None],
        cross_part[0],
        cross_part[1],
        cross_part[2],
        cross_part[3],
        cross_part[4],
    )


BF = jnp.bfloat16
F32 = jnp.float32
AXES = ("section", "dp", "seq")
PAIR = 2 * DH
STAT = 8
Q_ROWS = 256
K_ROWS = 256
AHEAD = 2


def swap(value, move):
    pairs = []
    for core in range(2):
        for group in range(4):
            for depth in range(4):
                to = move(core, group, depth)
                if to is not None:
                    pairs.append(
                        ((core * 4 + group) * 4 + depth, (to[0] * 4 + to[1]) * 4 + to[2])
                    )
    return lax.ppermute(value, AXES, pairs)


def to_core(value):
    return swap(value, lambda core, group, depth: (1 - core, group, depth))


def replace_block(whole, block, at, axis):
    size, count = block.shape[axis], whole.shape[axis]
    parts = [lax.slice_in_dim(whole, 0, at, axis=axis)] if at > 0 else []
    parts.append(block)
    if at + size < count:
        parts.append(lax.slice_in_dim(whole, at + size, count, axis=axis))
    return jnp.concatenate(parts, axis=axis)


def attend_pair(causal, q, k, v, ko, vo, qf, kf):
    size = q.shape[0]
    half = size // 2
    lane = lax.broadcasted_iota(jnp.int32, (size, PAIR), 1)
    low_lanes = lane < DH
    q = q * jnp.array(DH ** (-0.5), BF)
    kf, kfo = kf[:size], kf[size:]
    one = jnp.ones_like(v)
    tasks = []
    for head in range(2):
        mine = low_lanes if head == 0 else jnp.logical_not(low_lanes)
        qa = jnp.where(mine, q, qf)
        ka = [jnp.where(mine, k, kf), jnp.where(mine, ko, kfo)]
        va = [jnp.where(mine, v, one), jnp.where(mine, vo, one)]
        for start in range(0, size, Q_ROWS):
            rows = slice(start, start + Q_ROWS)
            if causal and start < half:
                kk = jnp.concatenate([ka[0][:half], ka[1][:half]], axis=0)
                vv = jnp.concatenate([va[0][:half], va[1][:half]], axis=0)
                diagonal = 0
            else:
                kk = jnp.concatenate(ka, axis=0)
                vv = jnp.concatenate(va, axis=0)
                diagonal = half if causal else None
            tasks.append((qa[rows], kk, vv, diagonal, start % half))

    def scores(task):
        qq, kk, _, _, _ = task
        return lax.dot_general(qq, kk, (((1,), (1,)), ((), ())), preferred_element_type=F32)

    def finish(task, s):
        _, _, vv, diagonal, first = task
        if diagonal is not None:
            row = lax.broadcasted_iota(jnp.int32, (Q_ROWS, half), 0) + first
            col = lax.broadcasted_iota(jnp.int32, (Q_ROWS, half), 1)
            cut = jnp.where(col <= row, s[:, diagonal : diagonal + half], NEGATIVE)
            s = replace_block(s, cut, diagonal, 1)
        top = jnp.max(s, axis=1, keepdims=True)
        p = jnp.exp(s - top).astype(BF)
        o = lax.dot_general(p, vv, (((1,), (0,)), ((), ())), preferred_element_type=F32)
        return o / pltpu.roll(o, DH, 1), top + jnp.log(o)

    done = []
    ahead = [scores(t) for t in tasks[:AHEAD]]
    for i, task in enumerate(tasks):
        if i + AHEAD < len(tasks):
            ahead.append(scores(tasks[i + AHEAD]))
        done.append(finish(task, ahead[i]))
    count = size // Q_ROWS
    outs = [jnp.concatenate([d[0] for d in done[h * count :][:count]], axis=0) for h in range(2)]
    stats = [jnp.concatenate([d[1] for d in done[h * count :][:count]], axis=0) for h in range(2)]
    return jnp.where(low_lanes, outs[0], outs[1]), jnp.where(low_lanes, stats[1], stats[0])


def split3(value):
    a = value.astype(BF)
    rest = value - a.astype(F32)
    b = rest.astype(BF)
    c = (rest - b.astype(F32)).astype(BF)
    return a, b, c


def with_stat(base, value, lane):
    a, b, c = split3(-value)
    at = lane & (DH - 1)
    base = jnp.where(at == STAT, a, base)
    base = jnp.where(at == STAT + 1, b, base)
    return jnp.where(at == STAT + 2, c, base)


def attend_back_head(causal, head, q, k, v, ko, vo, qf, kf, o, lse, do):
    size = q.shape[0]
    half = size // 2
    lane = lax.broadcasted_iota(jnp.int32, (size, PAIR), 1)
    mine = (lane >= head * DH) & (lane < head * DH + DH)
    scale = DH ** (-0.5)
    q = q * jnp.array(scale, BF)
    kf, kfo = kf[:size], kf[size:]
    inner = jnp.sum(jnp.where(mine, do.astype(F32) * o, 0.0), axis=1, keepdims=True)
    dstat = with_stat(jnp.zeros_like(do), jnp.broadcast_to(inner, o.shape), lane)
    qa = jnp.where(mine, q, with_stat(qf, lse, lane))
    da = jnp.where(mine, do, dstat)
    tasks = []
    for own, keys, values, marks in ((True, k, v, kf), (False, ko, vo, kfo)):
        ka = jnp.where(mine, keys, marks)
        va = jnp.where(mine, values, marks)
        for start in range(0, size, K_ROWS):
            rows = slice(start, start + K_ROWS)
            late = causal and start >= half
            first = half if late else 0
            diagonal = (start % half) if causal and own else None
            tasks.append((ka[rows], va[rows], keys[rows], qa[first:], da[first:], first, diagonal))

    def scores(task):
        ka, va, _, qa, da, _, _ = task
        s = lax.dot_general(ka, qa, (((1,), (1,)), ((), ())), preferred_element_type=F32)
        dp = lax.dot_general(va, da, (((1,), (1,)), ((), ())), preferred_element_type=F32)
        return s, dp

    def finish(task, both):
        _, _, keys, _, _, first, diagonal = task
        s, dp = both
        if diagonal is not None:
            row = lax.broadcasted_iota(jnp.int32, (K_ROWS, half), 0) + diagonal
            col = lax.broadcasted_iota(jnp.int32, (K_ROWS, half), 1)
            cut = jnp.where(row <= col, s[:, :half], NEGATIVE)
            s = replace_block(s, cut, 0, 1)
        p = jnp.exp(s)
        ds = (p * dp).astype(BF)
        pb = p.astype(BF)
        dv = lax.dot_general(
            pb, do[first:], (((1,), (0,)), ((), ())), preferred_element_type=F32
        )
        dk = lax.dot_general(ds, q[first:], (((1,), (0,)), ((), ())), preferred_element_type=F32)
        dq = lax.dot_general(keys, ds, (((0,), (0,)), ((), ())), preferred_element_type=F32)
        return dk, dv, dq

    done = []
    ahead = [scores(t) for t in tasks[:AHEAD]]
    for i, task in enumerate(tasks):
        if i + AHEAD < len(tasks):
            ahead.append(scores(tasks[i + AHEAD]))
        done.append(finish(task, ahead[i]))
    dk = jnp.concatenate([d[0] for d in done], axis=0)
    dv = jnp.concatenate([d[1] for d in done], axis=0)
    full = sum(d[2] for d, task in zip(done, tasks) if task[5] == 0)
    late = [d[2] for d, task in zip(done, tasks) if task[5] > 0]
    if late:
        full = jnp.concatenate([full[:, :half], full[:, half:] + sum(late)], axis=1)
    return mine, full.T * scale, dk[:size], dv[:size], dk[size:], dv[size:]


MESH = pl.DeviceIdType.MESH


def place():
    core = lax.axis_index("section")
    group = lax.axis_index("dp")
    depth = lax.axis_index("seq")
    return core, group, depth, ((depth + 1) // 2) % 2, depth // 2


def greet(others):
    barrier = pltpu.get_barrier_semaphore()
    for other in others:
        pl.semaphore_signal(barrier, inc=1, device_id=other, device_id_type=MESH)
    pl.semaphore_wait(barrier, len(others))


def row_mates(core, group, depth):
    mates = [(1 - core, group, depth)]
    for step in range(1, 4):
        there = (depth + step) % 4
        mates += [(core, group, there), (1 - core, group, there)]
    return mates


def remote(source, target, send, recv, device):
    return pltpu.make_async_remote_copy(
        src_ref=source,
        dst_ref=target,
        send_sem=send,
        recv_sem=recv,
        device_id=device,
        device_id_type=MESH,
    )


def write_features(seg_ref, target_ref, queries, order, layer, core, depth):
    span = seg_ref.shape[1] // 4
    at = lax.broadcasted_iota(jnp.int32, (PAIR, span), 0)
    at = jnp.where(at >= DH, at - DH, at)
    own_core = core
    for i in range(2 if queries else 4):
        first = pl.multiple_of(order[i] * span, span)
        seg = seg_ref[pl.ds(depth, 1), pl.ds(first, span)]
        seg = jnp.broadcast_to(seg, (PAIR, span))
        if queries:
            value = jnp.where((seg == at) | (at == 4 + i), 1.0, 0.0)
        else:
            bad = (seg != at) & (at < 4)
            value = jnp.where(bad, NEGATIVE, 0.0)
            if layer == 1:
                barred = [0.0, NEGATIVE, NEGATIVE * (1 - own_core).astype(F32), NEGATIVE][i]
                value = jnp.where(at == 4, barred, value)
                if i == 3:
                    value = jnp.where(at == 5, NEGATIVE * own_core.astype(F32), value)
            value = jnp.where((at >= STAT) & (at < STAT + 3), 1.0, value)
        target_ref[layer, i * span : (i + 1) * span, :] = value.T.astype(BF)


def spread_kernel(count, x_ref, source_seg, target_seg, *refs):
    weights, (x_out, qkv_out, *outs) = refs[:count], refs[count : 2 * count + 2]
    features = refs[2 * count + 2 : 2 * count + 4]
    refs = refs[2 * count + 4 :]
    x_held, x_got, w_both, qkv_got, *held = refs[: count + 3]
    x_send, x_recv, x_own, x_home, qkv_home, w_send, w_recv, w_own, w_out = refs[count + 3 :]
    core, group, depth, side, at = place()
    span = x_ref.shape[1]
    holders = [w_both.at[core]] + held
    loads = [pltpu.make_async_copy(weights[i], holders[i], w_own.at[i]) for i in range(count)]
    for load in loads:
        load.start()
    x_load = pltpu.make_async_copy(x_ref.at[depth], x_held, x_own)
    x_load.start()
    greet(row_mates(core, group, depth))
    seat = 2 * core + at
    copies = []
    for step in (2, 1, 3, 0):
        row = (depth + step) % 4
        target = x_got.at[core, pl.ds(pl.multiple_of(at * span, span), span)]
        if step == 0:
            there = remote(
                x_held, target, x_send.at[step], x_recv.at[seat], (side, group, row)
            )
            here = pltpu.make_async_copy(x_held, target, x_recv.at[seat])
            x_load.wait()

            @pl.when(side == core)
            def _():
                here.start()

            @pl.when(side != core)
            def _():
                there.start()
        else:
            there = remote(
                x_ref.at[row], target, x_send.at[step], x_recv.at[seat], (side, group, row)
            )
            there.start()
        copies.append((step, there))
    moves = []
    for i in range(count):
        loads[i].wait()
        landing = w_both.at[core] if i == 0 else outs[i].at[core]
        gone = remote(
            holders[i], landing, w_send.at[i], w_recv.at[i], (1 - core, group, depth)
        )
        gone.start()
        if i > 0:
            own = pltpu.make_async_copy(held[i - 1], outs[i].at[core], w_out.at[i])
            own.start()
            moves.append(own)
        moves.append(gone)
    order = [core, 3 - core, 1 - core, 2 + core]
    for layer, seg_ref in enumerate((source_seg, target_seg)):
        write_features(seg_ref, features[0], True, order, layer, core, depth)
        write_features(seg_ref, features[1], False, order, layer, core, depth)
    for move in moves:
        move.wait()
    own = pltpu.make_async_copy(w_both, outs[0], w_out.at[0])
    own.start()
    local = [own]
    for step, there in copies:
        if step == 0:

            @pl.when(side != core)
            def _():
                there.wait_send()
        else:
            there.wait_send()
    tile = x_ref.shape[2]
    for seat_from in range(4):
        layer = seat_from // 2
        rows = pl.ds((seat_from % 2) * span, span)
        block = x_got.at[layer, rows]
        pltpu.make_async_copy(x_held, block, x_recv.at[seat_from]).wait()
        local.append(pltpu.make_async_copy(block, x_out.at[layer, rows], x_home.at[seat_from]))
        local[-1].start()

        @pl.loop(0, 3)
        def _(i):
            columns = pl.ds(pl.multiple_of(i * tile, tile), tile)
            qkv_got[layer, rows, columns] = dot(
                x_got[layer, rows, :], w_both[layer, :, columns]
            ).astype(BF)

        local.append(
            pltpu.make_async_copy(
                qkv_got.at[layer, rows], qkv_out.at[layer, rows], qkv_home.at[seat_from]
            )
        )
        local[-1].start()
    for copy in local:
        copy.wait()


def spread(tokens, source_segments, target_segments, *weights):
    rows, span, width = tokens.shape
    count = len(weights)
    anywhere = pl.BlockSpec(memory_space=pl.ANY)
    resident = pl.BlockSpec(memory_space=pltpu.VMEM)
    dma = pltpu.SemaphoreType.DMA
    out = pl.pallas_call(
        functools.partial(spread_kernel, count),
        in_specs=[anywhere, resident, resident] + [anywhere] * count,
        out_specs=[anywhere] * (count + 2) + [resident] * 2,
        out_shape=[
            jax.ShapeDtypeStruct((2, 2 * span, width), BF),
            jax.ShapeDtypeStruct((2, 2 * span, 3 * width), BF),
        ]
        + [jax.ShapeDtypeStruct((2,) + w.shape, w.dtype) for w in weights]
        + [jax.ShapeDtypeStruct((2, n * span, PAIR), BF) for n in (2, 4)],
        scratch_shapes=[
            pltpu.VMEM((span, width), BF),
            pltpu.VMEM((2, 2 * span, width), BF),
            pltpu.VMEM((2,) + weights[0].shape, BF),
            pltpu.VMEM((2, 2 * span, 3 * width), BF),
        ]
        + [pltpu.VMEM(w.shape, w.dtype) for w in weights[1:]]
        + [dma((4,)), dma((4,)), dma, dma((4,)), dma((4,))]
        + [dma((count,))] * 4,
        compiler_params=pltpu.CompilerParams(
            collective_id=0, has_side_effects=True, vmem_limit_bytes=60 << 20
        ),
        name="spread",
    )(tokens, source_segments, target_segments, *weights)
    return out[0], out[1], out[2 : count + 2], out[count + 2 :]


class RowRider:
    def __init__(self, rows):
        self.array = rows
        self.shape = (2 * rows.shape[1], rows.shape[2])

    def copies(self, source, target, send, recv):
        core, group, depth, side, at = place()
        span = source.shape[1]
        slot = target.at[pl.ds(pl.multiple_of(at * span, span), span)]
        for i in range(2):
            row = 2 * core + i
            yield (
                remote(source.at[row], slot, send.at[i], recv.at[at], (side, group, row)),
                pltpu.make_async_copy(source.at[row], slot, recv.at[at]),
                (row == depth) & (side == core),
            )

    def arrivals(self, source, target, recv):
        span = source.shape[1]
        for i in range(2):
            slot = target.at[pl.ds(i * span, span)]
            yield pltpu.make_async_copy(source.at[0], slot, recv.at[i])

    def receives(self):
        return None


class HomeRider:
    def __init__(self, result, layer):
        self.array = result
        self.layer = layer
        self.shape = (4, result.shape[0] // 2, result.shape[1])

    def copies(self, source, target, send, recv):
        core, group, depth, side, at = place()
        span = source.shape[0] // 2
        slot = target.at[depth]
        for i in range(2):
            there = 2 * i + (core + i) % 2
            block = source.at[pl.ds(i * span, span)]
            yield (
                remote(block, slot, send.at[i], recv.at[depth], (self.layer, group, there)),
                pltpu.make_async_copy(block, slot, recv.at[depth]),
                (there == depth) & (core == self.layer),
            )

    def arrivals(self, source, target, recv):
        span = source.shape[0] // 2
        for i in range(4):
            yield pltpu.make_async_copy(source.at[pl.ds(0, span)], target.at[i], recv.at[i])

    def receives(self):
        return lax.axis_index("section") == self.layer


def ride_copies(rider, source, target, send, recv):
    for far, near, stays in rider.copies(source, target, send, recv):

        @pl.when(stays)
        def _():
            near.start()

        @pl.when(jnp.logical_not(stays))
        def _():
            far.start()


def ride_end(rider, source, target, send, recv):
    for far, near, stays in rider.copies(source, target, send, recv):

        @pl.when(jnp.logical_not(stays))
        def _():
            far.wait_send()

    def arrive():
        for copy in rider.arrivals(source, target, recv):
            copy.wait()

    if rider.receives() is None:
        arrive()
    else:
        pl.when(rider.receives())(arrive)


RESULT_OF = (0, 1, 0, 1, 2, 3, 2, 3, 4, 5, 6)
Z_FIRST = ()
LAG = (3,3,2,2,2,2,2)
HOME_SLOT = 16
LATE = (1,2,1,1,2,4,1)


def gradient_groups(width, hidden):
    folds = hidden // width
    groups = []
    for layer, up, down in ((1, 0, 1), (0, 2, 3)):
        groups.append((layer, [(up, 0, 0, hidden)]))
        groups.append((layer, [(down, i * width, 0, width) for i in range(folds)]))
    groups.append((None, [(8, 0, 0, width), (9, 0, 0, width), (10, 0, 0, 2 * width)]))
    for layer, o, q in ((1, 4, 5), (0, 6, 7)):
        groups.append((layer, [(o, 0, 0, width), (q, 0, 0, 3 * width)]))
    return groups


FAMILIES = ((0, 1), (2, 3), (4,), (5, 6))
CROSS_TABLE = {0: [(0, 0), (1, 0)], 1: [(0, 1), (1, 1)]}
SELF_TABLE = {
    0: [(0, 2), (1, 2), (2, 0), (3, 0)],
    2: [(0, 3), (1, 3), (2, 1), (3, 1)],
    5: [(0, 4), (1, 4)],
}


def wide(groups, chosen):
    return sum(p[3] for g in chosen for p in groups[g][1])


class Plan:
    def __init__(self, width, hidden, spans, made=()):
        self.groups = gradient_groups(width, hidden)
        self.half = width // 2
        self.spans = spans
        self.chosen = [g for f in sorted(spans) for g in FAMILIES[f]]
        self.enter = {g: spans[f][0] for f in spans for g in FAMILIES[f]}
        self.leave = {g: spans[f][1] for f in spans for g in FAMILIES[f]}
        self.final = [g for g in self.chosen if self.leave[g] == 10]
        self.arrays = sorted(
            {p[0] for g in self.chosen if self.enter[g] == 0 for p in self.groups[g][1]} - set(made)
        )
        self.made = made
        self.most = max(len(pieces) for _, pieces in self.groups)

    def columns(self, g, k):
        mates = self.level(k)
        return pl.ds(wide(self.groups, mates[: mates.index(g)]), wide(self.groups, [g]))

    def level(self, k):
        return [g for g in self.chosen if self.enter[g] <= k < min(self.leave[g], 5)]

    def family_columns(self, f, g):
        mates = FAMILIES[f]
        return pl.ds(wide(self.groups, mates[: mates.index(g)]), wide(self.groups, [g]))

    def rows(self, k):
        return self.half >> k

    def states_in(self):
        return [f for f in sorted(self.spans) if self.spans[f][0] > 0]

    def states_out(self):
        return [f for f in sorted(self.spans) if self.spans[f][1] < 10]

    def state_shape(self, f, stage):
        return jax.ShapeDtypeStruct((self.rows(stage - 1), wide(self.groups, FAMILIES[f])), BF)

    def scratch(self):
        dma = pltpu.SemaphoreType.DMA
        number = len(self.chosen)
        shapes = []
        first = self.level(0)
        shapes.append(
            pltpu.VMEM((2 * self.half, wide(self.groups, first)) if first else (16, 128), BF)
        )
        for k in range(5):
            columns = wide(self.groups, self.level(k))
            shapes.append(pltpu.VMEM((self.rows(k), columns or 128), BF))
        total = wide(self.groups, self.final)
        shapes.append(pltpu.VMEM((2 * self.half if total else 16, total or 128), BF))
        shapes += [dma((number, self.most))] * 2 + [dma((number, 1))] * 2 + [dma((number, 10))] * 2
        return shapes

    def count(self):
        return 13


class Reducer:
    def __init__(self, plan, parts, states, left, results, scratch, makers=None):
        self.makers = makers or {}
        self.plan, self.parts, self.results = plan, parts, results
        self.states, self.left = states, left
        self.own, self.got, self.total = scratch[0], scratch[1:6], scratch[6]
        self.own_sem, self.out_sem, self.send0, self.recv0, self.send, self.recv = scratch[7:13]
        self.core, group, depth, _, _ = place()
        core = self.core
        partner = (1 - core, group, depth)
        x_next = group + 1 - 2 * (group % 2)
        y_next = (group + 2) % 4
        first = x_next + core * (y_next - x_next)
        second = y_next + core * (x_next - y_next)
        z_next = depth + 1 - 2 * (depth % 2)
        z_far = (depth + 2) % 4
        self.across = [(core, first, depth), (core, second, depth)]
        along = [(core, group, z_next), (core, group, z_far)]
        bit_x, bit_y = group % 2, group // 2
        across_bits = [bit_x + core * (bit_y - bit_x), bit_y + core * (bit_x - bit_y)]
        along_bits = [depth % 2, depth // 2]
        self.orders = [
            ([partner] + self.across + along, [core] + across_bits + along_bits),
            ([partner] + along + self.across, [core] + along_bits + across_bits),
        ]
        self.first_rows = []
        for _, bits in self.orders:
            held = [core * plan.half]
            for k in range(1, 5):
                held.append(held[-1] + bits[k] * plan.rows(k))
            self.first_rows.append(held)

    def family(self, g):
        return [f for f in range(4) if g in FAMILIES[f]][0]

    def order(self, g):
        return self.orders[1 if g in Z_FIRST else 0]

    def held(self, g, k):
        f = self.family(g)
        if k == self.plan.enter[g] - 1:
            return self.states[f].at[:, self.plan.family_columns(f, g)]
        if k == self.plan.leave[g] - 1:
            return self.left[f].at[:, self.plan.family_columns(f, g)]
        return self.got[k].at[:, self.plan.columns(g, k)]

    def slot(self, g, k):
        return self.got[k].at[:, self.plan.columns(g, k)]

    def rows(self, first, count):
        return pl.ds(pl.multiple_of(first, 16), count)

    def own_rows(self, half):
        count = self.plan.half
        return self.rows(half * count, count)

    def away(self, g):
        index = self.plan.chosen.index(g)
        columns = self.plan.columns(g, 0)
        return remote(
            self.own.at[self.own_rows(1 - self.core), columns],
            self.got[0].at[:, columns],
            self.send0.at[index, 0],
            self.recv0.at[index, 0],
            self.orders[0][0][0],
        )

    def stage(self, g):
        index = self.plan.chosen.index(g)
        column = self.plan.columns(g, 0).start
        for i, (array, row, col, width) in enumerate(self.plan.groups[g][1]):
            if array in self.makers:
                column += width
                continue
            block = self.parts[array].at[pl.ds(row, 2 * self.plan.half), pl.ds(col, width)]
            yield pltpu.make_async_copy(
                block, self.own.at[:, pl.ds(column, width)], self.own_sem.at[index, i]
            )
            column += width

    def make(self, g):
        column = self.plan.columns(g, 0).start
        for array, row, col, width in self.plan.groups[g][1]:
            if array in self.makers:
                tokens, ready, grads, grads_ready = self.makers[array]
                ready()
                grads_ready()
                tile = tokens.shape[1]

                @pl.loop(0, width // tile)
                def _(i):
                    at = pl.multiple_of(i * tile, tile)
                    self.own[:, pl.ds(pl.multiple_of(column + at, tile), tile)] = dot_outer(
                        tokens[...], grads[:, pl.ds(at, tile)]
                    ).astype(BF)

            column += width

    def load(self):
        for g in self.plan.level(0):
            for copy in self.stage(g):
                copy.start()

    def add(self, target, arrived, source, first):
        count, strip = target.shape[0], 16

        @pl.loop(0, count // strip)
        def _(i):
            r = pl.multiple_of(i * strip, strip)
            mine = source[pl.ds(pl.multiple_of(first + r, strip), strip), :]
            target[pl.ds(r, strip), :] = mine + arrived[pl.ds(r, strip), :]

    def halving(self, g, k):
        index = self.plan.chosen.index(g)
        neighbours, bits = self.order(g)
        count = self.plan.rows(k)
        return remote(
            self.held(g, k - 1).at[self.rows((1 - bits[k]) * count, count)],
            self.slot(g, k),
            self.send.at[index, k],
            self.recv.at[index, k],
            neighbours[k],
        )

    def whole(self, g):
        mates = self.plan.final
        return pl.ds(
            wide(self.plan.groups, mates[: mates.index(g)]), wide(self.plan.groups, [g])
        )

    def doubling(self, g, k):
        index = self.plan.chosen.index(g)
        held = self.first_rows[1 if g in Z_FIRST else 0]
        block = self.total.at[self.rows(held[k], self.plan.rows(k)), self.whole(g)]
        return remote(
            block, block, self.send.at[index, 4 + k], self.recv.at[index, 4 + k], self.order(g)[0][k]
        )

    def joining(self, g):
        index = self.plan.chosen.index(g)
        half = self.plan.half
        block = self.total.at[self.rows(self.core * half, half), self.whole(g)]
        return remote(
            block, block, self.send.at[index, 9], self.recv.at[index, 9], self.orders[0][0][0]
        )

    def only(self, layer, there, act):
        if layer is None:
            act()
        else:
            pl.when((self.core == layer) if there else (self.core != layer))(act)

    def emit(self, g, wait):
        index = self.plan.chosen.index(g)
        layer, pieces = self.plan.groups[g]
        column = self.whole(g).start
        for i, (array, row, col, width) in enumerate(pieces):
            copy = pltpu.make_async_copy(
                self.total.at[:, pl.ds(column, width)],
                self.results[RESULT_OF[array]].at[
                    pl.ds(row, 2 * self.plan.half), pl.ds(col, width)
                ],
                self.out_sem.at[index, i],
            )
            column += width
            self.only(layer, True, copy.wait if wait else copy.start)

    def run(self, g, step):
        layer = self.plan.groups[g][0]
        enter, leave = self.plan.enter[g], self.plan.leave[g]
        if enter < step <= 5:
            k = step - 1
            if k == 0:
                self.away(g).wait()
                mine = self.own.at[:, self.plan.columns(g, 0)]
                self.add(self.held(g, 0), self.slot(g, 0), mine, self.core * self.plan.half)
            else:
                self.halving(g, k).wait()
                count = self.plan.rows(k)
                first = self.order(g)[1][k] * count
                self.add(self.held(g, k), self.slot(g, k), self.held(g, k - 1), first)
        if step == leave and leave < 10:
            return
        if step == 0:
            for copy in self.stage(g):
                copy.wait()
            self.make(g)
            self.away(g).start()
        elif step <= 4:
            self.halving(g, step).start()
        elif step == 5:
            held = self.first_rows[1 if g in Z_FIRST else 0]
            self.total[self.rows(held[4], self.plan.rows(4)), self.whole(g)] = self.held(g, 4)[...]
            self.doubling(g, 4).start()
        elif step <= 8:
            self.doubling(g, 10 - step).wait()
            self.doubling(g, 9 - step).start()
        elif step == 9:
            self.doubling(g, 1).wait()
            self.only(layer, False, self.joining(g).start)
        else:
            self.only(layer, False, self.joining(g).wait_send)
            self.only(layer, True, self.joining(g).wait_recv)
            self.emit(g, False)


def tail_slots(plan):
    table = {}
    for f in sorted(plan.spans):
        for g in FAMILIES[f]:
            for n, step in enumerate(range(plan.enter[g], 11)):
                table.setdefault(LATE[g] + LAG[g] * n, []).append((g, step))
    return table


def collect_kernel(plan, riders, recipe, *refs):
    count = len(riders)
    homes, refs = refs[:count], refs[count:]
    number = len({i for entry in recipe.values() for i, _ in entry})
    sources, refs = refs[:number], refs[number:]
    parts = dict(zip(plan.arrays, refs))
    refs = refs[len(plan.arrays) :]
    states = dict(zip(plan.states_in(), refs))
    refs = refs[len(states) :]
    small, refs = refs[0], refs[1:]
    home_outs, refs = refs[:count], refs[count:]
    results, small_out, refs = refs[:7], refs[7], refs[8:]
    small_got, home_send, home_recv, small_send, small_recv, source_sem = refs[:6]
    held, refs = refs[6 : 6 + number], refs[6 + number :]
    loads = [
        pltpu.make_async_copy(source, target, source_sem.at[i])
        for i, (source, target) in enumerate(zip(sources, held))
    ]
    waited = set()

    def ready(i):
        def act():
            if i not in waited:
                waited.add(i)
                loads[i].wait()

        return act

    makers = {}
    for array, entry in recipe.items():
        made = []
        for i, layer in entry:
            made += [held[i] if layer is None else held[i].at[layer], ready(i)]
        makers[array] = made
    reducer = Reducer(plan, parts, states, {}, results, refs, makers)
    core, group, depth, _, _ = place()
    for copy in loads:
        copy.start()
    reducer.load()
    greet(row_mates(core, group, depth) + reducer.across)

    def small_copy(k):
        return remote(
            small_out, small_got.at[k], small_send.at[k], small_recv.at[k], reducer.orders[0][0][k]
        )

    def small_step(k):
        if k > 0:
            small_copy(k - 1).wait()
            small_out[...] += small_got[k - 1]
        else:
            small_out[...] = small[...]
        if k < 5:
            small_copy(k).start()

    table = tail_slots(plan)
    for slot in range(max(max(table), 12) + 1):
        for g, step in sorted(reversed(table.get(slot, [])), key=lambda item: item[1] == 0):
            reducer.run(g, step)
        if slot == HOME_SLOT:
            for i, rider in enumerate(riders):
                ride_copies(rider, homes[i], home_outs[i], home_send.at[i], home_recv.at[i])
        if 2 <= slot <= 12 and slot % 2 == 0:
            small_step(slot // 2 - 1)
    for g in plan.chosen:
        reducer.emit(g, True)
    for i, rider in enumerate(riders):
        ride_end(rider, homes[i], home_outs[i], home_send.at[i], home_recv.at[i])


def collect(plan, riders, parts, states, small, products):
    sources = []
    recipe = {}
    for array, entry in products.items():
        recipe[array] = []
        for value, layer in entry:
            at = [i for i, known in enumerate(sources) if known is value]
            if not at:
                at = [len(sources)]
                sources.append(value)
            recipe[array].append((at[0], layer))
    count = len(riders)
    width = riders[0].array.shape[1]
    hidden = 4 * width
    anywhere = pl.BlockSpec(memory_space=pl.ANY)
    resident = pl.BlockSpec(memory_space=pltpu.VMEM)
    dma = pltpu.SemaphoreType.DMA
    shapes = [
        (width, hidden), (hidden, width), (width, width), (width, 3 * width),
        (width, width), (width, width), (width, 2 * width),
    ]
    out = pl.pallas_call(
        functools.partial(collect_kernel, plan, riders, recipe),
        in_specs=[resident] * count
        + [anywhere] * (len(sources) + len(plan.arrays))
        + [resident] * (len(plan.states_in()) + 1),
        out_specs=[anywhere] * (count + 7) + [resident],
        out_shape=[jax.ShapeDtypeStruct(rider.shape, BF) for rider in riders]
        + [jax.ShapeDtypeStruct(s, BF) for s in shapes]
        + [jax.ShapeDtypeStruct(small.shape, F32)],
        scratch_shapes=[
            pltpu.VMEM((5,) + small.shape, F32),
            dma((count, 2)),
            dma((count, 4)),
            dma((5,)),
            dma((5,)),
            dma((len(sources),)),
        ]
        + [pltpu.VMEM(v.shape, v.dtype) for v in sources]
        + plan.scratch(),
        compiler_params=pltpu.CompilerParams(
            collective_id=1, has_side_effects=True, vmem_limit_bytes=56 << 20
        ),
        name="collect",
    )(
        *[rider.array for rider in riders],
        *sources,
        *[parts[a] for a in plan.arrays],
        *[states[f] for f in plan.states_in()],
        small,
    )
    return out[:count], out[count : count + 7], out[count + 7]


def key_loads(offsets, source, staged, sem, layer, step):
    for t in range(2):
        first = pl.multiple_of((offsets[t] + step) * PAIR, PAIR)
        yield pltpu.make_async_copy(
            source.at[layer, :, pl.ds(first, PAIR)], staged.at[layer, step, t], sem.at[layer, step, t]
        )


def key_copies(staged, held, send, recv, layer, step):
    core, group, depth, _, _ = place()
    return [
        remote(
            staged.at[layer, step, t],
            held.at[layer, step, t],
            send.at[layer, step, t],
            recv.at[layer, step, t],
            (1 - core, group, depth),
        )
        for t in range(2)
    ]


def attend_steps(layers):
    return [(layer, step) for layer in range(layers) for step in range(4)]


def begin(layers, offsets, riders, ride, source, keys, reducer=None):
    staged, sem, held, send, recv = keys
    core, group, depth, _, _ = place()
    for layer, step in attend_steps(layers):
        for copy in key_loads(offsets, source, staged, sem, layer, step):
            copy.start()
    if reducer is not None:
        reducer.load()
    mates = row_mates(core, group, depth) if riders or reducer else [(1 - core, group, depth)]
    greet(mates + (reducer.across if reducer else []))
    for layer, step in attend_steps(layers):
        for copy in key_loads(offsets, source, staged, sem, layer, step):
            copy.wait()
        for copy in key_copies(staged, held, send, recv, layer, step):
            copy.start()
    for i, rider in enumerate(riders):
        ride_copies(rider, *[r[i] if j < 2 else r.at[i] for j, r in enumerate(ride)])


def end(layers, riders, ride, keys):
    staged, sem, held, send, recv = keys
    for layer, step in attend_steps(layers):
        for copy in key_copies(staged, held, send, recv, layer, step):
            copy.wait_send()
    for i, rider in enumerate(riders):
        ride_end(rider, *[r[i] if j < 2 else r.at[i] for j, r in enumerate(ride)])


def by_layer(causal, layer, act):
    for kind in sorted(set(causal)):
        if len(set(causal)) == 1:
            act(kind)
        else:
            pl.when(layer == causal.index(kind))(functools.partial(act, kind))


def attend_kernel(causal, offsets, riders, *refs):
    layers, count = len(causal), len(riders)
    q_ref, k_ref, v_ref, kv_ref, qf_ref, kf_ref = refs[:6]
    o_ref, of_ref, lse_ref = refs[6 + count : 9 + count]
    *keys, ride_send, ride_recv = refs[9 + 2 * count :]
    staged, _, held, send, recv = keys
    ride = (refs[6 : 6 + count], refs[9 + count : 9 + 2 * count], ride_send, ride_recv)
    layer, step = pl.program_id(0), pl.program_id(1)

    @pl.when((layer == 0) & (step == 0))
    def _():
        begin(layers, offsets, riders, ride, kv_ref, keys)

    for copy in key_copies(staged, held, send, recv, layer, step):
        copy.wait_recv()

    def work(kind):
        whole, stat = attend_pair(
            kind, q_ref[0], k_ref[0], v_ref[0], held[layer, step, 0], held[layer, step, 1],
            qf_ref[0], kf_ref[0],
        )
        o_ref[0] = whole.astype(BF)
        of_ref[0] = whole
        lse_ref[0] = stat

    by_layer(causal, layer, work)

    @pl.when((layer == layers - 1) & (step == 3))
    def _():
        end(layers, riders, ride, keys)


def grad_copies(gone, got, send, recv, layer, step):
    core, group, depth, _, _ = place()
    return [
        remote(
            gone.at[layer, step, t],
            got.at[layer, step, t],
            send.at[layer, step, t],
            recv.at[layer, step, t],
            (1 - core, group, depth),
        )
        for t in range(2)
    ]


def attend_back_kernel(causal, offsets, riders, joined, plan, table, *refs):
    layers, count = len(causal), len(riders)
    q_ref, k_ref, v_ref, kv_ref, qf_ref, kf_ref, o_ref, lse_ref, do_ref = refs[:9]
    sources, refs = refs[9 : 9 + count], refs[9 + count :]
    parts = dict(zip(plan.arrays, refs))
    refs = refs[len(parts) :]
    states = dict(zip(plan.states_in(), refs))
    refs = refs[len(states) :]
    outs = 1 if joined else 2
    dq_ref, dkv_ref, refs = refs[0], refs[outs - 1], refs[outs:]
    left = dict(zip(plan.states_out(), refs))
    refs = refs[len(left) :]
    targets, refs = refs[:count], refs[count:]
    keys, (gone, got, kept, g_send, g_recv) = refs[:5], refs[5:10]
    staged, _, held, send, recv = keys
    scratch, (ride_send, ride_recv) = refs[10:-2], refs[-2:]
    ride = (sources, targets, ride_send, ride_recv)
    layer, step = pl.program_id(0), pl.program_id(1)
    width = 4 * PAIR
    reducer = Reducer(plan, parts, states, left, [], scratch)

    @pl.when((layer == 0) & (step == 0))
    def _():
        begin(layers, offsets, riders, ride, kv_ref, keys, reducer)

    for slot in range(4 * layers):
        moves = table.get(slot, [])
        if moves:

            @pl.when((layer == slot // 4) & (step == slot % 4))
            def _():
                for g, stage in moves:
                    reducer.run(g, stage)

    for copy in key_copies(staged, held, send, recv, layer, step):
        copy.wait_recv()

    def work(kind):
        columns = pl.ds(pl.multiple_of(step * PAIR, PAIR), PAIR)

        @pl.loop(0, 2)
        def _(head):
            mine, dq, dk, dv, dko, dvo = attend_back_head(
                kind, head, q_ref[0], k_ref[0], v_ref[0], held[layer, step, 0],
                held[layer, step, 1], qf_ref[0], kf_ref[0], o_ref[0], lse_ref[0], do_ref[0],
            )
            dq_ref[layer, :, columns] = jnp.where(mine, dq.astype(BF), dq_ref[layer, :, columns])
            kept[layer, step, 0] = jnp.where(mine, dk, kept[layer, step, 0])
            kept[layer, step, 1] = jnp.where(mine, dv, kept[layer, step, 1])
            gone[layer, step, 0] = jnp.where(mine, dko.astype(BF), gone[layer, step, 0])
            gone[layer, step, 1] = jnp.where(mine, dvo.astype(BF), gone[layer, step, 1])

    by_layer(causal, layer, work)
    for copy in grad_copies(gone, got, g_send, g_recv, layer, step):
        copy.start()

    @pl.when((layer == layers - 1) & (step == 3))
    def _():
        for one, at in attend_steps(layers):
            for t, copy in enumerate(grad_copies(gone, got, g_send, g_recv, one, at)):
                copy.wait()
                first = (width if joined else 0) + t * width + at * PAIR
                dkv_ref[one, :, first : first + PAIR] = (
                    kept[one, at, t] + got[one, at, t].astype(F32)
                ).astype(BF)
        for g in plan.chosen:
            reducer.run(g, plan.leave[g])
        end(layers, riders, ride, keys)


def attend_specs(size, offsets, masks):
    def column(at):
        return pl.BlockSpec((1, size, PAIR), lambda l, p: (l, 0, at + p))

    def shared(rows, first):
        return pl.BlockSpec((1, rows, PAIR), lambda l, p: (l + first, 0, 0))

    return (
        [column(at) for at in offsets]
        + [pl.BlockSpec(memory_space=pl.ANY)]
        + [shared(size, masks[0]), shared(2 * size, masks[1])]
    ), column


def key_scratch(layers, size):
    slots = pltpu.VMEM((layers, 4, 2, size, PAIR), BF)
    sems = pltpu.SemaphoreType.DMA((layers, 4, 2))
    return [slots, sems, slots, sems, sems]


def attend_call(
    kernel, name, layers, riders, collective, in_specs, out_specs, out_shape, scratch, flops, args
):
    count = len(riders)
    dma = pltpu.SemaphoreType.DMA
    return pl.pallas_call(
        kernel,
        grid=(layers, 4),
        in_specs=in_specs,
        out_specs=out_specs + [pl.BlockSpec(memory_space=pl.ANY)] * count,
        out_shape=out_shape + [jax.ShapeDtypeStruct(rider.shape, BF) for rider in riders],
        scratch_shapes=scratch + [dma((max(count, 1), 2)), dma((max(count, 1), 4))],
        compiler_params=pltpu.CompilerParams(
            vmem_limit_bytes=56 << 20, collective_id=collective, has_side_effects=True
        ),
        cost_estimate=pl.CostEstimate(flops=flops, bytes_accessed=flops // 512, transcendentals=0),
        name=name,
    )(*args)


def attend_forward(q, kv, offsets, masks, features, causal, riders, collective):
    layers, size = len(causal), q.shape[1]
    width = 4 * PAIR
    in_specs, column = attend_specs(size, offsets, masks)
    dma = pltpu.SemaphoreType.DMA
    return attend_call(
        functools.partial(attend_kernel, causal, offsets[1:], riders),
        "attend_forward",
        layers,
        riders,
        collective,
        in_specs + [pl.BlockSpec(memory_space=pltpu.VMEM)] * len(riders),
        [column(0)] * 3,
        [jax.ShapeDtypeStruct((layers, size, width), t) for t in (BF, F32, F32)],
        key_scratch(layers, size),
        16 * layers * size * size * width,
        (q, kv, kv, kv, *features, *[rider.array for rider in riders]),
    )


def attend_backward(
    q, kv, offsets, masks, features, o, lse, do, causal, riders, collective, joined,
    plan, table, parts, states,
):
    layers, size = len(causal), q.shape[1]
    width = 4 * PAIR
    in_specs, column = attend_specs(size, offsets, masks)
    dma = pltpu.SemaphoreType.DMA
    resident = pl.BlockSpec(memory_space=pltpu.VMEM)
    anywhere = pl.BlockSpec(memory_space=pl.ANY)
    widths = [3 * width] if joined else [width, 2 * width]
    slots = (layers, 4, 2, size, PAIR)
    left = [plan.state_shape(f, plan.spans[f][1]) for f in plan.states_out()]
    return attend_call(
        functools.partial(
            attend_back_kernel, causal, offsets[1:], riders, joined, plan, table
        ),
        "attend_backward",
        layers,
        riders,
        collective,
        in_specs
        + [column(0)] * 3
        + [resident] * len(riders)
        + [anywhere] * len(plan.arrays)
        + [resident] * len(plan.states_in()),
        [resident] * (len(widths) + len(left)),
        [jax.ShapeDtypeStruct((layers, size, w), BF) for w in widths] + left,
        key_scratch(layers, size)
        + [
            pltpu.VMEM(slots, BF),
            pltpu.VMEM(slots, BF),
            pltpu.VMEM(slots, F32),
            dma((layers, 4, 2)),
            dma((layers, 4, 2)),
        ]
        + plan.scratch(),
        40 * layers * size * size * width,
        (
            q, kv, kv, kv, *features, o, lse, do,
            *[rider.array for rider in riders],
            *[parts[a] for a in plan.arrays],
            *[states[f] for f in plan.states_in()],
        ),
    )


def dot(a, b):
    return lax.dot_general(a, b, (((1,), (0,)), ((), ())), preferred_element_type=F32)


def dot_back(a, b):
    return lax.dot_general(a, b, (((1,), (1,)), ((), ())), preferred_element_type=F32)


def dot_outer(a, b):
    return lax.dot_general(a, b, (((0,), (0,)), ((), ())), preferred_element_type=F32)


def each(function, *stacked):
    return jnp.stack([function(*(s[i] for s in stacked)) for i in range(2)])


def widen_kernel(count, *refs):
    sums, homes, refs = refs[:count], refs[count : count + 4], refs[count + 4 :]
    wide, tokens, grads = refs[:count], refs[count], refs[count + 1]
    for source, target in zip(sums, wide):
        target[...] = source[...].astype(F32)
    core = lax.axis_index("section")

    @pl.when(core == 0)
    def _():
        tokens[...] = homes[0][...]
        grads[...] = homes[2][...].astype(F32)

    @pl.when(core != 0)
    def _():
        tokens[...] = homes[1][...]
        grads[...] = homes[3][...].astype(F32)


def widen(sums, homes, steps=4):
    def rows(shape):
        return pl.BlockSpec((shape[0] // steps,) + shape[1:], lambda i: (i, 0))

    homes = [h.reshape(-1, h.shape[-1]) for h in homes]
    shapes = [v.shape for v in sums] + [homes[0].shape] * 2
    types = [F32] * len(sums) + [BF, F32]
    return pl.pallas_call(
        functools.partial(widen_kernel, len(sums)),
        grid=(steps,),
        in_specs=[rows(v.shape) for v in (*sums, *homes)],
        out_specs=[rows(s) for s in shapes],
        out_shape=[jax.ShapeDtypeStruct(s, t) for s, t in zip(shapes, types)],
        name="widen",
    )(*sums, *homes)


def row_shards(
    inputs,
    cotangent,
    qkv_weight,
    out_weight,
    up_weight,
    down_weight,
    norm_gain,
    norm_bias,
    cross_q_weight,
    cross_kv_weight,
    cross_out_weight,
    cross_gain,
    cross_bias,
    source_segments,
    target_segments,
):
    core = lax.axis_index("section")
    depth = lax.axis_index("seq")
    span = inputs.shape[2]
    width = inputs.shape[3]

    x_both, qkv, both, features = spread(
        inputs[0],
        source_segments,
        target_segments,
        qkv_weight[0],
        out_weight[0],
        up_weight[0],
        down_weight[0],
        norm_gain[0],
        norm_bias[0],
    )
    qkv_both, out_both, up_both, down_both, gain_both, bias_both = both
    g_e, g_d = gain_both[0], gain_both[1]
    b_e, b_d = bias_both[0], bias_both[1]
    wu_e, wu_d = up_both[0], up_both[1]
    wd_e, wd_d = down_both[0], down_both[1]

    self_args = ((0, 4, 8), (0, 0), features)
    o, o_wide, lse, cot = attend_forward(
        qkv, qkv, *self_args, (False, True), [RowRider(cotangent)], 2
    )
    cot = cot.astype(F32)
    summed = x_both.astype(F32) + lax.dot_general(
        o, out_both, (((2,), (1,)), ((0,), (0,))), preferred_element_type=F32
    )
    s1, t1 = summed[0], summed[1]

    h_s = layer_norm(s1, g_e[0], b_e[0])
    h_s_low = h_s.astype(BF)
    u_s = dot(h_s_low, wu_e)
    gel_s = gelu_tanh(u_s).astype(BF)
    s2 = h_s + dot(gel_s, wd_e)
    memory = layer_norm(s2, g_e[1], b_e[1]).astype(BF)
    ckv = dot(memory, cross_kv_weight).astype(BF)

    h_t = layer_norm(t1, g_d[0], b_d[0])
    h_t_low = h_t.astype(BF)
    cq = dot(h_t_low, cross_q_weight).astype(BF)
    cross_args = ((0, 0, 4), (1, 0), features)
    o_c, oc_wide, lse_c = attend_forward(cq[None], ckv[None], *cross_args, (False,), [], 3)
    o_c = o_c[0]
    t2 = h_t + dot(o_c, cross_out_weight)
    c_t = layer_norm(t2, cross_gain, cross_bias)
    c_t_low = c_t.astype(BF)
    u_t = dot(c_t_low, wu_d)
    gel_t = gelu_tanh(u_t).astype(BF)
    t3 = c_t + dot(gel_t, wd_d)
    decoded, pull_t3 = jax.vjp(layer_norm, t3, g_d[1], b_d[1])
    decoded = decoded.astype(BF)

    grad_t3, gg_d1, gb_d1 = pull_t3(cot)
    low_t3 = grad_t3.astype(BF)
    gw_down_d = dot_outer(gel_t, low_t3).astype(BF)
    grad_u_t = jax.vjp(gelu_tanh, u_t)[1](dot_back(low_t3, wd_d))[0].astype(BF)
    gw_up_d = dot_outer(c_t_low, grad_u_t).astype(BF)
    grad_c = grad_t3 + dot_back(grad_u_t, wu_d)
    grad_t2, gg_c, gb_c = jax.vjp(layer_norm, t2, cross_gain, cross_bias)[1](grad_c)
    low_t2 = grad_t2.astype(BF)
    grad_o_c = dot_back(low_t2, cross_out_weight).astype(BF)
    hidden = wu_d.shape[1]
    parts = {0: gw_up_d, 1: gw_down_d}
    plan = Plan(width, hidden, {0: (0, 2)})
    grad_cq, grad_ckv, state_d, home_decoded = attend_backward(
        cq[None], ckv[None], *cross_args, oc_wide, lse_c, grad_o_c[None], (False,),
        [HomeRider(decoded, 1)], 4, False, plan, CROSS_TABLE, parts, {},
    )
    grad_cq, grad_ckv = grad_cq[0], grad_ckv[0]
    grad_h = grad_t2 + dot_back(grad_cq, cross_q_weight)
    grad_t1, gg_d0, gb_d0 = jax.vjp(layer_norm, t1, g_d[0], b_d[0])[1](grad_h)
    low_t1 = grad_t1.astype(BF)

    grad_memory = dot_back(grad_ckv, cross_kv_weight).astype(BF).astype(F32)
    grad_s2, gg_e1, gb_e1 = jax.vjp(layer_norm, s2, g_e[1], b_e[1])[1](grad_memory)
    low_s2 = grad_s2.astype(BF)
    gw_down_e = dot_outer(gel_s, low_s2).astype(BF)
    grad_u_s = jax.vjp(gelu_tanh, u_s)[1](dot_back(low_s2, wd_e))[0].astype(BF)
    gw_up_e = dot_outer(h_s_low, grad_u_s).astype(BF)
    grad_h = grad_s2 + dot_back(grad_u_s, wu_e)
    grad_s1, gg_e0, gb_e0 = jax.vjp(layer_norm, s1, g_e[0], b_e[0])[1](grad_h)
    low_s1 = grad_s1.astype(BF)

    low_1 = jnp.stack([low_s1, low_t1])
    grad_o = lax.dot_general(
        low_1, out_both, (((2,), (2,)), ((0,), (0,))), preferred_element_type=F32
    ).astype(BF)
    parts = {2: gw_up_e, 3: gw_down_e}
    plan = Plan(width, hidden, {0: (2, 5), 1: (0, 2)})
    grad_qkv, state_d, state_e, home_memory = attend_backward(
        qkv, qkv, *self_args, o_wide, lse, grad_o, (False, True), [HomeRider(memory, 0)], 5, True,
        plan, SELF_TABLE, parts, {0: state_d},
    )
    low_cross = low_t2
    products = {
        4: ((o, 1), (low_1, 1)),
        5: ((x_both, 1), (grad_qkv, 1)),
        6: ((o, 0), (low_1, 0)),
        7: ((x_both, 0), (grad_qkv, 0)),
        8: ((o_c, None), (low_cross, None)),
        9: ((h_t_low, None), (grad_cq, None)),
        10: ((memory, None), (grad_ckv, None)),
    }
    grad_x = jnp.stack([grad_s1, grad_t1]) + lax.dot_general(
        grad_qkv, qkv_both, (((2,), (2,)), ((0,), (0,))), preferred_element_type=F32
    )
    grad_x = grad_x.astype(BF)

    small = jnp.stack(
        [gg_e0, gg_e1, gb_e0, gb_e1, gg_d0, gg_d1, gb_d0, gb_d1, gg_c, gb_c]
        + [jnp.zeros_like(gg_c)] * 6
    )
    plan = Plan(width, hidden, {0: (5, 10), 1: (2, 10), 2: (0, 10), 3: (0, 10)}, tuple(products))
    (home_xs, home_xt), sums, small = collect(
        plan,
        [HomeRider(grad_x[0], 0), HomeRider(grad_x[1], 1)],
        {},
        {0: state_d, 1: state_e},
        small,
        products,
    )
    *wide_sums, outputs, grads = widen(sums, [home_memory, home_decoded, home_xs, home_xt])
    g_up, g_down, g_out, g_qkv, g_cross_out, g_cross_q, g_cross_kv = wide_sums
    local = (1, -1) + inputs.shape[2:]
    layer_small = jnp.where(core == 0, small[:4], small[4:8])
    return (
        outputs.reshape(local),
        grads.reshape(local),
        g_qkv[None],
        g_out[None],
        g_up[None],
        g_down[None],
        layer_small[None, :2],
        layer_small[None, 2:],
        g_cross_q,
        g_cross_kv,
        g_cross_out,
        small[8],
        small[9],
    )


def solution(mesh):
    in_specs = (
        P("section", "dp", "seq", None),
        P("dp", "seq", None),
        P("section", None, None),
        P("section", None, None),
        P("section", None, None),
        P("section", None, None),
        P("section", None, None),
        P("section", None, None),
        P(),
        P(),
        P(),
        P(),
        P(),
        P("dp", None),
        P("dp", None),
    )
    out_specs = (
        P("section", "dp", "seq", None),
        P("section", "dp", "seq", None),
        P("section", None, None),
        P("section", None, None),
        P("section", None, None),
        P("section", None, None),
        P("section", None, None),
        P("section", None, None),
        P(),
        P(),
        P(),
        P(),
        P(),
    )
    whole_rows = mesh.shape["section"] == 2 and mesh.shape["seq"] == 4 and mesh.shape["dp"] == 4
    body = row_shards if whole_rows else shards
    return jax.shard_map(body, mesh=mesh, in_specs=in_specs, out_specs=out_specs, check_vma=False)
```
